32 devices in a mesh: parts: 2 (over x), tok: 16 (over z, y, core).
Axes of the slice: x: 2, y: 2, z: 4, core: 2. Of those that a mesh axis runs over, the one named last changes fastest.
Arguments:
- queries: bfloat16 [32768, 1024], P(('parts', 'tok')), parts along dimension 0, may hold values from -6 to 6
- keys: bfloat16 [32768, 1024], P(('parts', 'tok')), parts along dimension 0, may hold values from -6 to 6
- values: bfloat16 [32768, 1024], P(('parts', 'tok')), parts along dimension 0, may hold values from -6 to 6
- step_size: float32 [4, 32768], P(None, ('parts', 'tok')), parts along dimension 1, may hold values from 10 to 100
- fast_in: float32 [4, 256, 1024], P(None, 'tok'), may hold values from -6 to 6
- fast_out: float32 [4, 512, 256], P(None, 'tok'), may hold values from -6 to 6
Outputs:
- output: bfloat16 [32768, 1024], P(('parts', 'tok')), parts along dimension 0
- fast_in_next: float32 [8, 256, 1024], P('parts', 'tok'), parts along dimension 0
- fast_out_next: float32 [8, 512, 256], P('parts', 'tok'), parts along dimension 0
The draws below stay inside these ranges and needn't reach their ends.
There are 2 independent parts, one for each index of `parts`. The reference program is written for one: setup_inputs(seed, part) draws one part's arguments, and reference() takes and returns one part's arrays. A program takes and returns all parts, laid end to end along the dimension named above; an argument that names none is the same for every part. Nothing has to cross between parts.
All inputs are finite; a program needn't handle non-finite values.
Results may differ from the reference program's by a relative error of at most 0.012.
The reference program's roundings to bfloat16 on the way count: a program that leaves them out, or rounds other values in their place, can miss the bound.
Values may be sent and summed in bfloat16 or wider, within the bound.
No kernel may reach another device: no remote copies, remote signals or barrier semaphores. Data moves between devices by JAX's collectives and lax.ppermute only.
A program may use at most 128 MiB of HBM per device.

```python
import math
import jax
import jax.numpy as jnp
from jax import lax

HEADS = 4
HDIM = 256
FAST = 512
BLOCK = 16384


def spiked(values, rng, source, target, shards_of, factor):
    owner, partner = [(jnp.arange(values.shape[axis_at]) // (values.shape[axis_at] // shards_of)).reshape([-1 if axis == axis_at else 1 for axis in range(values.ndim)]) for axis_at in (source, target)]
    chosen = jax.random.permutation(rng, shards_of)[partner]
    strong = (owner == chosen) | (owner == (partner + shards_of // 2) % shards_of)
    return jnp.where(strong, factor * values, values)


def level_of(own_key, shape, cuts, least, largest):
    level = 1.0
    for position, blocks in cuts:
        draws = jax.random.uniform(jax.random.fold_in(jax.random.fold_in(own_key, 6), position), (blocks,), jnp.float32, least / len(cuts), largest / len(cuts))
        level = level * jnp.repeat(jnp.exp(draws), shape[position] // blocks).reshape((-1,) + (1,) * (len(shape) - 1 - position))
    return level


def gaussian(rng, dims, width, bound, cuts=(), kind=jnp.bfloat16):
    result = width * jax.random.normal(rng, dims, jnp.float32)
    if cuts:
        result = result * level_of(rng, dims, cuts, -0.22, 0.18)
    return jnp.clip(result, -bound, bound).astype(kind)


def bell_draw_with(rng, shape, deviation, most, cuts, heavy, dtype=jnp.bfloat16):
    array = deviation * jax.random.normal(rng, shape, jnp.float32)
    if cuts:
        array = array * level_of(rng, shape, cuts, -0.22, 0.18)
    return jnp.clip(spiked(array, jax.random.fold_in(rng, 3), *heavy), -most, most).astype(dtype)


def setup_inputs(seed: int = 0, part: int = 0) -> dict:
    arg_keys = jax.random.split(jax.random.key(seed), 7)
    part_keys = jax.random.split(jax.random.fold_in(arg_keys[6], part), 7)
    return {
        "queries": gaussian(part_keys[0], (BLOCK, HEADS * HDIM), 1.0, 6.0, ((0, 16),)),
        "keys": bell_draw_with(part_keys[1], (BLOCK, HEADS * HDIM), 1.0, 6.0, ((0, 16),), (0, 1, 16, 2.0)),
        "values": gaussian(part_keys[2], (BLOCK, HEADS * HDIM), 1.0, 6.0, ((0, 16),)),
        "step_size": jnp.clip(jnp.exp(math.log(100.0) - 2.3025851 * jax.random.uniform(part_keys[3], (HEADS, BLOCK), jnp.float32) ** level_of(part_keys[3], (HEADS, BLOCK), ((1, 16),), -0.2, 0.2)), 10.0, 100.0),
        "fast_in": gaussian(arg_keys[4], (HEADS, HDIM, 2 * FAST), 1.0, 6.0, ((1, 16),), jnp.float32),
        "fast_out": gaussian(arg_keys[5], (HEADS, FAST, HDIM), 1.0, 6.0, ((1, 16),), jnp.float32),
    }


def rms_rows(matrix):
    return matrix * lax.rsqrt(lax.optimization_barrier(jnp.mean(matrix * matrix, axis=-1, keepdims=True)) + 1e-06)

def normalized_heads(tokens, heads, head_size):
    row_count = tokens.shape[0]
    wide = tokens.astype(jnp.float32).reshape(row_count, heads, head_size)
    return rms_rows(wide).astype(jnp.bfloat16)

def head_increments(key_rows, value_rows, rates, weight_in, weight_out, block_root):
    fast = weight_out.shape[0]
    in_root = 1.0 / math.sqrt(weight_in.shape[0])
    out_root = 1.0 / math.sqrt(fast)
    scaled = (rates[:, None] * block_root * value_rows.astype(jnp.float32)).astype(jnp.bfloat16)
    pre = jnp.dot(key_rows, weight_in, preferred_element_type=jnp.float32) * in_root
    gate = pre[:, :fast]
    upper = pre[:, fast:]
    sigma = jax.nn.sigmoid(gate)
    active = gate * sigma
    hidden = (active * upper).astype(jnp.bfloat16)
    back = lax.dot_general(scaled, weight_out, (((1,), (1,)), ((), ())), preferred_element_type=jnp.float32) * out_root
    d_gate = (back * upper * sigma * (1.0 + gate * (1.0 - sigma))).astype(jnp.bfloat16)
    d_up = (back * active).astype(jnp.bfloat16)
    joined = jnp.concatenate([d_gate, d_up], axis=1)
    inc_in = lax.dot_general(key_rows, joined, (((0,), (0,)), ((), ())), preferred_element_type=jnp.float32) * in_root
    inc_out = lax.dot_general(hidden, scaled, (((0,), (0,)), ((), ())), preferred_element_type=jnp.float32) * out_root
    return (inc_in, inc_out)

def renorm_in(matrix):
    heads, rows_here, double = matrix.shape
    split = matrix.reshape(heads, rows_here, 2, double // 2)
    return rms_rows(split).reshape(heads, rows_here, double)

def apply_head(query_rows, weight_in, weight_out):
    fast = weight_out.shape[0]
    pre = jnp.dot(query_rows, weight_in, preferred_element_type=jnp.float32) * (1.0 / math.sqrt(weight_in.shape[0]))
    gate = pre[:, :fast]
    hidden = (gate * jax.nn.sigmoid(gate) * pre[:, fast:]).astype(jnp.bfloat16)
    return jnp.dot(hidden, weight_out, preferred_element_type=jnp.float32) * (1.0 / math.sqrt(fast))

def reference(queries, keys, values, step_size, fast_in, fast_out):
    row_count = keys.shape[0]
    block_root = 1.0 / math.sqrt(row_count)
    keyn = normalized_heads(keys, HEADS, HDIM)
    queryn = normalized_heads(queries, HEADS, HDIM)
    w_in = fast_in.astype(jnp.bfloat16)
    w_out = fast_out.astype(jnp.bfloat16)
    list_in = []
    list_out = []
    for head_number in range(HEADS):
        value_rows = values[:, head_number * HDIM:(head_number + 1) * HDIM]
        part_in, part_out = head_increments(keyn[:, head_number, :], value_rows, step_size[head_number], w_in[head_number], w_out[head_number], block_root)
        list_in.append(part_in)
        list_out.append(part_out)
    fast_in_next = renorm_in(fast_in + jnp.stack(list_in))
    fast_out_next = rms_rows(fast_out + jnp.stack(list_out))
    next_in = fast_in_next.astype(jnp.bfloat16)
    next_out = fast_out_next.astype(jnp.bfloat16)
    pieces = []
    for head_number in range(HEADS):
        pieces.append(apply_head(queryn[:, head_number, :], next_in[head_number], next_out[head_number]))
    output = jnp.concatenate(pieces, axis=1).astype(jnp.bfloat16)
    return (output, fast_in_next, fast_out_next)
```

```python
import functools
import math

import jax
import jax.numpy as jnp
from jax import lax
from jax.experimental import pallas as pl
from jax.experimental.pallas import tpu as pltpu
from jax.sharding import PartitionSpec as P

BF16 = jnp.bfloat16
F32 = jnp.float32
VMEM_LIMIT = 48 * 1024 * 1024


def rms_rows(matrix):
    return matrix * lax.rsqrt(jnp.mean(matrix * matrix, axis=-1, keepdims=True) + 1e-06)


def normalized_heads(tokens, heads, head_size):
    row_count = tokens.shape[0]
    wide = tokens.astype(jnp.float32).reshape(row_count, heads, head_size)
    return rms_rows(wide).astype(jnp.bfloat16)


def head_increments(key_rows, value_rows, rates, weight_in, weight_out, block_root):
    fast = weight_out.shape[0]
    in_root = 1.0 / math.sqrt(weight_in.shape[0])
    out_root = 1.0 / math.sqrt(fast)
    scaled = (rates[:, None] * block_root * value_rows.astype(jnp.float32)).astype(jnp.bfloat16)
    pre = jnp.dot(key_rows, weight_in, preferred_element_type=jnp.float32) * in_root
    gate = pre[:, :fast]
    upper = pre[:, fast:]
    sigma = jax.nn.sigmoid(gate)
    active = gate * sigma
    hidden = (active * upper).astype(jnp.bfloat16)
    back = (
        lax.dot_general(
            scaled, weight_out, (((1,), (1,)), ((), ())), preferred_element_type=jnp.float32
        )
        * out_root
    )
    d_gate = (back * upper * sigma * (1.0 + gate * (1.0 - sigma))).astype(jnp.bfloat16)
    d_up = (back * active).astype(jnp.bfloat16)
    joined = jnp.concatenate([d_gate, d_up], axis=1)
    inc_in = (
        lax.dot_general(
            key_rows, joined, (((0,), (0,)), ((), ())), preferred_element_type=jnp.float32
        )
        * in_root
    )
    inc_out = (
        lax.dot_general(
            hidden, scaled, (((0,), (0,)), ((), ())), preferred_element_type=jnp.float32
        )
        * out_root
    )
    return (inc_in, inc_out)


def local_increments(keyn, values, step_size, weight_in, weight_out, block_root):
    heads = weight_in.shape[0]
    head_size = weight_in.shape[1]
    list_in = []
    list_out = []
    for head_number in range(heads):
        value_rows = values[:, head_number * head_size : (head_number + 1) * head_size]
        part_in, part_out = head_increments(
            keyn[:, head_number, :],
            value_rows,
            step_size[head_number],
            weight_in[head_number],
            weight_out[head_number],
            block_root,
        )
        list_in.append(part_in)
        list_out.append(part_out)
    return (jnp.stack(list_in), jnp.stack(list_out))


def renorm_in(matrix):
    heads, rows_here, double = matrix.shape
    split = matrix.reshape(heads, rows_here, 2, double // 2)
    return rms_rows(split).reshape(heads, rows_here, double)


def apply_head(query_rows, weight_in, weight_out):
    fast = weight_out.shape[0]
    pre = jnp.dot(query_rows, weight_in, preferred_element_type=jnp.float32) * (
        1.0 / math.sqrt(weight_in.shape[0])
    )
    gate = pre[:, :fast]
    hidden = (gate * jax.nn.sigmoid(gate) * pre[:, fast:]).astype(jnp.bfloat16)
    return jnp.dot(hidden, weight_out, preferred_element_type=jnp.float32) * (1.0 / math.sqrt(fast))


def apply_all(queryn, next_in, next_out):
    heads = next_in.shape[0]
    pieces = []
    for head_number in range(heads):
        pieces.append(
            apply_head(queryn[:, head_number, :], next_in[head_number], next_out[head_number])
        )
    return jnp.concatenate(pieces, axis=1).astype(jnp.bfloat16)


def per_device_generic(queries, keys, values, step_size, fast_in, fast_out):
    row_count = keys.shape[0]
    heads = fast_in.shape[0]
    head_size = keys.shape[1] // heads
    block_root = 1.0 / math.sqrt(row_count * lax.axis_size("tok"))
    keyn = normalized_heads(keys, heads, head_size)
    queryn = normalized_heads(queries, heads, head_size)
    master_in, master_out = (
        lax.all_gather(fast_in, "tok", axis=1, tiled=True),
        lax.all_gather(fast_out, "tok", axis=1, tiled=True),
    )
    inc_in, inc_out = local_increments(
        keyn,
        values,
        step_size,
        master_in.astype(jnp.bfloat16),
        master_out.astype(jnp.bfloat16),
        block_root,
    )
    total_in, total_out = lax.psum((inc_in, inc_out), "tok")
    whole_in = renorm_in(master_in + total_in)
    whole_out = rms_rows(master_out + total_out)
    output = apply_all(queryn, whole_in.astype(jnp.bfloat16), whole_out.astype(jnp.bfloat16))
    place = lax.axis_index("tok")
    fast_in_next = lax.dynamic_slice_in_dim(whole_in, place * fast_in.shape[1], fast_in.shape[1], 1)
    fast_out_next = lax.dynamic_slice_in_dim(
        whole_out, place * fast_out.shape[1], fast_out.shape[1], 1
    )
    return (output, fast_in_next, fast_out_next)


def swap(value, bits):
    count = lax.axis_size("tok")
    return lax.ppermute(value, "tok", [(place, place ^ bits) for place in range(count)])


def compiler_params():
    return pltpu.CompilerParams(vmem_limit_bytes=VMEM_LIMIT)


def normalize_head(block):
    wide = block.astype(F32)
    return (wide * lax.rsqrt(jnp.mean(wide * wide, axis=-1, keepdims=True) + 1e-06)).astype(BF16)


def prepare_kernel(block_root, heads, ids, k_ref, v_ref, r_ref, k_own, k_send, v_own, v_send):
    core = ids[1]
    half = heads // 2
    size = k_ref.shape[1] // heads

    def work(owner, k_out, v_out):
        for local in range(half):
            start = owner * half + local
            columns = pl.ds(pl.multiple_of(start * size, size), size)
            into = slice(local * size, (local + 1) * size)
            k_out[:, into] = normalize_head(k_ref[:, columns])
            first = r_ref[:, local : local + 1]
            second = r_ref[:, half + local : half + local + 1]
            rate = jnp.where(owner == 0, first, second)
            v_out[:, into] = (rate * block_root * v_ref[:, columns].astype(F32)).astype(BF16)

    work(core, k_own, v_own)
    work(1 - core, k_send, v_send)


def prepare(ids, keys, values, rates, block_root, heads):
    rows, width = keys.shape
    step = 256
    wide = pl.BlockSpec((step, width), lambda i, ids: (i, 0))
    narrow = pl.BlockSpec((step, width // 2), lambda i, ids: (i, 0))
    shape = jax.ShapeDtypeStruct((rows, width // 2), BF16)
    return pl.pallas_call(
        functools.partial(prepare_kernel, block_root, heads),
        grid_spec=pltpu.PrefetchScalarGridSpec(
            num_scalar_prefetch=1,
            grid=(rows // step,),
            in_specs=[wide, wide, pl.BlockSpec((step, heads), lambda i, ids: (i, 0))],
            out_specs=[narrow] * 4,
        ),
        out_shape=[shape] * 4,
        compiler_params=compiler_params(),
        cost_estimate=pl.CostEstimate(
            flops=rows * width * 10, bytes_accessed=rows * width * 8, transcendentals=0
        ),
        name="prepare",
    )(ids, keys, values, rates)


def normalize_kernel(heads, x_ref, o_ref):
    size = x_ref.shape[1] // heads
    for head in range(heads):
        columns = slice(head * size, (head + 1) * size)
        o_ref[:, columns] = normalize_head(x_ref[:, columns])


def normalize(tokens, heads):
    rows, width = tokens.shape
    step = 256
    spec = pl.BlockSpec((step, width), lambda i: (i, 0))
    return pl.pallas_call(
        functools.partial(normalize_kernel, heads),
        grid=(rows // step,),
        in_specs=[spec],
        out_specs=spec,
        out_shape=jax.ShapeDtypeStruct((rows, width), BF16),
        compiler_params=compiler_params(),
        cost_estimate=pl.CostEstimate(
            flops=rows * width * 5, bytes_accessed=rows * width * 4, transcendentals=0
        ),
        name="normalize",
    )(tokens)


def places(chip, core):
    for side in range(2):
        for slot in range(4):
            other = jnp.bitwise_xor(chip, 2 * slot + side)
            for source in range(2):
                yield side, slot, source, 2 * other + jnp.bitwise_xor(core, source)


def assemble(chip, core, sides, w_in, w_out):
    size = w_out.shape[1]
    blocks = w_in.shape[1] // size
    rows_in = w_in.shape[0] // 16
    rows_out = w_out.shape[0] // 16
    for side, slot, source, place in places(chip, core):
        ref = sides[side]
        into = pl.ds(pl.multiple_of(place * rows_in, rows_in), rows_in)
        for block in range(blocks):
            w_in[into, block * size : (block + 1) * size] = ref[
                slot, source, block * rows_in : (block + 1) * rows_in, :
            ]
        into = pl.ds(pl.multiple_of(place * rows_out, rows_out), rows_out)
        w_out[into, :] = ref[slot, source, blocks * rows_in :, :]


def update_kernel(
    local, ids, near, far, k_own, v_own, k_got, v_got, keep, send, w_in, w_out, acc_in, acc_out, turned
):
    step = pl.program_id(0)
    steps = pl.num_programs(0)
    chip, core = ids[0], ids[1]
    size = w_out.shape[1]
    fast = w_out.shape[0]
    in_root = 1.0 / math.sqrt(size)
    out_root = 1.0 / math.sqrt(fast)

    @pl.when(step == 0)
    def _():
        assemble(chip, core, (near, far), w_in, w_out)
        acc_in[...] = jnp.zeros_like(acc_in)
        acc_out[...] = jnp.zeros_like(acc_out)

    def work(k_ref, v_ref):
        keyn = k_ref[...]
        scaled = v_ref[...]
        chunk = 256
        for start in range(0, fast, chunk):
            gates = slice(start, start + chunk)
            ups = slice(fast + start, fast + start + chunk)
            gate = jnp.dot(keyn, w_in[:, gates], preferred_element_type=F32) * in_root
            upper = jnp.dot(keyn, w_in[:, ups], preferred_element_type=F32) * in_root
            back = (
                lax.dot_general(
                    scaled, w_out[gates, :], (((1,), (1,)), ((), ())), preferred_element_type=F32
                )
                * out_root
            )
            sigma = jax.nn.sigmoid(gate)
            active = gate * sigma
            hidden = (active * upper).astype(BF16)
            d_gate = (back * upper * sigma * (1.0 + gate * (1.0 - sigma))).astype(BF16)
            d_up = (back * active).astype(BF16)
            over = (((0,), (0,)), ((), ()))
            acc_in[:, gates] += lax.dot_general(keyn, d_gate, over, preferred_element_type=F32)
            acc_in[:, ups] += lax.dot_general(keyn, d_up, over, preferred_element_type=F32)
            acc_out[:, gates] += lax.dot_general(scaled, hidden, over, preferred_element_type=F32)

    @pl.when(step < steps // 2)
    def _():
        work(k_own, v_own)

    @pl.when(step >= steps // 2)
    def _():
        work(k_got, v_got)

    @pl.when(step == steps - 1)
    def _():
        turned[...] = acc_out[...].T
        blocks = acc_in.shape[1] // size
        rows_in = acc_in.shape[0] // 16
        rows_out = turned.shape[0] // 16
        for side, slot, source, place in places(chip, core):
            ref = (keep, send)[side]
            rows = pl.ds(pl.multiple_of(place * rows_in, rows_in), rows_in)
            for block in range(blocks):
                ref[slot, source, block * rows_in : (block + 1) * rows_in, :] = (
                    acc_in[rows, block * size : (block + 1) * size] * in_root
                ).astype(ref.dtype)
            rows = pl.ds(pl.multiple_of(place * rows_out, rows_out), rows_out)
            ref[slot, source, blocks * rows_in :, :] = (turned[rows, :] * out_root).astype(ref.dtype)


def increments(ids, local, near, far, k_own, v_own, k_got, v_got, fast):
    rows = k_own.shape[0]
    size = near.shape[-1]
    step = 512
    half = rows // step
    whole = pl.BlockSpec(near.shape, lambda i, ids: (0, 0, 0, 0))
    own = pl.BlockSpec((step, size), lambda i, ids: (jnp.minimum(i, half - 1), local))
    got = pl.BlockSpec((step, size), lambda i, ids: (jnp.maximum(i - half, 0), local))
    return pl.pallas_call(
        functools.partial(update_kernel, local),
        grid_spec=pltpu.PrefetchScalarGridSpec(
            num_scalar_prefetch=1,
            grid=(2 * half,),
            in_specs=[whole, whole, own, own, got, got],
            out_specs=[whole, whole],
            scratch_shapes=[
                pltpu.VMEM((size, 2 * fast), BF16),
                pltpu.VMEM((fast, size), BF16),
                pltpu.VMEM((size, 2 * fast), F32),
                pltpu.VMEM((size, fast), F32),
                pltpu.VMEM((fast, size), F32),
            ],
        ),
        out_shape=[jax.ShapeDtypeStruct(near.shape, F32), jax.ShapeDtypeStruct(near.shape, BF16)],
        compiler_params=compiler_params(),
        cost_estimate=pl.CostEstimate(
            flops=2 * rows * size * fast * 12, bytes_accessed=rows * size * 8, transcendentals=0
        ),
        name="increments",
    )(ids, near, far, k_own, v_own, k_got, v_got)


def renorm_kernel(size_in, master, kept, one, two, three, wide, short):
    fresh = (
        master[...]
        + kept[...]
        + one[...].astype(F32)
        + two[...].astype(F32)
        + three[...].astype(F32)
    )
    size = fresh.shape[-1]
    blocks = 4
    rows_in = size_in
    for source in range(2):
        for part in range(2):
            first = 2 * part * rows_in
            left = fresh[source, first : first + rows_in, :]
            right = fresh[source, first + rows_in : first + 2 * rows_in, :]
            total = jnp.sum(left * left + right * right, axis=-1, keepdims=True)
            factor = lax.rsqrt(total * (1.0 / (2 * size)) + 1e-06)
            for at, value in ((first, left), (first + rows_in, right)):
                done = value * factor
                wide[source, at : at + rows_in, :] = done
                short[source, at : at + rows_in, :] = done.astype(BF16)
        tail = fresh[source, blocks * rows_in :, :]
        done = tail * lax.rsqrt(jnp.mean(tail * tail, axis=-1, keepdims=True) + 1e-06)
        wide[source, blocks * rows_in :, :] = done
        short[source, blocks * rows_in :, :] = done.astype(BF16)


def renorm(master, kept, one, two, three, rows_in):
    shape = master.shape
    return pl.pallas_call(
        functools.partial(renorm_kernel, rows_in),
        out_shape=[jax.ShapeDtypeStruct(shape, F32), jax.ShapeDtypeStruct(shape, BF16)],
        compiler_params=compiler_params(),
        name="renorm",
    )(master, kept, one, two, three)


def apply_kernel(other, ids, near, far, q_ref, *rest):
    o_ref, w_in, w_out = rest[-3:]
    chip, core = ids[0], ids[1]
    fast = w_out.shape[0]

    @pl.when(pl.program_id(0) == 0)
    def _():
        assemble(chip, core ^ other, (near, far), w_in, w_out)

    query = q_ref[...]
    in_root = 1.0 / math.sqrt(w_out.shape[1])
    gate = jnp.dot(query, w_in[:, :fast], preferred_element_type=F32) * in_root
    upper = jnp.dot(query, w_in[:, fast:], preferred_element_type=F32) * in_root
    hidden = (gate * jax.nn.sigmoid(gate) * upper).astype(BF16)
    result = jnp.dot(hidden, w_out[...], preferred_element_type=F32) * (1.0 / math.sqrt(fast))
    o_ref[...] = result.astype(BF16)


def apply_fast(ids, local, other, near, far, queryn, output, fast, heads):
    rows, width = queryn.shape
    size = near.shape[-1]
    step = 512
    half = heads // 2
    whole = pl.BlockSpec(near.shape, lambda i, ids: (0, 0, 0, 0))
    column = pl.BlockSpec((step, size), lambda i, ids: (i, half * (ids[1] ^ other) + local))
    operands = [ids, near, far, queryn]
    specs = [whole, whole, column]
    aliases = {}
    if output is not None:
        operands.append(output)
        specs.append(pl.BlockSpec(memory_space=pl.ANY))
        aliases = {4: 0}
    return pl.pallas_call(
        functools.partial(apply_kernel, other),
        grid_spec=pltpu.PrefetchScalarGridSpec(
            num_scalar_prefetch=1,
            grid=(rows // step,),
            in_specs=specs,
            out_specs=column,
            scratch_shapes=[pltpu.VMEM((size, 2 * fast), BF16), pltpu.VMEM((fast, size), BF16)],
        ),
        out_shape=jax.ShapeDtypeStruct((rows, width), BF16),
        input_output_aliases=aliases,
        compiler_params=compiler_params(),
        cost_estimate=pl.CostEstimate(
            flops=2 * rows * size * fast * 3, bytes_accessed=rows * size * 4, transcendentals=0
        ),
        name="apply",
    )(*operands)


def pack(fast_in, fast_out):
    heads, rows, double = fast_in.shape
    size = fast_out.shape[-1]
    blocks = fast_in.reshape(heads, rows, double // size, size).transpose(0, 2, 1, 3)
    return jnp.concatenate([blocks.reshape(heads, -1, size), fast_out], axis=1)


def unpack(packed, rows):
    heads, _, size = packed.shape
    blocks = packed[:, : 4 * rows].reshape(heads, 4, rows, size).transpose(0, 2, 1, 3)
    return blocks.reshape(heads, rows, 4 * size), packed[:, 4 * rows :]


def gather_chips(shard):
    line = jnp.stack([shard, swap(shard, 4), swap(shard, 8), swap(shard, 12)])
    return line, swap(line, 2)


def per_device_cube(queries, keys, values, step_size, fast_in, fast_out):
    rows = keys.shape[0]
    heads = fast_in.shape[0]
    half = heads // 2
    fast = fast_in.shape[2] // 2
    rows_in = fast_in.shape[1]
    place = lax.axis_index("tok")
    core = place % 2
    ids = jnp.stack([place // 2, core]).astype(jnp.int32)
    block_root = 1.0 / math.sqrt(rows * lax.axis_size("tok"))

    packed = pack(fast_in, fast_out)
    own = lax.dynamic_slice_in_dim(packed, core * half, half, 0)
    theirs = lax.dynamic_slice_in_dim(packed, (1 - core) * half, half, 0)
    got = swap(theirs, 1)
    masters = [jnp.stack([own[local], got[local]]) for local in range(half)]
    lines = [gather_chips(master.astype(BF16)) for master in masters]

    k_own, k_send, v_own, v_send = prepare(ids, keys, values, step_size.T, block_root, heads)
    k_got, v_got = swap(k_send, 1), swap(v_send, 1)
    queryn = normalize(queries, heads)

    fresh = []
    for local in range(half):
        keep, send = increments(ids, local, *lines[local], k_own, v_own, k_got, v_got, fast)
        total = keep + swap(send, 2).astype(F32)
        arrived = [swap(total[slot].astype(BF16), 4 * slot) for slot in (1, 2, 3)]
        fresh.append(renorm(masters[local], total[0], *arrived, rows_in))

    output = None
    for local in range(half):
        near, far = gather_chips(fresh[local][1])
        near_other, far_other = swap(near, 1), swap(far, 1)
        output = apply_fast(ids, local, 0, near, far, queryn, output, fast, heads)
        output = apply_fast(ids, local, 1, near_other, far_other, queryn, output, fast, heads)

    mine = jnp.stack([wide[0] for wide, _ in fresh])
    back = swap(jnp.stack([wide[1] for wide, _ in fresh]), 1)
    both = jnp.where(core == 0, jnp.concatenate([mine, back]), jnp.concatenate([back, mine]))
    return (output, *unpack(both, rows_in))


def per_device(queries, keys, values, step_size, fast_in, fast_out):
    fits = lax.axis_size("tok") == 16 and fast_in.shape[1] % 16 == 0 and fast_in.shape[0] % 2 == 0
    chosen = per_device_cube if fits else per_device_generic
    return chosen(queries, keys, values, step_size, fast_in, fast_out)


def solution(mesh):
    placed = (
        P(("parts", "tok"), None),
        P(("parts", "tok"), None),
        P(("parts", "tok"), None),
        P(None, ("parts", "tok")),
        P(None, "tok", None),
        P(None, "tok", None),
    )
    return jax.shard_map(
        per_device,
        mesh=mesh,
        in_specs=placed,
        out_specs=(P(("parts", "tok"), None), P("parts", "tok", None), P("parts", "tok", None)),
        check_vma=False,
    )
```

```python
import functools
import math

import jax
import jax.numpy as jnp
from jax import lax
from jax.experimental import pallas as pl
from jax.experimental.pallas import tpu as pltpu
from jax.sharding import PartitionSpec as P

BF16 = jnp.bfloat16
F32 = jnp.float32
VMEM_LIMIT = 48 * 1024 * 1024


def rms_rows(matrix):
    return matrix * lax.rsqrt(jnp.mean(matrix * matrix, axis=-1, keepdims=True) + 1e-06)


def normalized_heads(tokens, heads, head_size):
    row_count = tokens.shape[0]
    wide = tokens.astype(jnp.float32).reshape(row_count, heads, head_size)
    return rms_rows(wide).astype(jnp.bfloat16)


def head_increments(key_rows, value_rows, rates, weight_in, weight_out, block_root):
    fast = weight_out.shape[0]
    in_root = 1.0 / math.sqrt(weight_in.shape[0])
    out_root = 1.0 / math.sqrt(fast)
    scaled = (rates[:, None] * block_root * value_rows.astype(jnp.float32)).astype(jnp.bfloat16)
    pre = jnp.dot(key_rows, weight_in, preferred_element_type=jnp.float32) * in_root
    gate = pre[:, :fast]
    upper = pre[:, fast:]
    sigma = jax.nn.sigmoid(gate)
    active = gate * sigma
    hidden = (active * upper).astype(jnp.bfloat16)
    back = (
        lax.dot_general(
            scaled, weight_out, (((1,), (1,)), ((), ())), preferred_element_type=jnp.float32
        )
        * out_root
    )
    d_gate = (back * upper * sigma * (1.0 + gate * (1.0 - sigma))).astype(jnp.bfloat16)
    d_up = (back * active).astype(jnp.bfloat16)
    joined = jnp.concatenate([d_gate, d_up], axis=1)
    inc_in = (
        lax.dot_general(
            key_rows, joined, (((0,), (0,)), ((), ())), preferred_element_type=jnp.float32
        )
        * in_root
    )
    inc_out = (
        lax.dot_general(
            hidden, scaled, (((0,), (0,)), ((), ())), preferred_element_type=jnp.float32
        )
        * out_root
    )
    return (inc_in, inc_out)


def local_increments(keyn, values, step_size, weight_in, weight_out, block_root):
    heads = weight_in.shape[0]
    head_size = weight_in.shape[1]
    list_in = []
    list_out = []
    for head_number in range(heads):
        value_rows = values[:, head_number * head_size : (head_number + 1) * head_size]
        part_in, part_out = head_increments(
            keyn[:, head_number, :],
            value_rows,
            step_size[head_number],
            weight_in[head_number],
            weight_out[head_number],
            block_root,
        )
        list_in.append(part_in)
        list_out.append(part_out)
    return (jnp.stack(list_in), jnp.stack(list_out))


def renorm_in(matrix):
    heads, rows_here, double = matrix.shape
    split = matrix.reshape(heads, rows_here, 2, double // 2)
    return rms_rows(split).reshape(heads, rows_here, double)


def apply_head(query_rows, weight_in, weight_out):
    fast = weight_out.shape[0]
    pre = jnp.dot(query_rows, weight_in, preferred_element_type=jnp.float32) * (
        1.0 / math.sqrt(weight_in.shape[0])
    )
    gate = pre[:, :fast]
    hidden = (gate * jax.nn.sigmoid(gate) * pre[:, fast:]).astype(jnp.bfloat16)
    return jnp.dot(hidden, weight_out, preferred_element_type=jnp.float32) * (1.0 / math.sqrt(fast))


def apply_all(queryn, next_in, next_out):
    heads = next_in.shape[0]
    pieces = []
    for head_number in range(heads):
        pieces.append(
            apply_head(queryn[:, head_number, :], next_in[head_number], next_out[head_number])
        )
    return jnp.concatenate(pieces, axis=1).astype(jnp.bfloat16)


def per_device_generic(queries, keys, values, step_size, fast_in, fast_out):
    row_count = keys.shape[0]
    heads = fast_in.shape[0]
    head_size = keys.shape[1] // heads
    block_root = 1.0 / math.sqrt(row_count * lax.axis_size("tok"))
    keyn = normalized_heads(keys, heads, head_size)
    queryn = normalized_heads(queries, heads, head_size)
    master_in, master_out = (
        lax.all_gather(fast_in, "tok", axis=1, tiled=True),
        lax.all_gather(fast_out, "tok", axis=1, tiled=True),
    )
    inc_in, inc_out = local_increments(
        keyn,
        values,
        step_size,
        master_in.astype(jnp.bfloat16),
        master_out.astype(jnp.bfloat16),
        block_root,
    )
    total_in, total_out = lax.psum((inc_in, inc_out), "tok")
    whole_in = renorm_in(master_in + total_in)
    whole_out = rms_rows(master_out + total_out)
    output = apply_all(queryn, whole_in.astype(jnp.bfloat16), whole_out.astype(jnp.bfloat16))
    place = lax.axis_index("tok")
    fast_in_next = lax.dynamic_slice_in_dim(whole_in, place * fast_in.shape[1], fast_in.shape[1], 1)
    fast_out_next = lax.dynamic_slice_in_dim(
        whole_out, place * fast_out.shape[1], fast_out.shape[1], 1
    )
    return (output, fast_in_next, fast_out_next)


def swap(value, bits):
    count = lax.axis_size("tok")
    return lax.ppermute(value, "tok", [(place, place ^ bits) for place in range(count)])


def swap_parts(value):
    return lax.ppermute(value, "parts", [(0, 1), (1, 0)])


def after(value, *before):
    return lax.optimization_barrier((value, before))[0]


def compiler_params():
    return pltpu.CompilerParams(vmem_limit_bytes=VMEM_LIMIT)


def head_of(ids, order, other):
    return 2 * jnp.bitwise_xor(ids[1], other) + jnp.bitwise_xor(ids[2], order)


def normalize_head(block):
    wide = block.astype(F32)
    return (wide * lax.rsqrt(jnp.mean(wide * wide, axis=-1, keepdims=True) + 1e-06)).astype(BF16)


def pack_kernel(ids, in_ref, out_ref, own, theirs):
    size = out_ref.shape[-1]
    rows = in_ref.shape[1]
    for other, ref in ((0, own), (1, theirs)):
        for order in range(2):
            head = head_of(ids, order, other)
            for block in range(in_ref.shape[2] // size):
                ref[order, block * rows : (block + 1) * rows, :] = in_ref[
                    head, :, block * size : (block + 1) * size
                ]
            ref[order, -out_ref.shape[1] :, :] = out_ref[head]


def pack(ids, fast_in, fast_out):
    rows = 4 * fast_in.shape[1] + fast_out.shape[1]
    shape = jax.ShapeDtypeStruct((2, rows, fast_out.shape[2]), F32)
    return pl.pallas_call(
        pack_kernel,
        in_specs=[pl.BlockSpec(memory_space=pltpu.SMEM)] + [pl.BlockSpec(memory_space=pltpu.VMEM)] * 2,
        out_shape=[shape, shape],
        compiler_params=compiler_params(),
        name="pack",
    )(ids, fast_in, fast_out)


def pair_kernel(own, got, master_one, master_two, shard):
    for source, ref in enumerate((own, got)):
        for order, master in enumerate((master_one, master_two)):
            master[source] = ref[order]
        shard[source] = ref[0].astype(BF16)


def pair(own, got):
    wide = jax.ShapeDtypeStruct(own.shape, F32)
    return pl.pallas_call(
        pair_kernel,
        out_shape=[wide, wide, jax.ShapeDtypeStruct(own.shape, BF16)],
        compiler_params=compiler_params(),
        name="pair",
    )(own, got)


def prepare_kernel(heads, ids, x_ref, *rest):
    own, send = rest[-2:]
    core = ids[1]
    half = heads // 2
    size = x_ref.shape[1] // heads

    def work(owner, out):
        for local in range(half):
            columns = pl.ds(pl.multiple_of((owner * half + local) * size, size), size)
            into = slice(local * size, (local + 1) * size)
            if len(rest) == 2:
                out[:, into] = normalize_head(x_ref[:, columns])
            else:
                first = rest[0][:, local : local + 1]
                second = rest[0][:, half + local : half + local + 1]
                rate = jnp.where(owner == 0, first, second)
                out[:, into] = (rate * x_ref[:, columns].astype(F32)).astype(BF16)

    work(core, own)
    work(1 - core, send)


def prepare(ids, tokens, rates, heads, name):
    rows, width = tokens.shape
    step = 256
    wide = pl.BlockSpec((step, width), lambda i, ids: (i, 0))
    narrow = pl.BlockSpec((step, width // 2), lambda i, ids: (i, 0))
    operands, specs = [tokens], [wide]
    if rates is not None:
        operands.append(rates)
        specs.append(pl.BlockSpec((step, heads), lambda i, ids: (i, 0)))
    shape = jax.ShapeDtypeStruct((rows, width // 2), BF16)
    return pl.pallas_call(
        functools.partial(prepare_kernel, heads),
        grid_spec=pltpu.PrefetchScalarGridSpec(
            num_scalar_prefetch=1,
            grid=(rows // step,),
            in_specs=specs,
            out_specs=[narrow] * 2,
        ),
        out_shape=[shape] * 2,
        compiler_params=compiler_params(),
        cost_estimate=pl.CostEstimate(
            flops=rows, bytes_accessed=rows, transcendentals=0
        ),
        name=name,
    )(ids, *operands)


def places(chip, core):
    for side in range(2):
        for slot in range(4):
            other = jnp.bitwise_xor(chip, 2 * slot + side)
            for source in range(2):
                yield side, slot, source, 2 * other + jnp.bitwise_xor(core, source)


def assemble(chip, core, lines, w_in, w_out):
    size = w_out.shape[1]
    blocks = w_in.shape[1] // size
    rows_in = w_in.shape[0] // 16
    rows_out = w_out.shape[0] // 16
    for side, slot, source, place in places(chip, core):
        ref = lines[2 * side + slot // 2].at[slot % 2]
        into = pl.ds(pl.multiple_of(place * rows_in, rows_in), rows_in)
        for block in range(blocks):
            w_in[into, block * size : (block + 1) * size] = ref[
                source, block * rows_in : (block + 1) * rows_in, :
            ]
        into = pl.ds(pl.multiple_of(place * rows_out, rows_out), rows_out)
        w_out[into, :] = ref[source, blocks * rows_in :, :]


def increments_kernel(
    ids, near_low, near_high, far_low, far_high, k_own, v_own, k_got, v_got,
    kept, low, high, w_in, w_out, acc_in, acc_out, turned,
):
    step = pl.program_id(0)
    steps = pl.num_programs(0)
    chip, core = ids[0], ids[1]
    size = w_out.shape[1]
    fast = w_out.shape[0]
    in_root = 1.0 / math.sqrt(size)
    out_root = 1.0 / math.sqrt(fast)

    @pl.when(step == 0)
    def _():
        assemble(chip, core, (near_low, near_high, far_low, far_high), w_in, w_out)

    def work(k_ref, v_ref, start_over):
        keyn = k_ref[...]
        scaled = v_ref[...]
        keyn_t = keyn.T
        scaled_t = scaled.T

        def add(ref, columns, value):
            if start_over:
                ref[:, columns] = value
            else:
                ref[:, columns] += value

        chunk = 256
        for start in range(0, fast, chunk):
            gates = slice(start, start + chunk)
            ups = slice(fast + start, fast + start + chunk)
            gate = jnp.dot(keyn, w_in[:, gates], preferred_element_type=F32) * in_root
            upper = jnp.dot(keyn, w_in[:, ups], preferred_element_type=F32) * in_root
            back = (
                lax.dot_general(
                    scaled, w_out[gates, :], (((1,), (1,)), ((), ())), preferred_element_type=F32
                )
                * out_root
            )
            sigma = 0.5 * jnp.tanh(0.5 * gate) + 0.5
            active = gate * sigma
            hidden = (active * upper).astype(BF16)
            d_gate = (back * upper * (sigma + active * (1.0 - sigma))).astype(BF16)
            d_up = (back * active).astype(BF16)
            add(acc_in, gates, jnp.dot(keyn_t, d_gate, preferred_element_type=F32))
            add(acc_in, ups, jnp.dot(keyn_t, d_up, preferred_element_type=F32))
            add(acc_out, gates, jnp.dot(scaled_t, hidden, preferred_element_type=F32))

    @pl.when(step == 0)
    def _():
        work(k_own, v_own, True)

    if k_own.shape[0] * 2 < 2048:

        @pl.when((step > 0) & (step < steps // 2))
        def _():
            work(k_own, v_own, False)

    @pl.when(step >= steps // 2)
    def _():
        work(k_got, v_got, False)

    @pl.when(step == steps - 1)
    def _():
        turned[...] = acc_out[...].T
        blocks = acc_in.shape[1] // size
        rows_in = acc_in.shape[0] // 16
        rows_out = turned.shape[0] // 16
        for side, slot, source, place in places(chip, core):
            ref = kept.at[slot] if side == 0 else (low, high)[slot // 2].at[slot % 2]
            rows = pl.ds(pl.multiple_of(place * rows_in, rows_in), rows_in)
            for block in range(blocks):
                ref[source, block * rows_in : (block + 1) * rows_in, :] = (
                    acc_in[rows, block * size : (block + 1) * size] * in_root
                ).astype(ref.dtype)
            rows = pl.ds(pl.multiple_of(place * rows_out, rows_out), rows_out)
            ref[source, blocks * rows_in :, :] = (turned[rows, :] * out_root).astype(ref.dtype)


def increments(ids, order, lines, k_own, v_own, k_got, v_got, fast):
    rows = k_own.shape[0]
    pair_shape = lines[0].shape
    size = pair_shape[-1]
    step = rows
    half = rows // step
    whole = pl.BlockSpec(pair_shape, lambda i, ids: (0, 0, 0, 0))
    line_shape = (4,) + pair_shape[1:]
    line = pl.BlockSpec(line_shape, lambda i, ids: (0, 0, 0, 0))
    own = pl.BlockSpec((step, size), lambda i, ids: (jnp.minimum(i, half - 1), ids[2] ^ order))
    got = pl.BlockSpec((step, size), lambda i, ids: (jnp.maximum(i - half, 0), ids[2] ^ order))
    return pl.pallas_call(
        increments_kernel,
        grid_spec=pltpu.PrefetchScalarGridSpec(
            num_scalar_prefetch=1,
            grid=(2 * half,),
            in_specs=[whole] * 4 + [own, own, got, got],
            out_specs=[line, whole, whole],
            scratch_shapes=[
                pltpu.VMEM((size, 2 * fast), BF16),
                pltpu.VMEM((fast, size), BF16),
                pltpu.VMEM((size, 2 * fast), F32),
                pltpu.VMEM((size, fast), F32),
                pltpu.VMEM((fast, size), F32),
            ],
        ),
        out_shape=[
            jax.ShapeDtypeStruct(line_shape, F32),
            jax.ShapeDtypeStruct(pair_shape, BF16),
            jax.ShapeDtypeStruct(pair_shape, BF16),
        ],
        compiler_params=compiler_params(),
        cost_estimate=pl.CostEstimate(
            flops=2 * rows * size * fast * 12, bytes_accessed=rows * size * 8, transcendentals=0
        ),
        name="increments",
    )(ids, *lines, k_own, v_own, k_got, v_got)


def add_kernel(kept, came, first, second):
    first[...] = (kept[0] + came[0].astype(F32)).astype(first.dtype)
    second[...] = (kept[1] + came[1].astype(F32)).astype(second.dtype)


def add_pair(kept, came, which, first_type):
    shape = came.shape
    flat = (0,) * (len(shape) - 1)
    return pl.pallas_call(
        add_kernel,
        grid=(1,),
        in_specs=[
            pl.BlockSpec(shape, lambda i: (which,) + flat),
            pl.BlockSpec(shape, lambda i: (0,) + flat),
        ],
        out_specs=[pl.BlockSpec(shape[1:], lambda i: flat)] * 2,
        out_shape=[
            jax.ShapeDtypeStruct(shape[1:], first_type),
            jax.ShapeDtypeStruct(shape[1:], BF16),
        ],
        compiler_params=compiler_params(),
        name="add_pair",
    )(kept, came)


def renorm_kernel(rows_in, master, kept, one, two, three, wide, short):
    size = master.shape[-1]
    for source in range(2):
        fresh = (
            master[source]
            + kept[source]
            + one[source].astype(F32)
            + two[source].astype(F32)
            + three[source].astype(F32)
        )
        for part in range(2):
            first = 2 * part * rows_in
            left = fresh[first : first + rows_in, :]
            right = fresh[first + rows_in : first + 2 * rows_in, :]
            total = jnp.sum(left * left + right * right, axis=-1, keepdims=True)
            factor = lax.rsqrt(total * (1.0 / (2 * size)) + 1e-06)
            for at, value in ((first, left), (first + rows_in, right)):
                done = value * factor
                wide[source, at : at + rows_in, :] = done
                short[source, at : at + rows_in, :] = done.astype(BF16)
        tail = fresh[4 * rows_in :, :]
        done = tail * lax.rsqrt(jnp.mean(tail * tail, axis=-1, keepdims=True) + 1e-06)
        wide[source, 4 * rows_in :, :] = done
        short[source, 4 * rows_in :, :] = done.astype(BF16)


def renorm(master, kept, one, two, three, rows_in):
    shape = master.shape
    return pl.pallas_call(
        functools.partial(renorm_kernel, rows_in),
        out_shape=[jax.ShapeDtypeStruct(shape, F32), jax.ShapeDtypeStruct(shape, BF16)],
        compiler_params=compiler_params(),
        name="renorm",
    )(master, kept, one, two, three)


def apply_kernel(other, ids, near_low, near_high, far_low, far_high, q_ref, *rest):
    o_ref, w_in, w_out = rest[-3:]
    chip, core = ids[0], ids[1]
    fast = w_out.shape[0]

    @pl.when(pl.program_id(0) == 0)
    def _():
        lines = (near_low, near_high, far_low, far_high)
        assemble(chip, jnp.bitwise_xor(core, other), lines, w_in, w_out)

    query = normalize_head(q_ref[...])
    in_root = 1.0 / math.sqrt(w_out.shape[1])
    gate = jnp.dot(query, w_in[:, :fast], preferred_element_type=F32) * in_root
    upper = jnp.dot(query, w_in[:, fast:], preferred_element_type=F32) * in_root
    hidden = (gate * (0.5 * jnp.tanh(0.5 * gate) + 0.5) * upper).astype(BF16)
    result = jnp.dot(hidden, w_out[...], preferred_element_type=F32) * (1.0 / math.sqrt(fast))
    o_ref[...] = result.astype(BF16)


def apply_fast(ids, order, other, lines, queries, output, fast):
    rows, width = queries.shape
    pair_shape = lines[0].shape
    size = pair_shape[-1]
    step = 512
    whole = pl.BlockSpec(pair_shape, lambda i, ids: (0, 0, 0, 0))
    column = pl.BlockSpec((step, size), lambda i, ids: (i, 2 * (ids[1] ^ other) + (ids[2] ^ order)))
    operands = [ids, *lines, queries]
    specs = [whole] * 4 + [column]
    aliases = {}
    if output is not None:
        operands.append(output)
        specs.append(pl.BlockSpec(memory_space=pl.ANY))
        aliases = {6: 0}
    return pl.pallas_call(
        functools.partial(apply_kernel, other),
        grid_spec=pltpu.PrefetchScalarGridSpec(
            num_scalar_prefetch=1,
            grid=(rows // step,),
            in_specs=specs,
            out_specs=column,
            scratch_shapes=[pltpu.VMEM((size, 2 * fast), BF16), pltpu.VMEM((fast, size), BF16)],
        ),
        out_shape=jax.ShapeDtypeStruct((rows, width), BF16),
        input_output_aliases=aliases,
        compiler_params=compiler_params(),
        cost_estimate=pl.CostEstimate(
            flops=2 * rows * size * fast * 3, bytes_accessed=rows * size * 4, transcendentals=0
        ),
        name="apply",
    )(*operands)


def finish_kernel(rows_in, ids, one, two, came, in_next, out_next):
    size = out_next.shape[-1]
    for order, mine in enumerate((one, two)):
        for other, ref in ((0, mine.at[0]), (1, came.at[order])):
            head = head_of(ids, order, other)
            for block in range(4):
                in_next[head, :, block * size : (block + 1) * size] = ref[
                    block * rows_in : (block + 1) * rows_in, :
                ]
            out_next[head] = ref[4 * rows_in :, :]


def finish(ids, one, two, came, fast_in, fast_out):
    return pl.pallas_call(
        functools.partial(finish_kernel, fast_in.shape[1]),
        in_specs=[pl.BlockSpec(memory_space=pltpu.SMEM)] + [pl.BlockSpec(memory_space=pltpu.VMEM)] * 3,
        out_shape=[
            jax.ShapeDtypeStruct(fast_in.shape, F32),
            jax.ShapeDtypeStruct(fast_out.shape, F32),
        ],
        compiler_params=compiler_params(),
        name="finish",
    )(ids, one, two, came)


def per_device_cube(queries, keys, values, step_size, fast_in, fast_out):
    rows = keys.shape[0]
    heads = fast_in.shape[0]
    fast = fast_in.shape[2] // 2
    rows_in = fast_in.shape[1]
    place = lax.axis_index("tok")
    ids = jnp.stack([place // 2, place % 2, lax.axis_index("parts")]).astype(jnp.int32)
    block_root = 1.0 / math.sqrt(rows * lax.axis_size("tok"))

    own, theirs = pack(ids, fast_in, fast_out)
    got = swap(theirs, 1)
    master_one, master_two, shard = pair(own, got)
    masters = (master_one, master_two)
    z1, z2, z3 = swap(shard, 4), swap(shard, 8), swap(shard, 12)
    near_low = jnp.stack([shard, z1])
    near_high = jnp.stack([z2, z3])
    far_low, far_high = swap(near_low, 2), swap(near_high, 2)
    first = (near_low, near_high, far_low, far_high)
    second = tuple(swap_parts(piece) for piece in first)

    k_own, k_send = prepare(ids, after(keys, shard), None, heads, "keys")
    v_own, v_send = prepare(ids, after(values, z1), step_size.T * block_root, heads, "values")
    k_got, v_got = swap(k_send, 1), swap(v_send, 1)

    kept, low, high = [], [], []
    for order, lines in enumerate((first, second)):
        a, b, c = increments(ids, order, lines, k_own, v_own, k_got, v_got, fast)
        kept.append(a)
        low.append(swap(b, 2))
        high.append(swap(c, 2))
    wide, short = [], []
    for order in range(2):
        sum2, sum3 = add_pair(kept[order], high[order], 1, BF16)
        sum0, sum1 = add_pair(kept[order], low[order], 0, F32)
        three, two, one = swap(sum3, 12), swap(sum2, 8), swap(sum1, 4)
        a, b = renorm(masters[order], sum0, one, two, three, rows_in)
        wide.append(a)
        short.append(b)

    output = None
    for order in range(2):
        shard = short[order]
        z3, z2, z1 = swap(shard, 12), swap(shard, 8), swap(shard, 4)
        near_low = jnp.stack([shard, z1])
        near_high = jnp.stack([z2, z3])
        far = (swap(near_low, 2), swap(near_high, 2))
        if order:
            far = after(far, output)
        mine = (near_low, near_high, *far)
        others = tuple(swap(piece, 1) for piece in mine)
        output = apply_fast(ids, order, 0, mine, queries, output, fast)
        output = apply_fast(ids, order, 1, others, queries, output, fast)

    came = swap(jnp.stack([wide[0][1], wide[1][1]]), 1)
    return (output, *finish(ids, wide[0], wide[1], came, fast_in, fast_out))


def per_device(queries, keys, values, step_size, fast_in, fast_out):
    fits = (
        lax.axis_size("tok") == 16
        and lax.axis_size("parts") == 2
        and fast_in.shape[0] == 4
        and fast_in.shape[1] % 16 == 0
    )
    chosen = per_device_cube if fits else per_device_generic
    return chosen(queries, keys, values, step_size, fast_in, fast_out)


def solution(mesh):
    placed = (
        P(("parts", "tok"), None),
        P(("parts", "tok"), None),
        P(("parts", "tok"), None),
        P(None, ("parts", "tok")),
        P(None, "tok", None),
        P(None, "tok", None),
    )
    return jax.shard_map(
        per_device,
        mesh=mesh,
        in_specs=placed,
        out_specs=(P(("parts", "tok"), None), P("parts", "tok", None), P("parts", "tok", None)),
        check_vma=False,
    )
```

```python
import functools
import math

import jax
import jax.numpy as jnp
from jax import lax
from jax.experimental import pallas as pl
from jax.experimental.pallas import tpu as pltpu
from jax.sharding import PartitionSpec as P

BF16 = jnp.bfloat16
F32 = jnp.float32
VMEM_LIMIT = 48 * 1024 * 1024
VMEM_ALL = 63 * 1024 * 1024


def rms_rows(matrix):
    return matrix * lax.rsqrt(jnp.mean(matrix * matrix, axis=-1, keepdims=True) + 1e-06)


def normalized_heads(tokens, heads, head_size):
    row_count = tokens.shape[0]
    wide = tokens.astype(jnp.float32).reshape(row_count, heads, head_size)
    return rms_rows(wide).astype(jnp.bfloat16)


def head_increments(key_rows, value_rows, rates, weight_in, weight_out, block_root):
    fast = weight_out.shape[0]
    in_root = 1.0 / math.sqrt(weight_in.shape[0])
    out_root = 1.0 / math.sqrt(fast)
    scaled = (rates[:, None] * block_root * value_rows.astype(jnp.float32)).astype(jnp.bfloat16)
    pre = jnp.dot(key_rows, weight_in, preferred_element_type=jnp.float32) * in_root
    gate = pre[:, :fast]
    upper = pre[:, fast:]
    sigma = jax.nn.sigmoid(gate)
    active = gate * sigma
    hidden = (active * upper).astype(jnp.bfloat16)
    back = (
        lax.dot_general(
            scaled, weight_out, (((1,), (1,)), ((), ())), preferred_element_type=jnp.float32
        )
        * out_root
    )
    d_gate = (back * upper * sigma * (1.0 + gate * (1.0 - sigma))).astype(jnp.bfloat16)
    d_up = (back * active).astype(jnp.bfloat16)
    joined = jnp.concatenate([d_gate, d_up], axis=1)
    inc_in = (
        lax.dot_general(
            key_rows, joined, (((0,), (0,)), ((), ())), preferred_element_type=jnp.float32
        )
        * in_root
    )
    inc_out = (
        lax.dot_general(
            hidden, scaled, (((0,), (0,)), ((), ())), preferred_element_type=jnp.float32
        )
        * out_root
    )
    return (inc_in, inc_out)


def local_increments(keyn, values, step_size, weight_in, weight_out, block_root):
    heads = weight_in.shape[0]
    head_size = weight_in.shape[1]
    list_in = []
    list_out = []
    for head_number in range(heads):
        value_rows = values[:, head_number * head_size : (head_number + 1) * head_size]
        part_in, part_out = head_increments(
            keyn[:, head_number, :],
            value_rows,
            step_size[head_number],
            weight_in[head_number],
            weight_out[head_number],
            block_root,
        )
        list_in.append(part_in)
        list_out.append(part_out)
    return (jnp.stack(list_in), jnp.stack(list_out))


def renorm_in(matrix):
    heads, rows_here, double = matrix.shape
    split = matrix.reshape(heads, rows_here, 2, double // 2)
    return rms_rows(split).reshape(heads, rows_here, double)


def apply_head(query_rows, weight_in, weight_out):
    fast = weight_out.shape[0]
    pre = jnp.dot(query_rows, weight_in, preferred_element_type=jnp.float32) * (
        1.0 / math.sqrt(weight_in.shape[0])
    )
    gate = pre[:, :fast]
    hidden = (gate * jax.nn.sigmoid(gate) * pre[:, fast:]).astype(jnp.bfloat16)
    return jnp.dot(hidden, weight_out, preferred_element_type=jnp.float32) * (1.0 / math.sqrt(fast))


def apply_all(queryn, next_in, next_out):
    heads = next_in.shape[0]
    pieces = []
    for head_number in range(heads):
        pieces.append(
            apply_head(queryn[:, head_number, :], next_in[head_number], next_out[head_number])
        )
    return jnp.concatenate(pieces, axis=1).astype(jnp.bfloat16)


def per_device_generic(queries, keys, values, step_size, fast_in, fast_out):
    row_count = keys.shape[0]
    heads = fast_in.shape[0]
    head_size = keys.shape[1] // heads
    block_root = 1.0 / math.sqrt(row_count * lax.axis_size("tok"))
    keyn = normalized_heads(keys, heads, head_size)
    queryn = normalized_heads(queries, heads, head_size)
    master_in, master_out = (
        lax.all_gather(fast_in, "tok", axis=1, tiled=True),
        lax.all_gather(fast_out, "tok", axis=1, tiled=True),
    )
    inc_in, inc_out = local_increments(
        keyn,
        values,
        step_size,
        master_in.astype(jnp.bfloat16),
        master_out.astype(jnp.bfloat16),
        block_root,
    )
    total_in, total_out = lax.psum((inc_in, inc_out), "tok")
    whole_in = renorm_in(master_in + total_in)
    whole_out = rms_rows(master_out + total_out)
    output = apply_all(queryn, whole_in.astype(jnp.bfloat16), whole_out.astype(jnp.bfloat16))
    place = lax.axis_index("tok")
    fast_in_next = lax.dynamic_slice_in_dim(whole_in, place * fast_in.shape[1], fast_in.shape[1], 1)
    fast_out_next = lax.dynamic_slice_in_dim(
        whole_out, place * fast_out.shape[1], fast_out.shape[1], 1
    )
    return (output, fast_in_next, fast_out_next)


def swap(value, bits):
    count = lax.axis_size("tok")
    return lax.ppermute(value, "tok", [(place, place ^ bits) for place in range(count)])


def swap_parts(value):
    return lax.ppermute(value, "parts", [(0, 1), (1, 0)])


def after(value, *before):
    return lax.optimization_barrier((value, before))[0]


def compiler_params(limit=VMEM_LIMIT):
    return pltpu.CompilerParams(vmem_limit_bytes=limit)


def head_of(ids, order, other):
    return 2 * jnp.bitwise_xor(ids[1], other) + jnp.bitwise_xor(ids[2], order)


def normalize_head(block):
    wide = block.astype(F32)
    return (wide * lax.rsqrt(jnp.mean(wide * wide, axis=-1, keepdims=True) + 1e-06)).astype(BF16)


def pack_kernel(ids, in_hbm, out_hbm, own, theirs, in_ref, out_ref, arrived):
    copies = [
        pltpu.make_async_copy(in_hbm, in_ref, arrived.at[0]),
        pltpu.make_async_copy(out_hbm, out_ref, arrived.at[1]),
    ]
    for copy in copies:
        copy.start()
    for copy in copies:
        copy.wait()
    size = out_ref.shape[-1]
    rows = in_ref.shape[1]
    for other, ref in ((0, own), (1, theirs)):
        for order in range(2):
            head = head_of(ids, order, other)
            for block in range(in_ref.shape[2] // size):
                ref[order, block * rows : (block + 1) * rows, :] = in_ref[
                    head, :, block * size : (block + 1) * size
                ]
            ref[order, -out_ref.shape[1] :, :] = out_ref[head]


def pack(ids, fast_in, fast_out):
    rows = 4 * fast_in.shape[1] + fast_out.shape[1]
    shape = jax.ShapeDtypeStruct((2, rows, fast_out.shape[2]), F32)
    return pl.pallas_call(
        pack_kernel,
        in_specs=[pl.BlockSpec(memory_space=pltpu.SMEM)] + [pl.BlockSpec(memory_space=pltpu.HBM)] * 2,
        out_shape=[shape, shape],
        scratch_shapes=[
            pltpu.VMEM(fast_in.shape, F32),
            pltpu.VMEM(fast_out.shape, F32),
            pltpu.SemaphoreType.DMA((2,)),
        ],
        compiler_params=compiler_params(VMEM_ALL),
        name="pack",
    )(ids, fast_in, fast_out)


def pair_kernel(own, got, master_one, master_two, shard):
    for source, ref in enumerate((own, got)):
        for order, master in enumerate((master_one, master_two)):
            master[source] = ref[order]
        shard[source] = ref[0].astype(BF16)


def pair(own, got):
    wide = jax.ShapeDtypeStruct(own.shape, F32)
    return pl.pallas_call(
        pair_kernel,
        out_shape=[wide, wide, jax.ShapeDtypeStruct(own.shape, BF16)],
        compiler_params=compiler_params(),
        name="pair",
    )(own, got)


def prepare_kernel(heads, ids, x_ref, *rest):
    own, send = rest[-2:]
    core = ids[1]
    half = heads // 2
    size = x_ref.shape[1] // heads

    def work(owner, out):
        for local in range(half):
            columns = pl.ds(pl.multiple_of((owner * half + local) * size, size), size)
            into = slice(local * size, (local + 1) * size)
            if len(rest) == 2:
                out[:, into] = normalize_head(x_ref[:, columns])
            else:
                first = rest[0][:, local : local + 1]
                second = rest[0][:, half + local : half + local + 1]
                rate = jnp.where(owner == 0, first, second)
                out[:, into] = (rate * x_ref[:, columns].astype(F32)).astype(BF16)

    work(core, own)
    work(1 - core, send)


def prepare(ids, tokens, rates, heads, name):
    rows, width = tokens.shape
    step = 256
    wide = pl.BlockSpec((step, width), lambda i, ids: (i, 0))
    narrow = pl.BlockSpec((step, width // 2), lambda i, ids: (i, 0))
    operands, specs = [tokens], [wide]
    if rates is not None:
        operands.append(rates)
        specs.append(pl.BlockSpec((step, heads), lambda i, ids: (i, 0)))
    shape = jax.ShapeDtypeStruct((rows, width // 2), BF16)
    return pl.pallas_call(
        functools.partial(prepare_kernel, heads),
        grid_spec=pltpu.PrefetchScalarGridSpec(
            num_scalar_prefetch=1,
            grid=(rows // step,),
            in_specs=specs,
            out_specs=[narrow] * 2,
        ),
        out_shape=[shape] * 2,
        compiler_params=compiler_params(VMEM_ALL),
        cost_estimate=pl.CostEstimate(
            flops=rows * width * 5, bytes_accessed=rows * width * 4, transcendentals=0
        ),
        name=name,
    )(ids, *operands)


def places(chip, core):
    for side in range(2):
        for slot in range(4):
            other = jnp.bitwise_xor(chip, 2 * slot + side)
            for source in range(2):
                yield side, slot, source, 2 * other + jnp.bitwise_xor(core, source)


def assemble(chip, core, lines, w_in, w_out):
    size = w_out.shape[1]
    blocks = w_in.shape[1] // size
    rows_in = w_in.shape[0] // 16
    rows_out = w_out.shape[0] // 16
    for side, slot, source, place in places(chip, core):
        ref = lines[2 * side + slot // 2].at[slot % 2]
        into = pl.ds(pl.multiple_of(place * rows_in, rows_in), rows_in)
        for block in range(blocks):
            w_in[into, block * size : (block + 1) * size] = ref[
                source, block * rows_in : (block + 1) * rows_in, :
            ]
        into = pl.ds(pl.multiple_of(place * rows_out, rows_out), rows_out)
        w_out[into, :] = ref[source, blocks * rows_in :, :]


def increments_kernel(
    ids, near_low, near_high, far_low, far_high, k_own, v_own, k_got, v_got,
    kept, low, high, w_in, w_out, acc_in, acc_out, turned,
):
    step = pl.program_id(0)
    steps = pl.num_programs(0)
    chip, core = ids[0], ids[1]
    size = w_out.shape[1]
    fast = w_out.shape[0]
    in_root = 1.0 / math.sqrt(size)
    out_root = 1.0 / math.sqrt(fast)

    @pl.when(step == 0)
    def _():
        assemble(chip, core, (near_low, near_high, far_low, far_high), w_in, w_out)

    def work(k_ref, v_ref, start_over):
        keyn = k_ref[...]
        scaled = v_ref[...]
        keyn_t = keyn.T
        scaled_t = scaled.T

        def add(ref, columns, value):
            if start_over:
                ref[:, columns] = value
            else:
                ref[:, columns] += value

        chunk = 256
        for start in range(0, fast, chunk):
            gates = slice(start, start + chunk)
            ups = slice(fast + start, fast + start + chunk)
            gate = jnp.dot(keyn, w_in[:, gates], preferred_element_type=F32) * in_root
            upper = jnp.dot(keyn, w_in[:, ups], preferred_element_type=F32) * in_root
            back = (
                lax.dot_general(
                    scaled, w_out[gates, :], (((1,), (1,)), ((), ())), preferred_element_type=F32
                )
                * out_root
            )
            sigma = 0.5 * jnp.tanh(0.5 * gate) + 0.5
            active = gate * sigma
            hidden = (active * upper).astype(BF16)
            d_gate = (back * upper * (sigma + active * (1.0 - sigma))).astype(BF16)
            d_up = (back * active).astype(BF16)
            add(acc_in, gates, jnp.dot(keyn_t, d_gate, preferred_element_type=F32))
            add(acc_in, ups, jnp.dot(keyn_t, d_up, preferred_element_type=F32))
            add(acc_out, gates, jnp.dot(scaled_t, hidden, preferred_element_type=F32))

    @pl.when(step == 0)
    def _():
        work(k_own, v_own, True)

    if k_own.shape[0] * 2 < 2048:

        @pl.when((step > 0) & (step < steps // 2))
        def _():
            work(k_own, v_own, False)

    @pl.when(step >= steps // 2)
    def _():
        work(k_got, v_got, False)

    @pl.when(step == steps - 1)
    def _():
        turned[...] = acc_out[...].T
        blocks = acc_in.shape[1] // size
        rows_in = acc_in.shape[0] // 16
        rows_out = turned.shape[0] // 16
        for side, slot, source, place in places(chip, core):
            ref = kept.at[slot] if side == 0 else (low, high)[slot // 2].at[slot % 2]
            rows = pl.ds(pl.multiple_of(place * rows_in, rows_in), rows_in)
            for block in range(blocks):
                ref[source, block * rows_in : (block + 1) * rows_in, :] = (
                    acc_in[rows, block * size : (block + 1) * size] * in_root
                ).astype(ref.dtype)
            rows = pl.ds(pl.multiple_of(place * rows_out, rows_out), rows_out)
            ref[source, blocks * rows_in :, :] = (turned[rows, :] * out_root).astype(ref.dtype)


def increments(ids, order, lines, k_own, v_own, k_got, v_got, fast):
    rows = k_own.shape[0]
    pair_shape = lines[0].shape
    size = pair_shape[-1]
    step = rows
    half = rows // step
    whole = pl.BlockSpec(pair_shape, lambda i, ids: (0, 0, 0, 0))
    line_shape = (4,) + pair_shape[1:]
    line = pl.BlockSpec(line_shape, lambda i, ids: (0, 0, 0, 0))
    own = pl.BlockSpec((step, size), lambda i, ids: (jnp.minimum(i, half - 1), ids[2] ^ order))
    got = pl.BlockSpec((step, size), lambda i, ids: (jnp.maximum(i - half, 0), ids[2] ^ order))
    return pl.pallas_call(
        increments_kernel,
        grid_spec=pltpu.PrefetchScalarGridSpec(
            num_scalar_prefetch=1,
            grid=(2 * half,),
            in_specs=[whole] * 4 + [own, own, got, got],
            out_specs=[line, whole, whole],
            scratch_shapes=[
                pltpu.VMEM((size, 2 * fast), BF16),
                pltpu.VMEM((fast, size), BF16),
                pltpu.VMEM((size, 2 * fast), F32),
                pltpu.VMEM((size, fast), F32),
                pltpu.VMEM((fast, size), F32),
            ],
        ),
        out_shape=[
            jax.ShapeDtypeStruct(line_shape, F32),
            jax.ShapeDtypeStruct(pair_shape, BF16),
            jax.ShapeDtypeStruct(pair_shape, BF16),
        ],
        compiler_params=compiler_params(),
        cost_estimate=pl.CostEstimate(
            flops=2 * rows * size * fast * 12, bytes_accessed=rows * size * 8, transcendentals=0
        ),
        name="increments",
    )(ids, *lines, k_own, v_own, k_got, v_got)


def add_kernel(kept, came, first, second):
    first[...] = (kept[0] + came[0].astype(F32)).astype(first.dtype)
    second[...] = (kept[1] + came[1].astype(F32)).astype(second.dtype)


def add_pair(kept, came, which, first_type):
    shape = came.shape
    flat = (0,) * (len(shape) - 1)
    return pl.pallas_call(
        add_kernel,
        grid=(1,),
        in_specs=[
            pl.BlockSpec(shape, lambda i: (which,) + flat),
            pl.BlockSpec(shape, lambda i: (0,) + flat),
        ],
        out_specs=[pl.BlockSpec(shape[1:], lambda i: flat)] * 2,
        out_shape=[
            jax.ShapeDtypeStruct(shape[1:], first_type),
            jax.ShapeDtypeStruct(shape[1:], BF16),
        ],
        compiler_params=compiler_params(),
        name="add_pair",
    )(kept, came)


def renorm_kernel(rows_in, master, kept, one, two, three, wide, short):
    size = master.shape[-1]
    for source in range(2):
        fresh = (
            master[source]
            + kept[source]
            + one[source].astype(F32)
            + two[source].astype(F32)
            + three[source].astype(F32)
        )
        for part in range(2):
            first = 2 * part * rows_in
            left = fresh[first : first + rows_in, :]
            right = fresh[first + rows_in : first + 2 * rows_in, :]
            total = jnp.sum(left * left + right * right, axis=-1, keepdims=True)
            factor = lax.rsqrt(total * (1.0 / (2 * size)) + 1e-06)
            for at, value in ((first, left), (first + rows_in, right)):
                done = value * factor
                wide[source, at : at + rows_in, :] = done
                short[source, at : at + rows_in, :] = done.astype(BF16)
        tail = fresh[4 * rows_in :, :]
        done = tail * lax.rsqrt(jnp.mean(tail * tail, axis=-1, keepdims=True) + 1e-06)
        wide[source, 4 * rows_in :, :] = done
        short[source, 4 * rows_in :, :] = done.astype(BF16)


def renorm(master, kept, one, two, three, rows_in):
    shape = master.shape
    return pl.pallas_call(
        functools.partial(renorm_kernel, rows_in),
        out_shape=[jax.ShapeDtypeStruct(shape, F32), jax.ShapeDtypeStruct(shape, BF16)],
        compiler_params=compiler_params(),
        name="renorm",
    )(master, kept, one, two, three)


def apply_kernel(other, ids, near_low, near_high, far_low, far_high, q_ref, *rest):
    o_ref, w_in, w_out = rest[-3:]
    chip, core = ids[0], ids[1]
    fast = w_out.shape[0]

    @pl.when(pl.program_id(0) == 0)
    def _():
        lines = (near_low, near_high, far_low, far_high)
        assemble(chip, jnp.bitwise_xor(core, other), lines, w_in, w_out)

    query = normalize_head(q_ref[...])
    in_root = 1.0 / math.sqrt(w_out.shape[1])
    gate = jnp.dot(query, w_in[:, :fast], preferred_element_type=F32) * in_root
    upper = jnp.dot(query, w_in[:, fast:], preferred_element_type=F32) * in_root
    hidden = (gate * (0.5 * jnp.tanh(0.5 * gate) + 0.5) * upper).astype(BF16)
    result = jnp.dot(hidden, w_out[...], preferred_element_type=F32) * (1.0 / math.sqrt(fast))
    o_ref[...] = result.astype(BF16)


def apply_fast(ids, order, other, lines, queries, output, fast):
    rows, width = queries.shape
    pair_shape = lines[0].shape
    size = pair_shape[-1]
    step = 512
    whole = pl.BlockSpec(pair_shape, lambda i, ids: (0, 0, 0, 0))
    column = pl.BlockSpec((step, size), lambda i, ids: (i, 2 * (ids[1] ^ other) + (ids[2] ^ order)))
    operands = [ids, *lines, queries]
    specs = [whole] * 4 + [column]
    aliases = {}
    if output is not None:
        operands.append(output)
        specs.append(pl.BlockSpec(memory_space=pl.ANY))
        aliases = {6: 0}
    return pl.pallas_call(
        functools.partial(apply_kernel, other),
        grid_spec=pltpu.PrefetchScalarGridSpec(
            num_scalar_prefetch=1,
            grid=(rows // step,),
            in_specs=specs,
            out_specs=column,
            scratch_shapes=[pltpu.VMEM((size, 2 * fast), BF16), pltpu.VMEM((fast, size), BF16)],
        ),
        out_shape=jax.ShapeDtypeStruct((rows, width), BF16),
        input_output_aliases=aliases,
        compiler_params=compiler_params(),
        cost_estimate=pl.CostEstimate(
            flops=2 * rows * size * fast * 3, bytes_accessed=rows * size * 4, transcendentals=0
        ),
        name="apply",
    )(*operands)


def finish_kernel(rows_in, ids, one, two, came, in_next, out_next):
    size = out_next.shape[-1]
    for order, mine in enumerate((one, two)):
        for other, ref in ((0, mine.at[0]), (1, came.at[order])):
            head = head_of(ids, order, other)
            for block in range(4):
                in_next[head, :, block * size : (block + 1) * size] = ref[
                    block * rows_in : (block + 1) * rows_in, :
                ]
            out_next[head] = ref[4 * rows_in :, :]


def finish(ids, one, two, came, fast_in, fast_out):
    return pl.pallas_call(
        functools.partial(finish_kernel, fast_in.shape[1]),
        in_specs=[pl.BlockSpec(memory_space=pltpu.SMEM)] + [pl.BlockSpec(memory_space=pltpu.VMEM)] * 3,
        out_shape=[
            jax.ShapeDtypeStruct(fast_in.shape, F32),
            jax.ShapeDtypeStruct(fast_out.shape, F32),
        ],
        compiler_params=compiler_params(),
        name="finish",
    )(ids, one, two, came)


def gather_chips(shard):
    z1, z3, z2 = swap(shard, 4), swap(shard, 12), swap(shard, 8)
    near_low, near_high = jnp.stack([shard, z1]), jnp.stack([z2, z3])
    far_low = swap(near_low, 2)
    near_high = after(near_high, far_low)
    return near_low, near_high, far_low, swap(near_high, 2)


def per_device_cube(queries, keys, values, step_size, fast_in, fast_out):
    rows = keys.shape[0]
    heads = fast_in.shape[0]
    fast = fast_in.shape[2] // 2
    rows_in = fast_in.shape[1]
    place = lax.axis_index("tok")
    ids = jnp.stack([place // 2, place % 2, lax.axis_index("parts")]).astype(jnp.int32)
    block_root = 1.0 / math.sqrt(rows * lax.axis_size("tok"))

    own, theirs = pack(ids, fast_in, fast_out)
    got = swap(theirs, 1)
    later = after(ids, own)
    k_own, k_send = prepare(later, keys, None, heads, "keys")
    v_own, v_send = prepare(later, values, (step_size * block_root).T, heads, "values")
    got = after(got, k_send, v_send)
    master_one, master_two, shard = pair(own, got)
    masters = (master_one, master_two)
    first = gather_chips(shard)
    second = tuple(swap_parts(piece) for piece in first)
    k_got, v_got = swap(k_send, 1), swap(v_send, 1)

    kept, low, high = [], [], []
    for order, lines in enumerate((first, second)):
        a, b, c = increments(ids, order, lines, k_own, v_own, k_got, v_got, fast)
        kept.append(a)
        low.append(swap(b, 2))
        high.append(swap(c, 2))
    wide, short = [], []
    for order in range(2):
        sum2, sum3 = add_pair(kept[order], high[order], 1, BF16)
        sum0, sum1 = add_pair(kept[order], low[order], 0, F32)
        three, two, one = swap(sum3, 12), swap(sum2, 8), swap(sum1, 4)
        a, b = renorm(masters[order], sum0, one, two, three, rows_in)
        wide.append(a)
        short.append(b)

    lines = [gather_chips(shard) for shard in short]
    near_low, near_high, far_low, far_high = lines[0]
    far_low, far_high = after((far_low, far_high), *lines[1][:2])
    mine = (near_low, near_high, far_low, far_high)
    others = tuple(swap(piece, 1) for piece in mine)
    output = apply_fast(ids, 0, 0, mine, queries, None, fast)
    output = apply_fast(ids, 0, 1, others, queries, output, fast)
    near_low, near_high, far_low, far_high = lines[1]
    far_high = after(far_high, output)
    mine = (near_low, near_high, far_low, far_high)
    others = tuple(swap(piece, 1) for piece in mine)
    output = apply_fast(ids, 1, 0, mine, queries, output, fast)
    output = apply_fast(ids, 1, 1, others, queries, output, fast)

    came = swap(jnp.stack([wide[0][1], wide[1][1]]), 1)
    return (output, *finish(ids, wide[0], wide[1], came, fast_in, fast_out))


def per_device(queries, keys, values, step_size, fast_in, fast_out):
    fits = (
        lax.axis_size("tok") == 16
        and lax.axis_size("parts") == 2
        and fast_in.shape[0] == 4
        and fast_in.shape[1] % 16 == 0
    )
    chosen = per_device_cube if fits else per_device_generic
    return chosen(queries, keys, values, step_size, fast_in, fast_out)


def solution(mesh):
    placed = (
        P(("parts", "tok"), None),
        P(("parts", "tok"), None),
        P(("parts", "tok"), None),
        P(None, ("parts", "tok")),
        P(None, "tok", None),
        P(None, "tok", None),
    )
    return jax.shard_map(
        per_device,
        mesh=mesh,
        in_specs=placed,
        out_specs=(P(("parts", "tok"), None), P("parts", "tok", None), P("parts", "tok", None)),
        check_vma=False,
    )
```

```python
import functools
import math

import jax
import jax.numpy as jnp
from jax import lax
from jax.experimental import pallas as pl
from jax.experimental.pallas import tpu as pltpu
from jax.sharding import PartitionSpec as P

BF16 = jnp.bfloat16
F32 = jnp.float32
VMEM_LIMIT = 32 * 1024 * 1024


def rms_rows(matrix):
    return matrix * lax.rsqrt(jnp.mean(matrix * matrix, axis=-1, keepdims=True) + 1e-06)


def normalized_heads(tokens, heads, head_size):
    row_count = tokens.shape[0]
    wide = tokens.astype(jnp.float32).reshape(row_count, heads, head_size)
    return rms_rows(wide).astype(jnp.bfloat16)


def head_increments(key_rows, value_rows, rates, weight_in, weight_out, block_root):
    fast = weight_out.shape[0]
    in_root = 1.0 / math.sqrt(weight_in.shape[0])
    out_root = 1.0 / math.sqrt(fast)
    scaled = (rates[:, None] * block_root * value_rows.astype(jnp.float32)).astype(jnp.bfloat16)
    pre = jnp.dot(key_rows, weight_in, preferred_element_type=jnp.float32) * in_root
    gate = pre[:, :fast]
    upper = pre[:, fast:]
    sigma = jax.nn.sigmoid(gate)
    active = gate * sigma
    hidden = (active * upper).astype(jnp.bfloat16)
    back = (
        lax.dot_general(
            scaled, weight_out, (((1,), (1,)), ((), ())), preferred_element_type=jnp.float32
        )
        * out_root
    )
    d_gate = (back * upper * sigma * (1.0 + gate * (1.0 - sigma))).astype(jnp.bfloat16)
    d_up = (back * active).astype(jnp.bfloat16)
    joined = jnp.concatenate([d_gate, d_up], axis=1)
    inc_in = (
        lax.dot_general(
            key_rows, joined, (((0,), (0,)), ((), ())), preferred_element_type=jnp.float32
        )
        * in_root
    )
    inc_out = (
        lax.dot_general(
            hidden, scaled, (((0,), (0,)), ((), ())), preferred_element_type=jnp.float32
        )
        * out_root
    )
    return (inc_in, inc_out)


def local_increments(keyn, values, step_size, weight_in, weight_out, block_root):
    heads = weight_in.shape[0]
    head_size = weight_in.shape[1]
    list_in = []
    list_out = []
    for head_number in range(heads):
        value_rows = values[:, head_number * head_size : (head_number + 1) * head_size]
        part_in, part_out = head_increments(
            keyn[:, head_number, :],
            value_rows,
            step_size[head_number],
            weight_in[head_number],
            weight_out[head_number],
            block_root,
        )
        list_in.append(part_in)
        list_out.append(part_out)
    return (jnp.stack(list_in), jnp.stack(list_out))


def renorm_in(matrix):
    heads, rows_here, double = matrix.shape
    split = matrix.reshape(heads, rows_here, 2, double // 2)
    return rms_rows(split).reshape(heads, rows_here, double)


def apply_head(query_rows, weight_in, weight_out):
    fast = weight_out.shape[0]
    pre = jnp.dot(query_rows, weight_in, preferred_element_type=jnp.float32) * (
        1.0 / math.sqrt(weight_in.shape[0])
    )
    gate = pre[:, :fast]
    hidden = (gate * jax.nn.sigmoid(gate) * pre[:, fast:]).astype(jnp.bfloat16)
    return jnp.dot(hidden, weight_out, preferred_element_type=jnp.float32) * (1.0 / math.sqrt(fast))


def apply_all(queryn, next_in, next_out):
    heads = next_in.shape[0]
    pieces = []
    for head_number in range(heads):
        pieces.append(
            apply_head(queryn[:, head_number, :], next_in[head_number], next_out[head_number])
        )
    return jnp.concatenate(pieces, axis=1).astype(jnp.bfloat16)


def per_device_generic(queries, keys, values, step_size, fast_in, fast_out):
    row_count = keys.shape[0]
    heads = fast_in.shape[0]
    head_size = keys.shape[1] // heads
    block_root = 1.0 / math.sqrt(row_count * lax.axis_size("tok"))
    keyn = normalized_heads(keys, heads, head_size)
    queryn = normalized_heads(queries, heads, head_size)
    master_in, master_out = (
        lax.all_gather(fast_in, "tok", axis=1, tiled=True),
        lax.all_gather(fast_out, "tok", axis=1, tiled=True),
    )
    inc_in, inc_out = local_increments(
        keyn,
        values,
        step_size,
        master_in.astype(jnp.bfloat16),
        master_out.astype(jnp.bfloat16),
        block_root,
    )
    total_in, total_out = lax.psum((inc_in, inc_out), "tok")
    whole_in = renorm_in(master_in + total_in)
    whole_out = rms_rows(master_out + total_out)
    output = apply_all(queryn, whole_in.astype(jnp.bfloat16), whole_out.astype(jnp.bfloat16))
    place = lax.axis_index("tok")
    fast_in_next = lax.dynamic_slice_in_dim(whole_in, place * fast_in.shape[1], fast_in.shape[1], 1)
    fast_out_next = lax.dynamic_slice_in_dim(
        whole_out, place * fast_out.shape[1], fast_out.shape[1], 1
    )
    return (output, fast_in_next, fast_out_next)


def swap(value, bits):
    count = lax.axis_size("tok")
    return lax.ppermute(value, "tok", [(place, place ^ bits) for place in range(count)])


def swap_parts(value):
    return lax.ppermute(value, "parts", [(0, 1), (1, 0)])


def after(value, *before):
    return lax.optimization_barrier((value, before))[0]


def compiler_params():
    return pltpu.CompilerParams(vmem_limit_bytes=VMEM_LIMIT)


def head_of(ids, order, other):
    return 2 * jnp.bitwise_xor(ids[1], other) + jnp.bitwise_xor(ids[2], order)


def normalize_head(block):
    wide = block.astype(F32)
    return (wide * lax.rsqrt(jnp.mean(wide * wide, axis=-1, keepdims=True) + 1e-06)).astype(BF16)


def pack_kernel(ids, in_hbm, out_hbm, own, theirs, in_ref, out_ref, arrived):
    copies = [
        pltpu.make_async_copy(in_hbm, in_ref, arrived.at[0]),
        pltpu.make_async_copy(out_hbm, out_ref, arrived.at[1]),
    ]
    for copy in copies:
        copy.start()
    for copy in copies:
        copy.wait()
    size = out_ref.shape[-1]
    rows = in_ref.shape[1]
    for other, ref in ((0, own), (1, theirs)):
        for order in range(2):
            head = head_of(ids, order, other)
            for block in range(in_ref.shape[2] // size):
                ref[order, block * rows : (block + 1) * rows, :] = in_ref[
                    head, :, block * size : (block + 1) * size
                ]
            ref[order, -out_ref.shape[1] :, :] = out_ref[head]


def pack(ids, fast_in, fast_out):
    rows = 4 * fast_in.shape[1] + fast_out.shape[1]
    shape = jax.ShapeDtypeStruct((2, rows, fast_out.shape[2]), F32)
    return pl.pallas_call(
        pack_kernel,
        in_specs=[pl.BlockSpec(memory_space=pltpu.SMEM)] + [pl.BlockSpec(memory_space=pltpu.HBM)] * 2,
        out_shape=[shape, shape],
        scratch_shapes=[
            pltpu.VMEM(fast_in.shape, F32),
            pltpu.VMEM(fast_out.shape, F32),
            pltpu.SemaphoreType.DMA((2,)),
        ],
        compiler_params=compiler_params(),
        name="pack",
    )(ids, fast_in, fast_out)


def pair_kernel(own, got, master_one, master_two, shard):
    for source, ref in enumerate((own, got)):
        for order, master in enumerate((master_one, master_two)):
            master[source] = ref[order]
        shard[source] = ref[0].astype(BF16)


def pair(own, got):
    wide = jax.ShapeDtypeStruct(own.shape, F32)
    return pl.pallas_call(
        pair_kernel,
        out_shape=[wide, wide, jax.ShapeDtypeStruct(own.shape, BF16)],
        compiler_params=compiler_params(),
        name="pair",
    )(own, got)


def prepare_kernel(heads, block_root, ids, x_ref, *rest):
    own, send = rest[-2:]
    core = ids[1]
    half = heads // 2
    size = x_ref.shape[1] // heads

    if len(rest) == 3:
        rates = rest[0][...]
        columns_of = jnp.concatenate([rates, rates], axis=0).T

    def work(owner, out):
        for local in range(half):
            columns = pl.ds(pl.multiple_of((owner * half + local) * size, size), size)
            into = slice(local * size, (local + 1) * size)
            if len(rest) == 2:
                out[:, into] = normalize_head(x_ref[:, columns])
            else:
                first = columns_of[:, local : local + 1]
                second = columns_of[:, half + local : half + local + 1]
                rate = jnp.where(owner == 0, first, second) * block_root
                out[:, into] = (rate * x_ref[:, columns].astype(F32)).astype(BF16)

    work(core, own)
    work(1 - core, send)


def prepare(ids, tokens, rates, heads, block_root, name):
    rows, width = tokens.shape
    step = 256
    wide = pl.BlockSpec((step, width), lambda i, ids: (i, 0))
    narrow = pl.BlockSpec((step, width // 2), lambda i, ids: (i, 0))
    operands, specs = [tokens], [wide]
    if rates is not None:
        operands.append(rates)
        specs.append(pl.BlockSpec((heads, step), lambda i, ids: (0, i)))
    shape = jax.ShapeDtypeStruct((rows, width // 2), BF16)
    return pl.pallas_call(
        functools.partial(prepare_kernel, heads, block_root),
        grid_spec=pltpu.PrefetchScalarGridSpec(
            num_scalar_prefetch=1,
            grid=(rows // step,),
            in_specs=specs,
            out_specs=[narrow] * 2,
        ),
        out_shape=[shape] * 2,
        compiler_params=compiler_params(),
        cost_estimate=pl.CostEstimate(
            flops=rows * width * 5, bytes_accessed=rows * width * 4, transcendentals=0
        ),
        name=name,
    )(ids, *operands)


def places(chip, core):
    for side in range(2):
        for slot in range(4):
            other = jnp.bitwise_xor(chip, 2 * slot + side)
            for source in range(2):
                yield side, slot, source, 2 * other + jnp.bitwise_xor(core, source)


def assemble(chip, core, lines, w_in, w_out):
    size = w_out.shape[1]
    blocks = w_in.shape[1] // size
    rows_in = w_in.shape[0] // 16
    rows_out = w_out.shape[0] // 16
    for side, slot, source, place in places(chip, core):
        ref = lines[2 * side + slot // 2].at[slot % 2]
        into = pl.ds(pl.multiple_of(place * rows_in, rows_in), rows_in)
        for block in range(blocks):
            w_in[into, block * size : (block + 1) * size] = ref[
                source, block * rows_in : (block + 1) * rows_in, :
            ]
        into = pl.ds(pl.multiple_of(place * rows_out, rows_out), rows_out)
        w_out[into, :] = ref[source, blocks * rows_in :, :]


def increments_kernel(
    ids, near_low, near_high, far_low, far_high, k_own, v_own, k_got, v_got,
    kept, low, high, w_in, w_out, acc_in, acc_out, turned,
):
    step = pl.program_id(0)
    steps = pl.num_programs(0)
    chip, core = ids[0], ids[1]
    size = w_out.shape[1]
    fast = w_out.shape[0]
    in_root = 1.0 / math.sqrt(size)
    out_root = 1.0 / math.sqrt(fast)

    @pl.when(step == 0)
    def _():
        assemble(chip, core, (near_low, near_high, far_low, far_high), w_in, w_out)

    def work(k_ref, v_ref, start_over):
        keyn = k_ref[...]
        scaled = v_ref[...]
        keyn_t = keyn.T
        scaled_t = scaled.T

        def add(ref, columns, value):
            if start_over:
                ref[:, columns] = value
            else:
                ref[:, columns] += value

        chunk = 256
        for start in range(0, fast, chunk):
            gates = slice(start, start + chunk)
            ups = slice(fast + start, fast + start + chunk)
            gate = jnp.dot(keyn, w_in[:, gates], preferred_element_type=F32) * in_root
            upper = jnp.dot(keyn, w_in[:, ups], preferred_element_type=F32) * in_root
            back = (
                lax.dot_general(
                    scaled, w_out[gates, :], (((1,), (1,)), ((), ())), preferred_element_type=F32
                )
                * out_root
            )
            sigma = 0.5 * jnp.tanh(0.5 * gate) + 0.5
            active = gate * sigma
            hidden = (active * upper).astype(BF16)
            d_gate = (back * upper * (sigma + active * (1.0 - sigma))).astype(BF16)
            d_up = (back * active).astype(BF16)
            add(acc_in, gates, jnp.dot(keyn_t, d_gate, preferred_element_type=F32))
            add(acc_in, ups, jnp.dot(keyn_t, d_up, preferred_element_type=F32))
            add(acc_out, gates, jnp.dot(scaled_t, hidden, preferred_element_type=F32))

    @pl.when(step == 0)
    def _():
        work(k_own, v_own, True)

    if k_own.shape[0] * 2 < 2048:

        @pl.when((step > 0) & (step < steps // 2))
        def _():
            work(k_own, v_own, False)

    @pl.when(step >= steps // 2)
    def _():
        work(k_got, v_got, False)

    @pl.when(step == steps - 1)
    def _():
        turned[...] = acc_out[...].T
        blocks = acc_in.shape[1] // size
        rows_in = acc_in.shape[0] // 16
        rows_out = turned.shape[0] // 16
        for side, slot, source, place in places(chip, core):
            ref = kept.at[slot] if side == 0 else (low, high)[slot // 2].at[slot % 2]
            rows = pl.ds(pl.multiple_of(place * rows_in, rows_in), rows_in)
            for block in range(blocks):
                ref[source, block * rows_in : (block + 1) * rows_in, :] = (
                    acc_in[rows, block * size : (block + 1) * size] * in_root
                ).astype(ref.dtype)
            rows = pl.ds(pl.multiple_of(place * rows_out, rows_out), rows_out)
            ref[source, blocks * rows_in :, :] = (turned[rows, :] * out_root).astype(ref.dtype)


def increments(ids, order, lines, k_own, v_own, k_got, v_got, fast):
    rows = k_own.shape[0]
    pair_shape = lines[0].shape
    size = pair_shape[-1]
    step = rows
    half = rows // step
    whole = pl.BlockSpec(pair_shape, lambda i, ids: (0, 0, 0, 0))
    line_shape = (4,) + pair_shape[1:]
    line = pl.BlockSpec(line_shape, lambda i, ids: (0, 0, 0, 0))
    own = pl.BlockSpec((step, size), lambda i, ids: (jnp.minimum(i, half - 1), ids[2] ^ order))
    got = pl.BlockSpec((step, size), lambda i, ids: (jnp.maximum(i - half, 0), ids[2] ^ order))
    return pl.pallas_call(
        increments_kernel,
        grid_spec=pltpu.PrefetchScalarGridSpec(
            num_scalar_prefetch=1,
            grid=(2 * half,),
            in_specs=[whole] * 4 + [own, own, got, got],
            out_specs=[line, whole, whole],
            scratch_shapes=[
                pltpu.VMEM((size, 2 * fast), BF16),
                pltpu.VMEM((fast, size), BF16),
                pltpu.VMEM((size, 2 * fast), F32),
                pltpu.VMEM((size, fast), F32),
                pltpu.VMEM((fast, size), F32),
            ],
        ),
        out_shape=[
            jax.ShapeDtypeStruct(line_shape, F32),
            jax.ShapeDtypeStruct(pair_shape, BF16),
            jax.ShapeDtypeStruct(pair_shape, BF16),
        ],
        compiler_params=compiler_params(),
        cost_estimate=pl.CostEstimate(
            flops=2 * rows * size * fast * 12, bytes_accessed=rows * size * 8, transcendentals=0
        ),
        name="increments",
    )(ids, *lines, k_own, v_own, k_got, v_got)


def add_kernel(kept, came, first, second):
    first[...] = (kept[0] + came[0].astype(F32)).astype(first.dtype)
    second[...] = (kept[1] + came[1].astype(F32)).astype(second.dtype)


def add_pair(kept, came, which, first_type):
    shape = came.shape
    flat = (0,) * (len(shape) - 1)
    return pl.pallas_call(
        add_kernel,
        grid=(1,),
        in_specs=[
            pl.BlockSpec(shape, lambda i: (which,) + flat),
            pl.BlockSpec(shape, lambda i: (0,) + flat),
        ],
        out_specs=[pl.BlockSpec(shape[1:], lambda i: flat)] * 2,
        out_shape=[
            jax.ShapeDtypeStruct(shape[1:], first_type),
            jax.ShapeDtypeStruct(shape[1:], BF16),
        ],
        compiler_params=compiler_params(),
        name="add_pair",
    )(kept, came)


def renorm_kernel(rows_in, master, kept, one, two, three, wide, short):
    size = master.shape[-1]
    for source in range(2):
        fresh = (
            master[source]
            + kept[source]
            + one[source].astype(F32)
            + two[source].astype(F32)
            + three[source].astype(F32)
        )
        for part in range(2):
            first = 2 * part * rows_in
            left = fresh[first : first + rows_in, :]
            right = fresh[first + rows_in : first + 2 * rows_in, :]
            total = jnp.sum(left * left + right * right, axis=-1, keepdims=True)
            factor = lax.rsqrt(total * (1.0 / (2 * size)) + 1e-06)
            for at, value in ((first, left), (first + rows_in, right)):
                done = value * factor
                wide[source, at : at + rows_in, :] = done
                short[source, at : at + rows_in, :] = done.astype(BF16)
        tail = fresh[4 * rows_in :, :]
        done = tail * lax.rsqrt(jnp.mean(tail * tail, axis=-1, keepdims=True) + 1e-06)
        wide[source, 4 * rows_in :, :] = done
        short[source, 4 * rows_in :, :] = done.astype(BF16)


def renorm(master, kept, one, two, three, rows_in):
    shape = master.shape
    return pl.pallas_call(
        functools.partial(renorm_kernel, rows_in),
        out_shape=[jax.ShapeDtypeStruct(shape, F32), jax.ShapeDtypeStruct(shape, BF16)],
        compiler_params=compiler_params(),
        name="renorm",
    )(master, kept, one, two, three)


def apply_kernel(other, ids, near_low, near_high, far_low, far_high, q_ref, *rest):
    o_ref, w_in, w_out = rest[-3:]
    chip, core = ids[0], ids[1]
    fast = w_out.shape[0]

    @pl.when(pl.program_id(0) == 0)
    def _():
        lines = (near_low, near_high, far_low, far_high)
        assemble(chip, jnp.bitwise_xor(core, other), lines, w_in, w_out)

    query = normalize_head(q_ref[...])
    in_root = 1.0 / math.sqrt(w_out.shape[1])
    gate = jnp.dot(query, w_in[:, :fast], preferred_element_type=F32) * in_root
    upper = jnp.dot(query, w_in[:, fast:], preferred_element_type=F32) * in_root
    hidden = (gate * (0.5 * jnp.tanh(0.5 * gate) + 0.5) * upper).astype(BF16)
    result = jnp.dot(hidden, w_out[...], preferred_element_type=F32) * (1.0 / math.sqrt(fast))
    o_ref[...] = result.astype(BF16)


def apply_fast(ids, order, other, lines, queries, output, fast):
    rows, width = queries.shape
    pair_shape = lines[0].shape
    size = pair_shape[-1]
    step = 512
    whole = pl.BlockSpec(pair_shape, lambda i, ids: (0, 0, 0, 0))
    column = pl.BlockSpec((step, size), lambda i, ids: (i, 2 * (ids[1] ^ other) + (ids[2] ^ order)))
    operands = [ids, *lines, queries]
    specs = [whole] * 4 + [column]
    aliases = {}
    if output is not None:
        operands.append(output)
        specs.append(pl.BlockSpec(memory_space=pl.ANY))
        aliases = {6: 0}
    return pl.pallas_call(
        functools.partial(apply_kernel, other),
        grid_spec=pltpu.PrefetchScalarGridSpec(
            num_scalar_prefetch=1,
            grid=(rows // step,),
            in_specs=specs,
            out_specs=column,
            scratch_shapes=[pltpu.VMEM((size, 2 * fast), BF16), pltpu.VMEM((fast, size), BF16)],
        ),
        out_shape=jax.ShapeDtypeStruct((rows, width), BF16),
        input_output_aliases=aliases,
        compiler_params=compiler_params(),
        cost_estimate=pl.CostEstimate(
            flops=2 * rows * size * fast * 3, bytes_accessed=rows * size * 4, transcendentals=0
        ),
        name="apply",
    )(*operands)


def finish_kernel(rows_in, ids, one, two, came, in_next, out_next):
    size = out_next.shape[-1]
    for order, mine in enumerate((one, two)):
        for other, ref in ((0, mine.at[0]), (1, came.at[order])):
            head = head_of(ids, order, other)
            for block in range(4):
                in_next[head, :, block * size : (block + 1) * size] = ref[
                    block * rows_in : (block + 1) * rows_in, :
                ]
            out_next[head] = ref[4 * rows_in :, :]


def finish(ids, one, two, came, fast_in, fast_out):
    return pl.pallas_call(
        functools.partial(finish_kernel, fast_in.shape[1]),
        in_specs=[pl.BlockSpec(memory_space=pltpu.SMEM)] + [pl.BlockSpec(memory_space=pltpu.VMEM)] * 3,
        out_shape=[
            jax.ShapeDtypeStruct(fast_in.shape, F32),
            jax.ShapeDtypeStruct(fast_out.shape, F32),
        ],
        compiler_params=compiler_params(),
        name="finish",
    )(ids, one, two, came)


def gather_chips(shard):
    z1, z3, z2 = swap(shard, 4), swap(shard, 12), swap(shard, 8)
    near_low, near_high = jnp.stack([shard, z1]), jnp.stack([z2, z3])
    far_low = swap(near_low, 2)
    near_high = after(near_high, far_low)
    return near_low, near_high, far_low, swap(near_high, 2)


def per_device_cube(queries, keys, values, step_size, fast_in, fast_out):
    rows = keys.shape[0]
    heads = fast_in.shape[0]
    fast = fast_in.shape[2] // 2
    rows_in = fast_in.shape[1]
    place = lax.axis_index("tok")
    ids = jnp.stack([place // 2, place % 2, lax.axis_index("parts")]).astype(jnp.int32)
    block_root = 1.0 / math.sqrt(rows * lax.axis_size("tok"))

    own, theirs = pack(ids, fast_in, fast_out)
    got = swap(theirs, 1)
    later = after(ids, own)
    k_own, k_send = prepare(later, keys, None, heads, None, "keys")
    v_own, v_send = prepare(later, values, step_size, heads, block_root, "values")
    got = after(got, k_send, v_send)
    master_one, master_two, shard = pair(own, got)
    masters = (master_one, master_two)
    first = gather_chips(shard)
    second = tuple(swap_parts(piece) for piece in first)
    k_got, v_got = swap(k_send, 1), swap(v_send, 1)

    kept, low, high = [], [], []
    for order, lines in enumerate((first, second)):
        a, b, c = increments(ids, order, lines, k_own, v_own, k_got, v_got, fast)
        kept.append(a)
        low.append(swap(b, 2))
        high.append(swap(c, 2))
    wide, short = [], []
    for order in range(2):
        sum2, sum3 = add_pair(kept[order], high[order], 1, BF16)
        sum0, sum1 = add_pair(kept[order], low[order], 0, F32)
        three, two, one = swap(sum3, 12), swap(sum2, 8), swap(sum1, 4)
        a, b = renorm(masters[order], sum0, one, two, three, rows_in)
        wide.append(a)
        short.append(b)

    z1, z3, z2 = swap(short[0], 4), swap(short[0], 12), swap(short[0], 8)
    near_low, near_high = jnp.stack([short[0], z1]), jnp.stack([z2, z3])
    far_low, far_high = swap(near_low, 2), swap(near_high, 2)
    second = after(short[1], near_low)
    z1 = swap(second, 4)
    second_low = after(jnp.stack([second, z1]), near_high)
    later = after(short[1], second_low)
    z3, z2 = swap(later, 12), swap(later, 8)
    second_high = jnp.stack([z2, z3])
    mine = (near_low, near_high, far_low, far_high)
    others = tuple(swap(piece, 1) for piece in mine)
    output = apply_fast(ids, 0, 0, mine, queries, None, fast)
    near_low, near_high = second_low, after(second_high, output)
    output = apply_fast(ids, 0, 1, others, queries, output, fast)
    far_low, far_high = swap(near_low, 2), swap(near_high, 2)
    far_high = after(far_high, output)
    mine = (near_low, near_high, far_low, far_high)
    others = tuple(swap(piece, 1) for piece in mine)
    output = apply_fast(ids, 1, 0, mine, queries, output, fast)
    output = apply_fast(ids, 1, 1, others, queries, output, fast)

    came = swap(jnp.stack([wide[0][1], wide[1][1]]), 1)
    return (output, *finish(ids, wide[0], wide[1], came, fast_in, fast_out))


def per_device(queries, keys, values, step_size, fast_in, fast_out):
    fits = (
        lax.axis_size("tok") == 16
        and lax.axis_size("parts") == 2
        and fast_in.shape[0] == 4
        and fast_in.shape[1] % 16 == 0
    )
    chosen = per_device_cube if fits else per_device_generic
    return chosen(queries, keys, values, step_size, fast_in, fast_out)


def solution(mesh):
    placed = (
        P(("parts", "tok"), None),
        P(("parts", "tok"), None),
        P(("parts", "tok"), None),
        P(None, ("parts", "tok")),
        P(None, "tok", None),
        P(None, "tok", None),
    )
    return jax.shard_map(
        per_device,
        mesh=mesh,
        in_specs=placed,
        out_specs=(P(("parts", "tok"), None), P("parts", "tok", None), P("parts", "tok", None)),
        check_vma=False,
    )
```

```python
import functools
import math

import jax
import jax.numpy as jnp
from jax import lax
from jax.experimental import pallas as pl
from jax.experimental.pallas import tpu as pltpu
from jax.sharding import PartitionSpec as P

BF16 = jnp.bfloat16
F32 = jnp.float32
VMEM_LIMIT = 32 * 1024 * 1024


def rms_rows(matrix):
    return matrix * lax.rsqrt(jnp.mean(matrix * matrix, axis=-1, keepdims=True) + 1e-06)


def normalized_heads(tokens, heads, head_size):
    row_count = tokens.shape[0]
    wide = tokens.astype(jnp.float32).reshape(row_count, heads, head_size)
    return rms_rows(wide).astype(jnp.bfloat16)


def head_increments(key_rows, value_rows, rates, weight_in, weight_out, block_root):
    fast = weight_out.shape[0]
    in_root = 1.0 / math.sqrt(weight_in.shape[0])
    out_root = 1.0 / math.sqrt(fast)
    scaled = (rates[:, None] * block_root * value_rows.astype(jnp.float32)).astype(jnp.bfloat16)
    pre = jnp.dot(key_rows, weight_in, preferred_element_type=jnp.float32) * in_root
    gate = pre[:, :fast]
    upper = pre[:, fast:]
    sigma = jax.nn.sigmoid(gate)
    active = gate * sigma
    hidden = (active * upper).astype(jnp.bfloat16)
    back = (
        lax.dot_general(
            scaled, weight_out, (((1,), (1,)), ((), ())), preferred_element_type=jnp.float32
        )
        * out_root
    )
    d_gate = (back * upper * sigma * (1.0 + gate * (1.0 - sigma))).astype(jnp.bfloat16)
    d_up = (back * active).astype(jnp.bfloat16)
    joined = jnp.concatenate([d_gate, d_up], axis=1)
    inc_in = (
        lax.dot_general(
            key_rows, joined, (((0,), (0,)), ((), ())), preferred_element_type=jnp.float32
        )
        * in_root
    )
    inc_out = (
        lax.dot_general(
            hidden, scaled, (((0,), (0,)), ((), ())), preferred_element_type=jnp.float32
        )
        * out_root
    )
    return (inc_in, inc_out)


def local_increments(keyn, values, step_size, weight_in, weight_out, block_root):
    heads = weight_in.shape[0]
    head_size = weight_in.shape[1]
    list_in = []
    list_out = []
    for head_number in range(heads):
        value_rows = values[:, head_number * head_size : (head_number + 1) * head_size]
        part_in, part_out = head_increments(
            keyn[:, head_number, :],
            value_rows,
            step_size[head_number],
            weight_in[head_number],
            weight_out[head_number],
            block_root,
        )
        list_in.append(part_in)
        list_out.append(part_out)
    return (jnp.stack(list_in), jnp.stack(list_out))


def renorm_in(matrix):
    heads, rows_here, double = matrix.shape
    split = matrix.reshape(heads, rows_here, 2, double // 2)
    return rms_rows(split).reshape(heads, rows_here, double)


def apply_head(query_rows, weight_in, weight_out):
    fast = weight_out.shape[0]
    pre = jnp.dot(query_rows, weight_in, preferred_element_type=jnp.float32) * (
        1.0 / math.sqrt(weight_in.shape[0])
    )
    gate = pre[:, :fast]
    hidden = (gate * jax.nn.sigmoid(gate) * pre[:, fast:]).astype(jnp.bfloat16)
    return jnp.dot(hidden, weight_out, preferred_element_type=jnp.float32) * (1.0 / math.sqrt(fast))


def apply_all(queryn, next_in, next_out):
    heads = next_in.shape[0]
    pieces = []
    for head_number in range(heads):
        pieces.append(
            apply_head(queryn[:, head_number, :], next_in[head_number], next_out[head_number])
        )
    return jnp.concatenate(pieces, axis=1).astype(jnp.bfloat16)


def per_device_generic(queries, keys, values, step_size, fast_in, fast_out):
    row_count = keys.shape[0]
    heads = fast_in.shape[0]
    head_size = keys.shape[1] // heads
    block_root = 1.0 / math.sqrt(row_count * lax.axis_size("tok"))
    keyn = normalized_heads(keys, heads, head_size)
    queryn = normalized_heads(queries, heads, head_size)
    master_in, master_out = (
        lax.all_gather(fast_in, "tok", axis=1, tiled=True),
        lax.all_gather(fast_out, "tok", axis=1, tiled=True),
    )
    inc_in, inc_out = local_increments(
        keyn,
        values,
        step_size,
        master_in.astype(jnp.bfloat16),
        master_out.astype(jnp.bfloat16),
        block_root,
    )
    total_in, total_out = lax.psum((inc_in, inc_out), "tok")
    whole_in = renorm_in(master_in + total_in)
    whole_out = rms_rows(master_out + total_out)
    output = apply_all(queryn, whole_in.astype(jnp.bfloat16), whole_out.astype(jnp.bfloat16))
    place = lax.axis_index("tok")
    fast_in_next = lax.dynamic_slice_in_dim(whole_in, place * fast_in.shape[1], fast_in.shape[1], 1)
    fast_out_next = lax.dynamic_slice_in_dim(
        whole_out, place * fast_out.shape[1], fast_out.shape[1], 1
    )
    return (output, fast_in_next, fast_out_next)


def swap(value, bits):
    count = lax.axis_size("tok")
    return lax.ppermute(value, "tok", [(place, place ^ bits) for place in range(count)])


def swap_parts(value):
    return lax.ppermute(value, "parts", [(0, 1), (1, 0)])


def after(value, *before):
    return lax.optimization_barrier((value, before))[0]


def compiler_params():
    return pltpu.CompilerParams(vmem_limit_bytes=VMEM_LIMIT)


def head_of(ids, order, other):
    return 2 * jnp.bitwise_xor(ids[1], other) + jnp.bitwise_xor(ids[2], order)


def normalize_head(block):
    wide = block.astype(F32)
    return (wide * lax.rsqrt(jnp.mean(wide * wide, axis=-1, keepdims=True) + 1e-06)).astype(BF16)


def pack_kernel(ids, in_hbm, out_hbm, own, theirs, in_ref, out_ref, arrived):
    copies = [
        pltpu.make_async_copy(in_hbm, in_ref, arrived.at[0]),
        pltpu.make_async_copy(out_hbm, out_ref, arrived.at[1]),
    ]
    for copy in copies:
        copy.start()
    for copy in copies:
        copy.wait()
    size = out_ref.shape[-1]
    rows = in_ref.shape[1]
    for other, ref in ((0, own), (1, theirs)):
        for order in range(2):
            head = head_of(ids, order, other)
            for block in range(in_ref.shape[2] // size):
                ref[order, block * rows : (block + 1) * rows, :] = in_ref[
                    head, :, block * size : (block + 1) * size
                ]
            ref[order, -out_ref.shape[1] :, :] = out_ref[head]


def pack(ids, fast_in, fast_out):
    rows = 4 * fast_in.shape[1] + fast_out.shape[1]
    shape = jax.ShapeDtypeStruct((2, rows, fast_out.shape[2]), F32)
    return pl.pallas_call(
        pack_kernel,
        in_specs=[pl.BlockSpec(memory_space=pltpu.SMEM)] + [pl.BlockSpec(memory_space=pltpu.HBM)] * 2,
        out_shape=[shape, shape],
        scratch_shapes=[
            pltpu.VMEM(fast_in.shape, F32),
            pltpu.VMEM(fast_out.shape, F32),
            pltpu.SemaphoreType.DMA((2,)),
        ],
        compiler_params=compiler_params(),
        name="pack",
    )(ids, fast_in, fast_out)


def pair_kernel(own, got, master_one, master_two, shard):
    for source, ref in enumerate((own, got)):
        for order, master in enumerate((master_one, master_two)):
            master[source] = ref[order]
        shard[source] = ref[0].astype(BF16)


def pair(own, got):
    wide = jax.ShapeDtypeStruct(own.shape, F32)
    return pl.pallas_call(
        pair_kernel,
        out_shape=[wide, wide, jax.ShapeDtypeStruct(own.shape, BF16)],
        compiler_params=compiler_params(),
        name="pair",
    )(own, got)


def prepare_kernel(heads, block_root, ids, x_ref, *rest):
    own, send = rest[-2:]
    core = ids[1]
    half = heads // 2
    size = x_ref.shape[1] // heads

    if len(rest) == 3:
        rates = rest[0][...]
        columns_of = jnp.concatenate([rates, rates], axis=0).T

    def work(owner, out):
        for local in range(half):
            columns = pl.ds(pl.multiple_of((owner * half + local) * size, size), size)
            into = slice(local * size, (local + 1) * size)
            if len(rest) == 2:
                out[:, into] = normalize_head(x_ref[:, columns])
            else:
                first = columns_of[:, local : local + 1]
                second = columns_of[:, half + local : half + local + 1]
                rate = jnp.where(owner == 0, first, second) * block_root
                out[:, into] = (rate * x_ref[:, columns].astype(F32)).astype(BF16)

    work(core, own)
    work(1 - core, send)


def prepare(ids, tokens, rates, heads, block_root, name):
    rows, width = tokens.shape
    step = 256
    wide = pl.BlockSpec((step, width), lambda i, ids: (i, 0))
    narrow = pl.BlockSpec((step, width // 2), lambda i, ids: (i, 0))
    operands, specs = [tokens], [wide]
    if rates is not None:
        operands.append(rates)
        specs.append(pl.BlockSpec((heads, step), lambda i, ids: (0, i)))
    shape = jax.ShapeDtypeStruct((rows, width // 2), BF16)
    return pl.pallas_call(
        functools.partial(prepare_kernel, heads, block_root),
        grid_spec=pltpu.PrefetchScalarGridSpec(
            num_scalar_prefetch=1,
            grid=(rows // step,),
            in_specs=specs,
            out_specs=[narrow] * 2,
        ),
        out_shape=[shape] * 2,
        compiler_params=compiler_params(),
        cost_estimate=pl.CostEstimate(
            flops=rows * width * 5, bytes_accessed=rows * width * 4, transcendentals=0
        ),
        name=name,
    )(ids, *operands)


def places(chip, core):
    for side in range(2):
        for slot in range(4):
            other = jnp.bitwise_xor(chip, 2 * slot + side)
            for source in range(2):
                yield side, slot, source, 2 * other + jnp.bitwise_xor(core, source)


def assemble(chip, core, lines, w_in, w_out):
    size = w_out.shape[1]
    blocks = w_in.shape[1] // size
    rows_in = w_in.shape[0] // 16
    rows_out = w_out.shape[0] // 16
    for side, slot, source, place in places(chip, core):
        ref = lines[2 * side + slot // 2].at[slot % 2]
        into = pl.ds(pl.multiple_of(place * rows_in, rows_in), rows_in)
        for block in range(blocks):
            w_in[into, block * size : (block + 1) * size] = ref[
                source, block * rows_in : (block + 1) * rows_in, :
            ]
        into = pl.ds(pl.multiple_of(place * rows_out, rows_out), rows_out)
        w_out[into, :] = ref[source, blocks * rows_in :, :]


def increments_kernel(
    ids, near_low, near_high, far_low, far_high, k_own, v_own, k_got, v_got,
    kept, low, high, w_in, w_out, acc_in, acc_out, turned,
):
    step = pl.program_id(0)
    steps = pl.num_programs(0)
    chip, core = ids[0], ids[1]
    size = w_out.shape[1]
    fast = w_out.shape[0]
    in_root = 1.0 / math.sqrt(size)
    out_root = 1.0 / math.sqrt(fast)

    @pl.when(step == 0)
    def _():
        assemble(chip, core, (near_low, near_high, far_low, far_high), w_in, w_out)

    def work(k_ref, v_ref, start_over):
        keyn = k_ref[...]
        scaled = v_ref[...]
        keyn_t = keyn.T
        scaled_t = scaled.T

        def add(ref, columns, value):
            if start_over:
                ref[:, columns] = value
            else:
                ref[:, columns] += value

        chunk = 256
        for start in range(0, fast, chunk):
            gates = slice(start, start + chunk)
            ups = slice(fast + start, fast + start + chunk)
            gate = jnp.dot(keyn, w_in[:, gates], preferred_element_type=F32) * in_root
            upper = jnp.dot(keyn, w_in[:, ups], preferred_element_type=F32) * in_root
            back = (
                lax.dot_general(
                    scaled, w_out[gates, :], (((1,), (1,)), ((), ())), preferred_element_type=F32
                )
                * out_root
            )
            sigma = 0.5 * jnp.tanh(0.5 * gate) + 0.5
            active = gate * sigma
            hidden = (active * upper).astype(BF16)
            d_gate = (back * upper * (sigma + active * (1.0 - sigma))).astype(BF16)
            d_up = (back * active).astype(BF16)
            add(acc_in, gates, jnp.dot(keyn_t, d_gate, preferred_element_type=F32))
            add(acc_in, ups, jnp.dot(keyn_t, d_up, preferred_element_type=F32))
            add(acc_out, gates, jnp.dot(scaled_t, hidden, preferred_element_type=F32))

    @pl.when(step == 0)
    def _():
        work(k_own, v_own, True)

    if k_own.shape[0] * 2 < 2048:

        @pl.when((step > 0) & (step < steps // 2))
        def _():
            work(k_own, v_own, False)

    @pl.when(step >= steps // 2)
    def _():
        work(k_got, v_got, False)

    @pl.when(step == steps - 1)
    def _():
        turned[...] = acc_out[...].T
        blocks = acc_in.shape[1] // size
        rows_in = acc_in.shape[0] // 16
        rows_out = turned.shape[0] // 16
        for side, slot, source, place in places(chip, core):
            ref = kept.at[slot] if side == 0 else (low, high)[slot // 2].at[slot % 2]
            rows = pl.ds(pl.multiple_of(place * rows_in, rows_in), rows_in)
            for block in range(blocks):
                ref[source, block * rows_in : (block + 1) * rows_in, :] = (
                    acc_in[rows, block * size : (block + 1) * size] * in_root
                ).astype(ref.dtype)
            rows = pl.ds(pl.multiple_of(place * rows_out, rows_out), rows_out)
            ref[source, blocks * rows_in :, :] = (turned[rows, :] * out_root).astype(ref.dtype)


def increments(ids, order, lines, k_own, v_own, k_got, v_got, fast):
    rows = k_own.shape[0]
    pair_shape = lines[0].shape
    size = pair_shape[-1]
    step = rows
    half = rows // step
    whole = pl.BlockSpec(pair_shape, lambda i, ids: (0, 0, 0, 0))
    line_shape = (4,) + pair_shape[1:]
    line = pl.BlockSpec(line_shape, lambda i, ids: (0, 0, 0, 0))
    own = pl.BlockSpec((step, size), lambda i, ids: (jnp.minimum(i, half - 1), ids[2] ^ order))
    got = pl.BlockSpec((step, size), lambda i, ids: (jnp.maximum(i - half, 0), ids[2] ^ order))
    return pl.pallas_call(
        increments_kernel,
        grid_spec=pltpu.PrefetchScalarGridSpec(
            num_scalar_prefetch=1,
            grid=(2 * half,),
            in_specs=[whole] * 4 + [own, own, got, got],
            out_specs=[line, whole, whole],
            scratch_shapes=[
                pltpu.VMEM((size, 2 * fast), BF16),
                pltpu.VMEM((fast, size), BF16),
                pltpu.VMEM((size, 2 * fast), F32),
                pltpu.VMEM((size, fast), F32),
                pltpu.VMEM((fast, size), F32),
            ],
        ),
        out_shape=[
            jax.ShapeDtypeStruct(line_shape, F32),
            jax.ShapeDtypeStruct(pair_shape, BF16),
            jax.ShapeDtypeStruct(pair_shape, BF16),
        ],
        compiler_params=compiler_params(),
        cost_estimate=pl.CostEstimate(
            flops=2 * rows * size * fast * 12, bytes_accessed=rows * size * 8, transcendentals=0
        ),
        name="increments",
    )(ids, *lines, k_own, v_own, k_got, v_got)


def add_kernel(kept, came, first, second):
    first[...] = (kept[0] + came[0].astype(F32)).astype(first.dtype)
    second[...] = (kept[1] + came[1].astype(F32)).astype(second.dtype)


def add_pair(kept, came, which, first_type):
    shape = came.shape
    flat = (0,) * (len(shape) - 1)
    return pl.pallas_call(
        add_kernel,
        grid=(1,),
        in_specs=[
            pl.BlockSpec(shape, lambda i: (which,) + flat),
            pl.BlockSpec(shape, lambda i: (0,) + flat),
        ],
        out_specs=[pl.BlockSpec(shape[1:], lambda i: flat)] * 2,
        out_shape=[
            jax.ShapeDtypeStruct(shape[1:], first_type),
            jax.ShapeDtypeStruct(shape[1:], BF16),
        ],
        compiler_params=compiler_params(),
        name="add_pair",
    )(kept, came)


def renorm_kernel(rows_in, master, kept, one, two, three, wide, short):
    size = master.shape[-1]
    for source in range(2):
        fresh = (
            master[source]
            + kept[source]
            + one[source].astype(F32)
            + two[source].astype(F32)
            + three[source].astype(F32)
        )
        for part in range(2):
            first = 2 * part * rows_in
            left = fresh[first : first + rows_in, :]
            right = fresh[first + rows_in : first + 2 * rows_in, :]
            total = jnp.sum(left * left + right * right, axis=-1, keepdims=True)
            factor = lax.rsqrt(total * (1.0 / (2 * size)) + 1e-06)
            for at, value in ((first, left), (first + rows_in, right)):
                done = value * factor
                wide[source, at : at + rows_in, :] = done
                short[source, at : at + rows_in, :] = done.astype(BF16)
        tail = fresh[4 * rows_in :, :]
        done = tail * lax.rsqrt(jnp.mean(tail * tail, axis=-1, keepdims=True) + 1e-06)
        wide[source, 4 * rows_in :, :] = done
        short[source, 4 * rows_in :, :] = done.astype(BF16)


def renorm(master, kept, one, two, three, rows_in):
    shape = master.shape
    return pl.pallas_call(
        functools.partial(renorm_kernel, rows_in),
        out_shape=[jax.ShapeDtypeStruct(shape, F32), jax.ShapeDtypeStruct(shape, BF16)],
        compiler_params=compiler_params(),
        name="renorm",
    )(master, kept, one, two, three)


def apply_kernel(order, other, ids, near_low, near_high, far_low, far_high, q_ref, *rest):
    o_ref, w_in, w_out = rest[-3:]
    chip, core = ids[0], ids[1]
    fast, size = w_out.shape
    lines = (near_low, near_high, far_low, far_high)
    assemble(chip, jnp.bitwise_xor(core, other), lines, w_in, w_out)
    columns = pl.ds(pl.multiple_of(head_of(ids, order, other) * size, size), size)
    in_root = 1.0 / math.sqrt(size)
    out_root = 1.0 / math.sqrt(fast)
    step = 512
    for start in range(0, q_ref.shape[0], step):
        rows = slice(start, start + step)
        query = normalize_head(q_ref[rows, columns])
        gate = jnp.dot(query, w_in[:, :fast], preferred_element_type=F32) * in_root
        upper = jnp.dot(query, w_in[:, fast:], preferred_element_type=F32) * in_root
        hidden = (gate * (0.5 * jnp.tanh(0.5 * gate) + 0.5) * upper).astype(BF16)
        result = jnp.dot(hidden, w_out[...], preferred_element_type=F32) * out_root
        o_ref[rows, :] = result.astype(BF16)


def apply_fast(ids, order, other, lines, queries, output, fast):
    rows, width = queries.shape
    size = lines[0].shape[-1]
    inside = pl.BlockSpec(memory_space=pltpu.VMEM)
    operands = [ids, *lines, queries]
    specs = [inside] * 5
    aliases = {}
    if output is not None:
        operands.append(output)
        specs.append(pl.BlockSpec(memory_space=pl.ANY))
        aliases = {6: 0}
    return pl.pallas_call(
        functools.partial(apply_kernel, order, other),
        grid_spec=pltpu.PrefetchScalarGridSpec(
            num_scalar_prefetch=1,
            grid=(1,),
            in_specs=specs,
            out_specs=pl.BlockSpec((rows, size), lambda i, ids: (0, head_of(ids, order, other))),
            scratch_shapes=[pltpu.VMEM((size, 2 * fast), BF16), pltpu.VMEM((fast, size), BF16)],
        ),
        out_shape=jax.ShapeDtypeStruct((rows, width), BF16),
        input_output_aliases=aliases,
        compiler_params=compiler_params(),
        cost_estimate=pl.CostEstimate(
            flops=2 * rows * size * fast * 3, bytes_accessed=rows * size * 4, transcendentals=0
        ),
        name="apply",
    )(*operands)


def finish_kernel(rows_in, ids, one, two, came, in_next, out_next):
    size = out_next.shape[-1]
    for order, mine in enumerate((one, two)):
        for other, ref in ((0, mine.at[0]), (1, came.at[order])):
            head = head_of(ids, order, other)
            for block in range(4):
                in_next[head, :, block * size : (block + 1) * size] = ref[
                    block * rows_in : (block + 1) * rows_in, :
                ]
            out_next[head] = ref[4 * rows_in :, :]


def finish(ids, one, two, came, fast_in, fast_out):
    return pl.pallas_call(
        functools.partial(finish_kernel, fast_in.shape[1]),
        in_specs=[pl.BlockSpec(memory_space=pltpu.SMEM)] + [pl.BlockSpec(memory_space=pltpu.VMEM)] * 3,
        out_shape=[
            jax.ShapeDtypeStruct(fast_in.shape, F32),
            jax.ShapeDtypeStruct(fast_out.shape, F32),
        ],
        compiler_params=compiler_params(),
        name="finish",
    )(ids, one, two, came)


def gather_chips(shard):
    z1, z3, z2 = swap(shard, 4), swap(shard, 12), swap(shard, 8)
    near_low, near_high = jnp.stack([shard, z1]), jnp.stack([z2, z3])
    far_low = swap(near_low, 2)
    near_high = after(near_high, far_low)
    return near_low, near_high, far_low, swap(near_high, 2)


def per_device_cube(queries, keys, values, step_size, fast_in, fast_out):
    rows = keys.shape[0]
    heads = fast_in.shape[0]
    fast = fast_in.shape[2] // 2
    rows_in = fast_in.shape[1]
    place = lax.axis_index("tok")
    ids = jnp.stack([place // 2, place % 2, lax.axis_index("parts")]).astype(jnp.int32)
    block_root = 1.0 / math.sqrt(rows * lax.axis_size("tok"))

    own, theirs = pack(ids, fast_in, fast_out)
    got = swap(theirs, 1)
    later = after(ids, own)
    k_own, k_send = prepare(later, keys, None, heads, None, "keys")
    v_own, v_send = prepare(later, values, step_size, heads, block_root, "values")
    got = after(got, k_send, v_send)
    master_one, master_two, shard = pair(own, got)
    masters = (master_one, master_two)
    first = gather_chips(shard)
    second = tuple(swap_parts(piece) for piece in first)
    k_got, v_got = swap(k_send, 1), swap(v_send, 1)

    wide, short = [], []
    for order in range(2):
        lines = second if order else first
        kept, low, high = increments(ids, order, lines, k_own, v_own, k_got, v_got, fast)
        high, low = swap(high, 2), swap(low, 2)
        sum2, sum3 = add_pair(kept, high, 1, BF16)
        sum0, sum1 = add_pair(kept, low, 0, F32)
        three, two, one = swap(sum3, 12), swap(sum2, 8), swap(sum1, 4)
        a, b = renorm(masters[order], sum0, one, two, three, rows_in)
        wide.append(a)
        short.append(b)

    z1, z3, z2 = swap(short[0], 4), swap(short[0], 12), swap(short[0], 8)
    near_low, near_high = jnp.stack([short[0], z1]), jnp.stack([z2, z3])
    far_low, far_high = swap(near_low, 2), swap(near_high, 2)
    second = after(short[1], near_low)
    z1 = swap(second, 4)
    second_low = after(jnp.stack([second, z1]), near_high)
    later = after(short[1], second_low)
    z3, z2 = swap(later, 12), swap(later, 8)
    second_high = jnp.stack([z2, z3])
    mine = (near_low, near_high, far_low, far_high)
    others = tuple(swap(piece, 1) for piece in mine)
    output = apply_fast(ids, 0, 0, mine, queries, None, fast)
    near_low, near_high = second_low, second_high
    came = swap(jnp.stack([wide[0][1], wide[1][1]]), 1)
    updated = finish(ids, wide[0], wide[1], came, fast_in, fast_out)
    output = after(output, *updated)
    output = apply_fast(ids, 0, 1, others, queries, output, fast)
    far_low, far_high = swap(near_low, 2), swap(near_high, 2)
    far_high = after(far_high, output)
    mine = (near_low, near_high, far_low, far_high)
    others = tuple(swap(piece, 1) for piece in mine)
    output = apply_fast(ids, 1, 0, mine, queries, output, fast)
    output = apply_fast(ids, 1, 1, others, queries, output, fast)

    return (output, *updated)


def per_device(queries, keys, values, step_size, fast_in, fast_out):
    fits = (
        lax.axis_size("tok") == 16
        and lax.axis_size("parts") == 2
        and fast_in.shape[0] == 4
        and fast_in.shape[1] % 16 == 0
    )
    chosen = per_device_cube if fits else per_device_generic
    return chosen(queries, keys, values, step_size, fast_in, fast_out)


def solution(mesh):
    placed = (
        P(("parts", "tok"), None),
        P(("parts", "tok"), None),
        P(("parts", "tok"), None),
        P(None, ("parts", "tok")),
        P(None, "tok", None),
        P(None, "tok", None),
    )
    return jax.shard_map(
        per_device,
        mesh=mesh,
        in_specs=placed,
        out_specs=(P(("parts", "tok"), None), P("parts", "tok", None), P("parts", "tok", None)),
        check_vma=False,
    )
```

```python
import functools
import math

import jax
import jax.numpy as jnp
from jax import lax
from jax.experimental import pallas as pl
from jax.experimental.pallas import tpu as pltpu
from jax.sharding import PartitionSpec as P

BF16 = jnp.bfloat16
F32 = jnp.float32
VMEM_LIMIT = 32 * 1024 * 1024


def rms_rows(matrix):
    return matrix * lax.rsqrt(jnp.mean(matrix * matrix, axis=-1, keepdims=True) + 1e-06)


def normalized_heads(tokens, heads, head_size):
    row_count = tokens.shape[0]
    wide = tokens.astype(jnp.float32).reshape(row_count, heads, head_size)
    return rms_rows(wide).astype(jnp.bfloat16)


def head_increments(key_rows, value_rows, rates, weight_in, weight_out, block_root):
    fast = weight_out.shape[0]
    in_root = 1.0 / math.sqrt(weight_in.shape[0])
    out_root = 1.0 / math.sqrt(fast)
    scaled = (rates[:, None] * block_root * value_rows.astype(jnp.float32)).astype(jnp.bfloat16)
    pre = jnp.dot(key_rows, weight_in, preferred_element_type=jnp.float32) * in_root
    gate = pre[:, :fast]
    upper = pre[:, fast:]
    sigma = jax.nn.sigmoid(gate)
    active = gate * sigma
    hidden = (active * upper).astype(jnp.bfloat16)
    back = (
        lax.dot_general(
            scaled, weight_out, (((1,), (1,)), ((), ())), preferred_element_type=jnp.float32
        )
        * out_root
    )
    d_gate = (back * upper * sigma * (1.0 + gate * (1.0 - sigma))).astype(jnp.bfloat16)
    d_up = (back * active).astype(jnp.bfloat16)
    joined = jnp.concatenate([d_gate, d_up], axis=1)
    inc_in = (
        lax.dot_general(
            key_rows, joined, (((0,), (0,)), ((), ())), preferred_element_type=jnp.float32
        )
        * in_root
    )
    inc_out = (
        lax.dot_general(
            hidden, scaled, (((0,), (0,)), ((), ())), preferred_element_type=jnp.float32
        )
        * out_root
    )
    return (inc_in, inc_out)


def local_increments(keyn, values, step_size, weight_in, weight_out, block_root):
    heads = weight_in.shape[0]
    head_size = weight_in.shape[1]
    list_in = []
    list_out = []
    for head_number in range(heads):
        value_rows = values[:, head_number * head_size : (head_number + 1) * head_size]
        part_in, part_out = head_increments(
            keyn[:, head_number, :],
            value_rows,
            step_size[head_number],
            weight_in[head_number],
            weight_out[head_number],
            block_root,
        )
        list_in.append(part_in)
        list_out.append(part_out)
    return (jnp.stack(list_in), jnp.stack(list_out))


def renorm_in(matrix):
    heads, rows_here, double = matrix.shape
    split = matrix.reshape(heads, rows_here, 2, double // 2)
    return rms_rows(split).reshape(heads, rows_here, double)


def apply_head(query_rows, weight_in, weight_out):
    fast = weight_out.shape[0]
    pre = jnp.dot(query_rows, weight_in, preferred_element_type=jnp.float32) * (
        1.0 / math.sqrt(weight_in.shape[0])
    )
    gate = pre[:, :fast]
    hidden = (gate * jax.nn.sigmoid(gate) * pre[:, fast:]).astype(jnp.bfloat16)
    return jnp.dot(hidden, weight_out, preferred_element_type=jnp.float32) * (1.0 / math.sqrt(fast))


def apply_all(queryn, next_in, next_out):
    heads = next_in.shape[0]
    pieces = []
    for head_number in range(heads):
        pieces.append(
            apply_head(queryn[:, head_number, :], next_in[head_number], next_out[head_number])
        )
    return jnp.concatenate(pieces, axis=1).astype(jnp.bfloat16)


def per_device_generic(queries, keys, values, step_size, fast_in, fast_out):
    row_count = keys.shape[0]
    heads = fast_in.shape[0]
    head_size = keys.shape[1] // heads
    block_root = 1.0 / math.sqrt(row_count * lax.axis_size("tok"))
    keyn = normalized_heads(keys, heads, head_size)
    queryn = normalized_heads(queries, heads, head_size)
    master_in, master_out = (
        lax.all_gather(fast_in, "tok", axis=1, tiled=True),
        lax.all_gather(fast_out, "tok", axis=1, tiled=True),
    )
    inc_in, inc_out = local_increments(
        keyn,
        values,
        step_size,
        master_in.astype(jnp.bfloat16),
        master_out.astype(jnp.bfloat16),
        block_root,
    )
    total_in, total_out = lax.psum((inc_in, inc_out), "tok")
    whole_in = renorm_in(master_in + total_in)
    whole_out = rms_rows(master_out + total_out)
    output = apply_all(queryn, whole_in.astype(jnp.bfloat16), whole_out.astype(jnp.bfloat16))
    place = lax.axis_index("tok")
    fast_in_next = lax.dynamic_slice_in_dim(whole_in, place * fast_in.shape[1], fast_in.shape[1], 1)
    fast_out_next = lax.dynamic_slice_in_dim(
        whole_out, place * fast_out.shape[1], fast_out.shape[1], 1
    )
    return (output, fast_in_next, fast_out_next)


def swap(value, bits):
    count = lax.axis_size("tok")
    return lax.ppermute(value, "tok", [(place, place ^ bits) for place in range(count)])


def swap_parts(value):
    return lax.ppermute(value, "parts", [(0, 1), (1, 0)])


def after(value, *before):
    return lax.optimization_barrier((value, before))[0]


def compiler_params():
    return pltpu.CompilerParams(vmem_limit_bytes=VMEM_LIMIT)


def head_of(ids, order, other):
    return 2 * jnp.bitwise_xor(ids[1], other) + jnp.bitwise_xor(ids[2], order)


def normalize_head(block):
    wide = block.astype(F32)
    return (wide * lax.rsqrt(jnp.mean(wide * wide, axis=-1, keepdims=True) + 1e-06)).astype(BF16)


def pack_kernel(ids, in_hbm, out_hbm, own, theirs, in_ref, out_ref, arrived):
    copies = [
        pltpu.make_async_copy(in_hbm, in_ref, arrived.at[0]),
        pltpu.make_async_copy(out_hbm, out_ref, arrived.at[1]),
    ]
    for copy in copies:
        copy.start()
    for copy in copies:
        copy.wait()
    size = out_ref.shape[-1]
    rows = in_ref.shape[1]
    for other, ref in ((0, own), (1, theirs)):
        for order in range(2):
            head = head_of(ids, order, other)
            for block in range(in_ref.shape[2] // size):
                ref[order, block * rows : (block + 1) * rows, :] = in_ref[
                    head, :, block * size : (block + 1) * size
                ]
            ref[order, -out_ref.shape[1] :, :] = out_ref[head]


def pack(ids, fast_in, fast_out):
    rows = 4 * fast_in.shape[1] + fast_out.shape[1]
    shape = jax.ShapeDtypeStruct((2, rows, fast_out.shape[2]), F32)
    return pl.pallas_call(
        pack_kernel,
        in_specs=[pl.BlockSpec(memory_space=pltpu.SMEM)] + [pl.BlockSpec(memory_space=pltpu.HBM)] * 2,
        out_shape=[shape, shape],
        scratch_shapes=[
            pltpu.VMEM(fast_in.shape, F32),
            pltpu.VMEM(fast_out.shape, F32),
            pltpu.SemaphoreType.DMA((2,)),
        ],
        compiler_params=compiler_params(),
        name="pack",
    )(ids, fast_in, fast_out)


def pair_kernel(own, got, master_one, master_two, shard):
    for source, ref in enumerate((own, got)):
        for order, master in enumerate((master_one, master_two)):
            master[source] = ref[order]
        shard[source] = ref[0].astype(BF16)


def pair(own, got):
    wide = jax.ShapeDtypeStruct(own.shape, F32)
    return pl.pallas_call(
        pair_kernel,
        out_shape=[wide, wide, jax.ShapeDtypeStruct(own.shape, BF16)],
        compiler_params=compiler_params(),
        name="pair",
    )(own, got)


def prepare_kernel(heads, block_root, ids, x_ref, *rest):
    own, send = rest[-2:]
    core = ids[1]
    half = heads // 2
    size = x_ref.shape[1] // heads

    if len(rest) == 3:
        rates = rest[0][...]
        columns_of = jnp.concatenate([rates, rates], axis=0).T

    def work(owner, out):
        for local in range(half):
            columns = pl.ds(pl.multiple_of((owner * half + local) * size, size), size)
            into = slice(local * size, (local + 1) * size)
            if len(rest) == 2:
                out[:, into] = normalize_head(x_ref[:, columns])
            else:
                first = columns_of[:, local : local + 1]
                second = columns_of[:, half + local : half + local + 1]
                rate = jnp.where(owner == 0, first, second) * block_root
                out[:, into] = (rate * x_ref[:, columns].astype(F32)).astype(BF16)

    work(core, own)
    work(1 - core, send)


def prepare(ids, tokens, rates, heads, block_root, name):
    rows, width = tokens.shape
    step = 256
    wide = pl.BlockSpec((step, width), lambda i, ids: (i, 0))
    narrow = pl.BlockSpec((step, width // 2), lambda i, ids: (i, 0))
    operands, specs = [tokens], [wide]
    if rates is not None:
        operands.append(rates)
        specs.append(pl.BlockSpec((heads, step), lambda i, ids: (0, i)))
    shape = jax.ShapeDtypeStruct((rows, width // 2), BF16)
    return pl.pallas_call(
        functools.partial(prepare_kernel, heads, block_root),
        grid_spec=pltpu.PrefetchScalarGridSpec(
            num_scalar_prefetch=1,
            grid=(rows // step,),
            in_specs=specs,
            out_specs=[narrow] * 2,
        ),
        out_shape=[shape] * 2,
        compiler_params=compiler_params(),
        cost_estimate=pl.CostEstimate(
            flops=rows * width * 5, bytes_accessed=rows * width * 4, transcendentals=0
        ),
        name=name,
    )(ids, *operands)


def places(chip, core):
    for side in range(2):
        for slot in range(4):
            other = jnp.bitwise_xor(chip, 2 * slot + side)
            for source in range(2):
                yield side, slot, source, 2 * other + jnp.bitwise_xor(core, source)


def assemble(chip, core, lines, w_in, w_out):
    size = w_out.shape[1]
    blocks = w_in.shape[1] // size
    rows_in = w_in.shape[0] // 16
    rows_out = w_out.shape[0] // 16
    for side, slot, source, place in places(chip, core):
        ref = lines[2 * side + slot // 2].at[slot % 2]
        into = pl.ds(pl.multiple_of(place * rows_in, rows_in), rows_in)
        for block in range(blocks):
            w_in[into, block * size : (block + 1) * size] = ref[
                source, block * rows_in : (block + 1) * rows_in, :
            ]
        into = pl.ds(pl.multiple_of(place * rows_out, rows_out), rows_out)
        w_out[into, :] = ref[source, blocks * rows_in :, :]


def increments_kernel(
    ids, near_low, near_high, far_low, far_high, k_own, v_own, k_got, v_got,
    kept, low, high, w_in, w_out, acc_in, acc_out, turned,
):
    step = pl.program_id(0)
    steps = pl.num_programs(0)
    chip, core = ids[0], ids[1]
    size = w_out.shape[1]
    fast = w_out.shape[0]
    in_root = 1.0 / math.sqrt(size)
    out_root = 1.0 / math.sqrt(fast)

    @pl.when(step == 0)
    def _():
        assemble(chip, core, (near_low, near_high, far_low, far_high), w_in, w_out)

    def work(k_ref, v_ref, start_over):
        keyn = k_ref[...]
        scaled = v_ref[...]
        keyn_t = keyn.T
        scaled_t = scaled.T

        def add(ref, columns, value):
            if start_over:
                ref[:, columns] = value
            else:
                ref[:, columns] += value

        chunk = 256
        for start in range(0, fast, chunk):
            gates = slice(start, start + chunk)
            ups = slice(fast + start, fast + start + chunk)
            gate = jnp.dot(keyn, w_in[:, gates], preferred_element_type=F32) * in_root
            upper = jnp.dot(keyn, w_in[:, ups], preferred_element_type=F32) * in_root
            back = (
                lax.dot_general(
                    scaled, w_out[gates, :], (((1,), (1,)), ((), ())), preferred_element_type=F32
                )
                * out_root
            )
            sigma = 0.5 * jnp.tanh(0.5 * gate) + 0.5
            active = gate * sigma
            hidden = (active * upper).astype(BF16)
            d_gate = (back * upper * (sigma + active * (1.0 - sigma))).astype(BF16)
            d_up = (back * active).astype(BF16)
            add(acc_in, gates, jnp.dot(keyn_t, d_gate, preferred_element_type=F32))
            add(acc_in, ups, jnp.dot(keyn_t, d_up, preferred_element_type=F32))
            add(acc_out, gates, jnp.dot(scaled_t, hidden, preferred_element_type=F32))

    @pl.when(step == 0)
    def _():
        work(k_own, v_own, True)

    if k_own.shape[0] * 2 < 2048:

        @pl.when((step > 0) & (step < steps // 2))
        def _():
            work(k_own, v_own, False)

    @pl.when(step >= steps // 2)
    def _():
        work(k_got, v_got, False)

    @pl.when(step == steps - 1)
    def _():
        turned[...] = acc_out[...].T
        blocks = acc_in.shape[1] // size
        rows_in = acc_in.shape[0] // 16
        rows_out = turned.shape[0] // 16
        for side, slot, source, place in places(chip, core):
            ref = kept.at[slot] if side == 0 else (low, high)[slot // 2].at[slot % 2]
            rows = pl.ds(pl.multiple_of(place * rows_in, rows_in), rows_in)
            for block in range(blocks):
                ref[source, block * rows_in : (block + 1) * rows_in, :] = (
                    acc_in[rows, block * size : (block + 1) * size] * in_root
                ).astype(ref.dtype)
            rows = pl.ds(pl.multiple_of(place * rows_out, rows_out), rows_out)
            ref[source, blocks * rows_in :, :] = (turned[rows, :] * out_root).astype(ref.dtype)


def increments(ids, order, lines, k_own, v_own, k_got, v_got, fast):
    rows = k_own.shape[0]
    pair_shape = lines[0].shape
    size = pair_shape[-1]
    step = rows
    half = rows // step
    whole = pl.BlockSpec(pair_shape, lambda i, ids: (0, 0, 0, 0))
    line_shape = (4,) + pair_shape[1:]
    line = pl.BlockSpec(line_shape, lambda i, ids: (0, 0, 0, 0))
    own = pl.BlockSpec((step, size), lambda i, ids: (jnp.minimum(i, half - 1), ids[2] ^ order))
    got = pl.BlockSpec((step, size), lambda i, ids: (jnp.maximum(i - half, 0), ids[2] ^ order))
    return pl.pallas_call(
        increments_kernel,
        grid_spec=pltpu.PrefetchScalarGridSpec(
            num_scalar_prefetch=1,
            grid=(2 * half,),
            in_specs=[whole] * 4 + [own, own, got, got],
            out_specs=[line, whole, whole],
            scratch_shapes=[
                pltpu.VMEM((size, 2 * fast), BF16),
                pltpu.VMEM((fast, size), BF16),
                pltpu.VMEM((size, 2 * fast), F32),
                pltpu.VMEM((size, fast), F32),
                pltpu.VMEM((fast, size), F32),
            ],
        ),
        out_shape=[
            jax.ShapeDtypeStruct(line_shape, F32),
            jax.ShapeDtypeStruct(pair_shape, BF16),
            jax.ShapeDtypeStruct(pair_shape, BF16),
        ],
        compiler_params=compiler_params(),
        cost_estimate=pl.CostEstimate(
            flops=2 * rows * size * fast * 12, bytes_accessed=rows * size * 8, transcendentals=0
        ),
        name="increments",
    )(ids, *lines, k_own, v_own, k_got, v_got)


def add_kernel(kept, came, first, second):
    first[...] = (kept[0] + came[0].astype(F32)).astype(first.dtype)
    second[...] = (kept[1] + came[1].astype(F32)).astype(second.dtype)


def add_pair(kept, came, which, first_type):
    shape = came.shape
    flat = (0,) * (len(shape) - 1)
    return pl.pallas_call(
        add_kernel,
        grid=(1,),
        in_specs=[
            pl.BlockSpec(shape, lambda i: (which,) + flat),
            pl.BlockSpec(shape, lambda i: (0,) + flat),
        ],
        out_specs=[pl.BlockSpec(shape[1:], lambda i: flat)] * 2,
        out_shape=[
            jax.ShapeDtypeStruct(shape[1:], first_type),
            jax.ShapeDtypeStruct(shape[1:], BF16),
        ],
        compiler_params=compiler_params(),
        name="add_pair",
    )(kept, came)


def renorm_kernel(rows_in, master, kept, one, two, three, wide, short):
    size = master.shape[-1]
    for source in range(2):
        fresh = (
            master[source]
            + kept[source]
            + one[source].astype(F32)
            + two[source].astype(F32)
            + three[source].astype(F32)
        )
        for part in range(2):
            first = 2 * part * rows_in
            left = fresh[first : first + rows_in, :]
            right = fresh[first + rows_in : first + 2 * rows_in, :]
            total = jnp.sum(left * left + right * right, axis=-1, keepdims=True)
            factor = lax.rsqrt(total * (1.0 / (2 * size)) + 1e-06)
            for at, value in ((first, left), (first + rows_in, right)):
                done = value * factor
                wide[source, at : at + rows_in, :] = done
                short[source, at : at + rows_in, :] = done.astype(BF16)
        tail = fresh[4 * rows_in :, :]
        done = tail * lax.rsqrt(jnp.mean(tail * tail, axis=-1, keepdims=True) + 1e-06)
        wide[source, 4 * rows_in :, :] = done
        short[source, 4 * rows_in :, :] = done.astype(BF16)


def renorm(master, kept, one, two, three, rows_in):
    shape = master.shape
    return pl.pallas_call(
        functools.partial(renorm_kernel, rows_in),
        out_shape=[jax.ShapeDtypeStruct(shape, F32), jax.ShapeDtypeStruct(shape, BF16)],
        compiler_params=compiler_params(),
        name="renorm",
    )(master, kept, one, two, three)


def apply_kernel(order, other, ids, near_low, near_high, far_low, far_high, q_ref, *rest):
    o_ref, w_in, w_out = rest[-3:]
    chip, core = ids[0], ids[1]
    fast, size = w_out.shape
    lines = (near_low, near_high, far_low, far_high)
    assemble(chip, jnp.bitwise_xor(core, other), lines, w_in, w_out)
    columns = pl.ds(pl.multiple_of(head_of(ids, order, other) * size, size), size)
    in_root = 1.0 / math.sqrt(size)
    out_root = 1.0 / math.sqrt(fast)
    step = 512
    for start in range(0, q_ref.shape[0], step):
        rows = slice(start, start + step)
        query = normalize_head(q_ref[rows, columns])
        gate = jnp.dot(query, w_in[:, :fast], preferred_element_type=F32) * in_root
        upper = jnp.dot(query, w_in[:, fast:], preferred_element_type=F32) * in_root
        hidden = (gate * (0.5 * jnp.tanh(0.5 * gate) + 0.5) * upper).astype(BF16)
        result = jnp.dot(hidden, w_out[...], preferred_element_type=F32) * out_root
        o_ref[rows, :] = result.astype(BF16)


def apply_fast(ids, order, other, lines, queries, output, fast):
    rows, width = queries.shape
    size = lines[0].shape[-1]
    inside = pl.BlockSpec(memory_space=pltpu.VMEM)
    operands = [ids, *lines, queries]
    specs = [inside] * 5
    aliases = {}
    if output is not None:
        operands.append(output)
        specs.append(pl.BlockSpec(memory_space=pl.ANY))
        aliases = {6: 0}
    return pl.pallas_call(
        functools.partial(apply_kernel, order, other),
        grid_spec=pltpu.PrefetchScalarGridSpec(
            num_scalar_prefetch=1,
            grid=(1,),
            in_specs=specs,
            out_specs=pl.BlockSpec((rows, size), lambda i, ids: (0, head_of(ids, order, other))),
            scratch_shapes=[pltpu.VMEM((size, 2 * fast), BF16), pltpu.VMEM((fast, size), BF16)],
        ),
        out_shape=jax.ShapeDtypeStruct((rows, width), BF16),
        input_output_aliases=aliases,
        compiler_params=compiler_params(),
        cost_estimate=pl.CostEstimate(
            flops=2 * rows * size * fast * 3, bytes_accessed=rows * size * 4, transcendentals=0
        ),
        name="apply",
    )(*operands)


def finish_kernel(rows_in, ids, one, two, came, in_next, out_next):
    size = out_next.shape[-1]
    for order, mine in enumerate((one, two)):
        for other, ref in ((0, mine.at[0]), (1, came.at[order])):
            head = head_of(ids, order, other)
            for block in range(4):
                in_next[head, :, block * size : (block + 1) * size] = ref[
                    block * rows_in : (block + 1) * rows_in, :
                ]
            out_next[head] = ref[4 * rows_in :, :]


def finish(ids, one, two, came, fast_in, fast_out):
    return pl.pallas_call(
        functools.partial(finish_kernel, fast_in.shape[1]),
        in_specs=[pl.BlockSpec(memory_space=pltpu.SMEM)] + [pl.BlockSpec(memory_space=pltpu.VMEM)] * 3,
        out_shape=[
            jax.ShapeDtypeStruct(fast_in.shape, F32),
            jax.ShapeDtypeStruct(fast_out.shape, F32),
        ],
        compiler_params=compiler_params(),
        name="finish",
    )(ids, one, two, came)


def per_device_cube(queries, keys, values, step_size, fast_in, fast_out):
    rows = keys.shape[0]
    heads = fast_in.shape[0]
    fast = fast_in.shape[2] // 2
    rows_in = fast_in.shape[1]
    place = lax.axis_index("tok")
    ids = jnp.stack([place // 2, place % 2, lax.axis_index("parts")]).astype(jnp.int32)
    block_root = 1.0 / math.sqrt(rows * lax.axis_size("tok"))

    own, theirs = pack(ids, fast_in, fast_out)
    got = swap(theirs, 1)
    later = after(ids, own)
    k_own, k_send = prepare(later, keys, None, heads, None, "keys")
    v_own, v_send = prepare(later, values, step_size, heads, block_root, "values")
    got = after(got, k_send, v_send)
    master_one, master_two, shard = pair(own, got)
    masters = (master_one, master_two)
    k_got, v_got = swap(k_send, 1), swap(v_send, 1)
    z1, z3, z2 = swap(shard, 4), swap(shard, 12), swap(shard, 8)
    near_low = after(jnp.stack([shard, z1]), k_got, v_got)
    far_low, other_near_low = swap(near_low, 2), swap_parts(near_low)
    near_high = after(jnp.stack([z2, z3]), far_low, other_near_low)
    far_high = swap(near_high, 2)
    first = (near_low, near_high, far_low, far_high)
    second = (other_near_low, *(swap_parts(piece) for piece in first[1:]))

    wide, short = [], []
    for order in range(2):
        lines = second if order else first
        later = ids if order else after(ids, second[2])
        kept, low, high = increments(later, order, lines, k_own, v_own, k_got, v_got, fast)
        high, low = swap(high, 2), swap(low, 2)
        sum2, sum3 = add_pair(kept, high, 1, BF16)
        sum0, sum1 = add_pair(kept, low, 0, F32)
        three, two, one = swap(sum3, 12), swap(sum2, 8), swap(sum1, 4)
        a, b = renorm(masters[order], sum0, one, two, three, rows_in)
        wide.append(a)
        short.append(b)

    z1, z3, z2 = swap(short[0], 4), swap(short[0], 12), swap(short[0], 8)
    near_low, near_high = jnp.stack([short[0], z1]), jnp.stack([z2, z3])
    far_low, far_high = swap(near_low, 2), swap(near_high, 2)
    second = after(short[1], near_low)
    z1 = swap(second, 4)
    second_low = after(jnp.stack([second, z1]), near_high)
    later = after(short[1], second_low)
    z3, z2 = swap(later, 12), swap(later, 8)
    second_high = jnp.stack([z2, z3])
    mine = (near_low, near_high, far_low, far_high)
    others = tuple(swap(piece, 1) for piece in mine)
    output = apply_fast(ids, 0, 0, mine, queries, None, fast)
    near_low, near_high = second_low, second_high
    came = swap(jnp.stack([wide[0][1], wide[1][1]]), 1)
    updated = finish(ids, wide[0], wide[1], came, fast_in, fast_out)
    output = after(output, *updated)
    output = apply_fast(ids, 0, 1, others, queries, output, fast)
    far_low, far_high = swap(near_low, 2), swap(near_high, 2)
    far_high = after(far_high, output)
    mine = (near_low, near_high, far_low, far_high)
    others = tuple(swap(piece, 1) for piece in mine)
    output = apply_fast(ids, 1, 0, mine, queries, output, fast)
    output = apply_fast(ids, 1, 1, others, queries, output, fast)

    return (output, *updated)


def per_device(queries, keys, values, step_size, fast_in, fast_out):
    fits = (
        lax.axis_size("tok") == 16
        and lax.axis_size("parts") == 2
        and fast_in.shape[0] == 4
        and fast_in.shape[1] % 16 == 0
    )
    chosen = per_device_cube if fits else per_device_generic
    return chosen(queries, keys, values, step_size, fast_in, fast_out)


def solution(mesh):
    placed = (
        P(("parts", "tok"), None),
        P(("parts", "tok"), None),
        P(("parts", "tok"), None),
        P(None, ("parts", "tok")),
        P(None, "tok", None),
        P(None, "tok", None),
    )
    return jax.shard_map(
        per_device,
        mesh=mesh,
        in_specs=placed,
        out_specs=(P(("parts", "tok"), None), P("parts", "tok", None), P("parts", "tok", None)),
        check_vma=False,
    )
```

```python
import functools
import math

import jax
import jax.numpy as jnp
from jax import lax
from jax.experimental import pallas as pl
from jax.experimental.pallas import tpu as pltpu
from jax.sharding import PartitionSpec as P

BF16 = jnp.bfloat16
F32 = jnp.float32
VMEM_LIMIT = 32 * 1024 * 1024


def rms_rows(matrix):
    return matrix * lax.rsqrt(jnp.mean(matrix * matrix, axis=-1, keepdims=True) + 1e-06)


def normalized_heads(tokens, heads, head_size):
    row_count = tokens.shape[0]
    wide = tokens.astype(jnp.float32).reshape(row_count, heads, head_size)
    return rms_rows(wide).astype(jnp.bfloat16)


def head_increments(key_rows, value_rows, rates, weight_in, weight_out, block_root):
    fast = weight_out.shape[0]
    in_root = 1.0 / math.sqrt(weight_in.shape[0])
    out_root = 1.0 / math.sqrt(fast)
    scaled = (rates[:, None] * block_root * value_rows.astype(jnp.float32)).astype(jnp.bfloat16)
    pre = jnp.dot(key_rows, weight_in, preferred_element_type=jnp.float32) * in_root
    gate = pre[:, :fast]
    upper = pre[:, fast:]
    sigma = jax.nn.sigmoid(gate)
    active = gate * sigma
    hidden = (active * upper).astype(jnp.bfloat16)
    back = (
        lax.dot_general(
            scaled, weight_out, (((1,), (1,)), ((), ())), preferred_element_type=jnp.float32
        )
        * out_root
    )
    d_gate = (back * upper * sigma * (1.0 + gate * (1.0 - sigma))).astype(jnp.bfloat16)
    d_up = (back * active).astype(jnp.bfloat16)
    joined = jnp.concatenate([d_gate, d_up], axis=1)
    inc_in = (
        lax.dot_general(
            key_rows, joined, (((0,), (0,)), ((), ())), preferred_element_type=jnp.float32
        )
        * in_root
    )
    inc_out = (
        lax.dot_general(
            hidden, scaled, (((0,), (0,)), ((), ())), preferred_element_type=jnp.float32
        )
        * out_root
    )
    return (inc_in, inc_out)


def local_increments(keyn, values, step_size, weight_in, weight_out, block_root):
    heads = weight_in.shape[0]
    head_size = weight_in.shape[1]
    list_in = []
    list_out = []
    for head_number in range(heads):
        value_rows = values[:, head_number * head_size : (head_number + 1) * head_size]
        part_in, part_out = head_increments(
            keyn[:, head_number, :],
            value_rows,
            step_size[head_number],
            weight_in[head_number],
            weight_out[head_number],
            block_root,
        )
        list_in.append(part_in)
        list_out.append(part_out)
    return (jnp.stack(list_in), jnp.stack(list_out))


def renorm_in(matrix):
    heads, rows_here, double = matrix.shape
    split = matrix.reshape(heads, rows_here, 2, double // 2)
    return rms_rows(split).reshape(heads, rows_here, double)


def apply_head(query_rows, weight_in, weight_out):
    fast = weight_out.shape[0]
    pre = jnp.dot(query_rows, weight_in, preferred_element_type=jnp.float32) * (
        1.0 / math.sqrt(weight_in.shape[0])
    )
    gate = pre[:, :fast]
    hidden = (gate * jax.nn.sigmoid(gate) * pre[:, fast:]).astype(jnp.bfloat16)
    return jnp.dot(hidden, weight_out, preferred_element_type=jnp.float32) * (1.0 / math.sqrt(fast))


def apply_all(queryn, next_in, next_out):
    heads = next_in.shape[0]
    pieces = []
    for head_number in range(heads):
        pieces.append(
            apply_head(queryn[:, head_number, :], next_in[head_number], next_out[head_number])
        )
    return jnp.concatenate(pieces, axis=1).astype(jnp.bfloat16)


def per_device_generic(queries, keys, values, step_size, fast_in, fast_out):
    row_count = keys.shape[0]
    heads = fast_in.shape[0]
    head_size = keys.shape[1] // heads
    block_root = 1.0 / math.sqrt(row_count * lax.axis_size("tok"))
    keyn = normalized_heads(keys, heads, head_size)
    queryn = normalized_heads(queries, heads, head_size)
    master_in, master_out = (
        lax.all_gather(fast_in, "tok", axis=1, tiled=True),
        lax.all_gather(fast_out, "tok", axis=1, tiled=True),
    )
    inc_in, inc_out = local_increments(
        keyn,
        values,
        step_size,
        master_in.astype(jnp.bfloat16),
        master_out.astype(jnp.bfloat16),
        block_root,
    )
    total_in, total_out = lax.psum((inc_in, inc_out), "tok")
    whole_in = renorm_in(master_in + total_in)
    whole_out = rms_rows(master_out + total_out)
    output = apply_all(queryn, whole_in.astype(jnp.bfloat16), whole_out.astype(jnp.bfloat16))
    place = lax.axis_index("tok")
    fast_in_next = lax.dynamic_slice_in_dim(whole_in, place * fast_in.shape[1], fast_in.shape[1], 1)
    fast_out_next = lax.dynamic_slice_in_dim(
        whole_out, place * fast_out.shape[1], fast_out.shape[1], 1
    )
    return (output, fast_in_next, fast_out_next)


def swap(value, bits):
    count = lax.axis_size("tok")
    return lax.ppermute(value, "tok", [(place, place ^ bits) for place in range(count)])


def swap_parts(value):
    return lax.ppermute(value, "parts", [(0, 1), (1, 0)])


def after(value, *before):
    return lax.optimization_barrier((value, before))[0]


def compiler_params():
    return pltpu.CompilerParams(vmem_limit_bytes=VMEM_LIMIT)


def head_of(ids, order, other):
    return 2 * jnp.bitwise_xor(ids[1], other) + jnp.bitwise_xor(ids[2], order)


def normalize_head(block):
    wide = block.astype(F32)
    return (wide * lax.rsqrt(jnp.mean(wide * wide, axis=-1, keepdims=True) + 1e-06)).astype(BF16)


def pack_kernel(ids, in_hbm, out_hbm, own, theirs, in_ref, out_ref, arrived):
    copies = [
        pltpu.make_async_copy(in_hbm, in_ref, arrived.at[0]),
        pltpu.make_async_copy(out_hbm, out_ref, arrived.at[1]),
    ]
    for copy in copies:
        copy.start()
    for copy in copies:
        copy.wait()
    size = out_ref.shape[-1]
    rows = in_ref.shape[1]
    for other, ref in ((0, own), (1, theirs)):
        for order in range(2):
            head = head_of(ids, order, other)
            for block in range(in_ref.shape[2] // size):
                ref[order, block * rows : (block + 1) * rows, :] = in_ref[
                    head, :, block * size : (block + 1) * size
                ]
            ref[order, -out_ref.shape[1] :, :] = out_ref[head]


def pack(ids, fast_in, fast_out):
    rows = 4 * fast_in.shape[1] + fast_out.shape[1]
    shape = jax.ShapeDtypeStruct((2, rows, fast_out.shape[2]), F32)
    return pl.pallas_call(
        pack_kernel,
        in_specs=[pl.BlockSpec(memory_space=pltpu.SMEM)] + [pl.BlockSpec(memory_space=pltpu.HBM)] * 2,
        out_shape=[shape, shape],
        scratch_shapes=[
            pltpu.VMEM(fast_in.shape, F32),
            pltpu.VMEM(fast_out.shape, F32),
            pltpu.SemaphoreType.DMA((2,)),
        ],
        compiler_params=compiler_params(),
        name="pack",
    )(ids, fast_in, fast_out)


def pair_kernel(own, got, master_one, master_two, shard):
    for source, ref in enumerate((own, got)):
        for order, master in enumerate((master_one, master_two)):
            master[source] = ref[order]
        shard[source] = ref[0].astype(BF16)


def pair(own, got):
    wide = jax.ShapeDtypeStruct(own.shape, F32)
    return pl.pallas_call(
        pair_kernel,
        out_shape=[wide, wide, jax.ShapeDtypeStruct(own.shape, BF16)],
        compiler_params=compiler_params(),
        name="pair",
    )(own, got)


def prepare_kernel(heads, block_root, ids, x_ref, *rest):
    own, send = rest[-2:]
    core = ids[1]
    half = heads // 2
    size = x_ref.shape[1] // heads

    if len(rest) == 3:
        rates = rest[0][...]
        columns_of = jnp.concatenate([rates, rates], axis=0).T

    def work(owner, out):
        for local in range(half):
            columns = pl.ds(pl.multiple_of((owner * half + local) * size, size), size)
            into = slice(local * size, (local + 1) * size)
            if len(rest) == 2:
                out[:, into] = normalize_head(x_ref[:, columns])
            else:
                first = columns_of[:, local : local + 1]
                second = columns_of[:, half + local : half + local + 1]
                rate = jnp.where(owner == 0, first, second) * block_root
                out[:, into] = (rate * x_ref[:, columns].astype(F32)).astype(BF16)

    work(core, own)
    work(1 - core, send)


def prepare(ids, tokens, rates, heads, block_root, name):
    rows, width = tokens.shape
    step = 256
    wide = pl.BlockSpec((step, width), lambda i, ids: (i, 0))
    narrow = pl.BlockSpec((step, width // 2), lambda i, ids: (i, 0))
    operands, specs = [tokens], [wide]
    if rates is not None:
        operands.append(rates)
        specs.append(pl.BlockSpec((heads, step), lambda i, ids: (0, i)))
    shape = jax.ShapeDtypeStruct((rows, width // 2), BF16)
    return pl.pallas_call(
        functools.partial(prepare_kernel, heads, block_root),
        grid_spec=pltpu.PrefetchScalarGridSpec(
            num_scalar_prefetch=1,
            grid=(rows // step,),
            in_specs=specs,
            out_specs=[narrow] * 2,
        ),
        out_shape=[shape] * 2,
        compiler_params=compiler_params(),
        cost_estimate=pl.CostEstimate(
            flops=rows * width * 5, bytes_accessed=rows * width * 4, transcendentals=0
        ),
        name=name,
    )(ids, *operands)


def places(chip, core):
    for side in range(2):
        for slot in range(4):
            other = jnp.bitwise_xor(chip, 2 * slot + side)
            for source in range(2):
                yield side, slot, source, 2 * other + jnp.bitwise_xor(core, source)


def assemble(chip, core, lines, w_in, w_out):
    size = w_out.shape[1]
    blocks = w_in.shape[1] // size
    rows_in = w_in.shape[0] // 16
    rows_out = w_out.shape[0] // 16
    for side, slot, source, place in places(chip, core):
        ref = lines[2 * side + slot // 2].at[slot % 2]
        into = pl.ds(pl.multiple_of(place * rows_in, rows_in), rows_in)
        for block in range(blocks):
            w_in[into, block * size : (block + 1) * size] = ref[
                source, block * rows_in : (block + 1) * rows_in, :
            ]
        into = pl.ds(pl.multiple_of(place * rows_out, rows_out), rows_out)
        w_out[into, :] = ref[source, blocks * rows_in :, :]


def increments_kernel(
    ids, near_low, near_high, far_low, far_high, k_own, v_own, k_got, v_got,
    kept, low, high, w_in, w_out, acc_in, acc_out, turned,
):
    step = pl.program_id(0)
    steps = pl.num_programs(0)
    chip, core = ids[0], ids[1]
    size = w_out.shape[1]
    fast = w_out.shape[0]
    in_root = 1.0 / math.sqrt(size)
    out_root = 1.0 / math.sqrt(fast)

    @pl.when(step == 0)
    def _():
        assemble(chip, core, (near_low, near_high, far_low, far_high), w_in, w_out)

    def work(k_ref, v_ref, start_over):
        keyn = k_ref[...]
        scaled = v_ref[...]
        keyn_t = keyn.T
        scaled_t = scaled.T

        def add(ref, columns, value):
            if start_over:
                ref[:, columns] = value
            else:
                ref[:, columns] += value

        chunk = 256
        for start in range(0, fast, chunk):
            gates = slice(start, start + chunk)
            ups = slice(fast + start, fast + start + chunk)
            gate = jnp.dot(keyn, w_in[:, gates], preferred_element_type=F32) * in_root
            upper = jnp.dot(keyn, w_in[:, ups], preferred_element_type=F32) * in_root
            back = (
                lax.dot_general(
                    scaled, w_out[gates, :], (((1,), (1,)), ((), ())), preferred_element_type=F32
                )
                * out_root
            )
            sigma = 0.5 * jnp.tanh(0.5 * gate) + 0.5
            active = gate * sigma
            hidden = (active * upper).astype(BF16)
            d_gate = (back * upper * (sigma + active * (1.0 - sigma))).astype(BF16)
            d_up = (back * active).astype(BF16)
            add(acc_in, gates, jnp.dot(keyn_t, d_gate, preferred_element_type=F32))
            add(acc_in, ups, jnp.dot(keyn_t, d_up, preferred_element_type=F32))
            add(acc_out, gates, jnp.dot(scaled_t, hidden, preferred_element_type=F32))

    @pl.when(step == 0)
    def _():
        work(k_own, v_own, True)

    if k_own.shape[0] * 2 < 2048:

        @pl.when((step > 0) & (step < steps // 2))
        def _():
            work(k_own, v_own, False)

    @pl.when(step >= steps // 2)
    def _():
        work(k_got, v_got, False)

    @pl.when(step == steps - 1)
    def _():
        turned[...] = acc_out[...].T
        blocks = acc_in.shape[1] // size
        rows_in = acc_in.shape[0] // 16
        rows_out = turned.shape[0] // 16
        for side, slot, source, place in places(chip, core):
            ref = kept.at[slot] if side == 0 else (low, high)[slot // 2].at[slot % 2]
            rows = pl.ds(pl.multiple_of(place * rows_in, rows_in), rows_in)
            for block in range(blocks):
                ref[source, block * rows_in : (block + 1) * rows_in, :] = (
                    acc_in[rows, block * size : (block + 1) * size] * in_root
                ).astype(ref.dtype)
            rows = pl.ds(pl.multiple_of(place * rows_out, rows_out), rows_out)
            ref[source, blocks * rows_in :, :] = (turned[rows, :] * out_root).astype(ref.dtype)


def increments(ids, order, lines, k_own, v_own, k_got, v_got, fast):
    rows = k_own.shape[0]
    pair_shape = lines[0].shape
    size = pair_shape[-1]
    step = rows
    half = rows // step
    whole = pl.BlockSpec(pair_shape, lambda i, ids: (0, 0, 0, 0))
    line_shape = (4,) + pair_shape[1:]
    line = pl.BlockSpec(line_shape, lambda i, ids: (0, 0, 0, 0))
    own = pl.BlockSpec((step, size), lambda i, ids: (jnp.minimum(i, half - 1), ids[2] ^ order))
    got = pl.BlockSpec((step, size), lambda i, ids: (jnp.maximum(i - half, 0), ids[2] ^ order))
    return pl.pallas_call(
        increments_kernel,
        grid_spec=pltpu.PrefetchScalarGridSpec(
            num_scalar_prefetch=1,
            grid=(2 * half,),
            in_specs=[whole] * 4 + [own, own, got, got],
            out_specs=[line, whole, whole],
            scratch_shapes=[
                pltpu.VMEM((size, 2 * fast), BF16),
                pltpu.VMEM((fast, size), BF16),
                pltpu.VMEM((size, 2 * fast), F32),
                pltpu.VMEM((size, fast), F32),
                pltpu.VMEM((fast, size), F32),
            ],
        ),
        out_shape=[
            jax.ShapeDtypeStruct(line_shape, F32),
            jax.ShapeDtypeStruct(pair_shape, BF16),
            jax.ShapeDtypeStruct(pair_shape, BF16),
        ],
        compiler_params=compiler_params(),
        cost_estimate=pl.CostEstimate(
            flops=2 * rows * size * fast * 12, bytes_accessed=rows * size * 8, transcendentals=0
        ),
        name="increments",
    )(ids, *lines, k_own, v_own, k_got, v_got)


def add_kernel(kept, came, first, second):
    first[...] = (kept[0] + came[0].astype(F32)).astype(first.dtype)
    second[...] = (kept[1] + came[1].astype(F32)).astype(second.dtype)


def add_pair(kept, came, which, first_type):
    shape = came.shape
    flat = (0,) * (len(shape) - 1)
    return pl.pallas_call(
        add_kernel,
        grid=(1,),
        in_specs=[
            pl.BlockSpec(shape, lambda i: (which,) + flat),
            pl.BlockSpec(shape, lambda i: (0,) + flat),
        ],
        out_specs=[pl.BlockSpec(shape[1:], lambda i: flat)] * 2,
        out_shape=[
            jax.ShapeDtypeStruct(shape[1:], first_type),
            jax.ShapeDtypeStruct(shape[1:], BF16),
        ],
        compiler_params=compiler_params(),
        name="add_pair",
    )(kept, came)


def renorm_kernel(rows_in, master, kept, one, two, three, wide, short):
    size = master.shape[-1]
    for source in range(2):
        fresh = (
            master[source]
            + kept[source]
            + one[source].astype(F32)
            + two[source].astype(F32)
            + three[source].astype(F32)
        )
        for part in range(2):
            first = 2 * part * rows_in
            left = fresh[first : first + rows_in, :]
            right = fresh[first + rows_in : first + 2 * rows_in, :]
            total = jnp.sum(left * left + right * right, axis=-1, keepdims=True)
            factor = lax.rsqrt(total * (1.0 / (2 * size)) + 1e-06)
            for at, value in ((first, left), (first + rows_in, right)):
                done = value * factor
                wide[source, at : at + rows_in, :] = done
                short[source, at : at + rows_in, :] = done.astype(BF16)
        tail = fresh[4 * rows_in :, :]
        done = tail * lax.rsqrt(jnp.mean(tail * tail, axis=-1, keepdims=True) + 1e-06)
        wide[source, 4 * rows_in :, :] = done
        short[source, 4 * rows_in :, :] = done.astype(BF16)


def renorm(master, kept, one, two, three, rows_in):
    shape = master.shape
    return pl.pallas_call(
        functools.partial(renorm_kernel, rows_in),
        out_shape=[jax.ShapeDtypeStruct(shape, F32), jax.ShapeDtypeStruct(shape, BF16)],
        compiler_params=compiler_params(),
        name="renorm",
    )(master, kept, one, two, three)


def apply_kernel(order, other, ids, near_low, near_high, far_low, far_high, q_ref, *rest):
    o_ref, w_in, w_out = rest[-3:]
    chip, core = ids[0], ids[1]
    fast, size = w_out.shape
    lines = (near_low, near_high, far_low, far_high)
    assemble(chip, jnp.bitwise_xor(core, other), lines, w_in, w_out)
    columns = pl.ds(pl.multiple_of(head_of(ids, order, other) * size, size), size)
    in_root = 1.0 / math.sqrt(size)
    out_root = 1.0 / math.sqrt(fast)
    step = 512
    for start in range(0, q_ref.shape[0], step):
        rows = slice(start, start + step)
        query = normalize_head(q_ref[rows, columns])
        gate = jnp.dot(query, w_in[:, :fast], preferred_element_type=F32) * in_root
        upper = jnp.dot(query, w_in[:, fast:], preferred_element_type=F32) * in_root
        hidden = (gate * (0.5 * jnp.tanh(0.5 * gate) + 0.5) * upper).astype(BF16)
        result = jnp.dot(hidden, w_out[...], preferred_element_type=F32) * out_root
        o_ref[rows, :] = result.astype(BF16)


def apply_fast(ids, order, other, lines, queries, output, fast):
    rows, width = queries.shape
    size = lines[0].shape[-1]
    inside = pl.BlockSpec(memory_space=pltpu.VMEM)
    operands = [ids, *lines, queries]
    specs = [inside] * 5
    aliases = {}
    if output is not None:
        operands.append(output)
        specs.append(pl.BlockSpec(memory_space=pl.ANY))
        aliases = {6: 0}
    return pl.pallas_call(
        functools.partial(apply_kernel, order, other),
        grid_spec=pltpu.PrefetchScalarGridSpec(
            num_scalar_prefetch=1,
            grid=(1,),
            in_specs=specs,
            out_specs=pl.BlockSpec((rows, size), lambda i, ids: (0, head_of(ids, order, other))),
            scratch_shapes=[pltpu.VMEM((size, 2 * fast), BF16), pltpu.VMEM((fast, size), BF16)],
        ),
        out_shape=jax.ShapeDtypeStruct((rows, width), BF16),
        input_output_aliases=aliases,
        compiler_params=compiler_params(),
        cost_estimate=pl.CostEstimate(
            flops=2 * rows * size * fast * 3, bytes_accessed=rows * size * 4, transcendentals=0
        ),
        name="apply",
    )(*operands)


def finish_kernel(rows_in, ids, one, two, came, in_next, out_next):
    size = out_next.shape[-1]
    for order, mine in enumerate((one, two)):
        for other, ref in ((0, mine.at[0]), (1, came.at[order])):
            head = head_of(ids, order, other)
            for block in range(4):
                in_next[head, :, block * size : (block + 1) * size] = ref[
                    block * rows_in : (block + 1) * rows_in, :
                ]
            out_next[head] = ref[4 * rows_in :, :]


def finish(ids, one, two, came, fast_in, fast_out):
    return pl.pallas_call(
        functools.partial(finish_kernel, fast_in.shape[1]),
        in_specs=[pl.BlockSpec(memory_space=pltpu.SMEM)] + [pl.BlockSpec(memory_space=pltpu.VMEM)] * 3,
        out_shape=[
            jax.ShapeDtypeStruct(fast_in.shape, F32),
            jax.ShapeDtypeStruct(fast_out.shape, F32),
        ],
        compiler_params=compiler_params(),
        name="finish",
    )(ids, one, two, came)


def per_device_cube(queries, keys, values, step_size, fast_in, fast_out):
    rows = keys.shape[0]
    heads = fast_in.shape[0]
    fast = fast_in.shape[2] // 2
    rows_in = fast_in.shape[1]
    place = lax.axis_index("tok")
    ids = jnp.stack([place // 2, place % 2, lax.axis_index("parts")]).astype(jnp.int32)
    block_root = 1.0 / math.sqrt(rows * lax.axis_size("tok"))

    own, theirs = pack(ids, fast_in, fast_out)
    got = swap(theirs, 1)
    later = after(ids, got)
    k_own, k_send = prepare(later, keys, None, heads, None, "keys")
    v_own, v_send = prepare(later, values, step_size, heads, block_root, "values")
    master_one, master_two, shard = pair(own, after(got, k_send, v_send))
    masters = (master_one, master_two)
    k_got, v_got = swap(k_send, 1), swap(v_send, 1)
    z1, z3, z2 = swap(shard, 4), swap(shard, 12), swap(shard, 8)
    near_low = after(jnp.stack([shard, z1]), k_got, v_got)
    far_low, other_near_low = swap(near_low, 2), swap_parts(near_low)
    near_high = after(jnp.stack([z2, z3]), far_low, other_near_low)
    far_high = swap(near_high, 2)
    first = (near_low, near_high, far_low, far_high)
    second = (other_near_low, *(swap_parts(piece) for piece in first[1:]))

    wide, short = [], []
    for order in range(2):
        lines = second if order else first
        later = ids if order else after(ids, second[2])
        kept, low, high = increments(later, order, lines, k_own, v_own, k_got, v_got, fast)
        high, low = swap(high, 2), swap(low, 2)
        sum2, sum3 = add_pair(kept, high, 1, BF16)
        sum0, sum1 = add_pair(kept, low, 0, F32)
        three, two, one = swap(sum3, 12), swap(sum2, 8), swap(sum1, 4)
        a, b = renorm(masters[order], sum0, one, two, three, rows_in)
        wide.append(a)
        short.append(b)

    z1, z3, z2 = swap(short[0], 4), swap(short[0], 12), swap(short[0], 8)
    near_low, near_high = jnp.stack([short[0], z1]), jnp.stack([z2, z3])
    far_low, far_high = swap(near_low, 2), swap(near_high, 2)
    second = after(short[1], near_low)
    z1 = swap(second, 4)
    second_low = after(jnp.stack([second, z1]), near_high)
    later = after(short[1], second_low)
    z3, z2 = swap(later, 12), swap(later, 8)
    second_high = jnp.stack([z2, z3])
    mine = (near_low, near_high, far_low, far_high)
    others = tuple(swap(piece, 1) for piece in mine)
    output = apply_fast(ids, 0, 0, mine, queries, None, fast)
    came = swap(jnp.stack([wide[0][1], wide[1][1]]), 1)
    updated = finish(ids, wide[0], wide[1], came, fast_in, fast_out)
    near_low, near_high = second_low, after(second_high, *updated)
    output = apply_fast(ids, 0, 1, others, queries, output, fast)
    far_low, far_high = swap(near_low, 2), swap(near_high, 2)
    far_high = after(far_high, output)
    mine = (near_low, near_high, far_low, far_high)
    others = tuple(swap(piece, 1) for piece in mine)
    output = apply_fast(ids, 1, 0, mine, queries, output, fast)
    output = apply_fast(ids, 1, 1, others, queries, output, fast)

    return (output, *updated)


def per_device(queries, keys, values, step_size, fast_in, fast_out):
    fits = (
        lax.axis_size("tok") == 16
        and lax.axis_size("parts") == 2
        and fast_in.shape[0] == 4
        and fast_in.shape[1] % 16 == 0
    )
    chosen = per_device_cube if fits else per_device_generic
    return chosen(queries, keys, values, step_size, fast_in, fast_out)


def solution(mesh):
    placed = (
        P(("parts", "tok"), None),
        P(("parts", "tok"), None),
        P(("parts", "tok"), None),
        P(None, ("parts", "tok")),
        P(None, "tok", None),
        P(None, "tok", None),
    )
    return jax.shard_map(
        per_device,
        mesh=mesh,
        in_specs=placed,
        out_specs=(P(("parts", "tok"), None), P("parts", "tok", None), P("parts", "tok", None)),
        check_vma=False,
    )
```

```python
import functools
import math

import jax
import jax.numpy as jnp
from jax import lax
from jax.experimental import pallas as pl
from jax.experimental.pallas import tpu as pltpu
from jax.sharding import PartitionSpec as P

BF16 = jnp.bfloat16
F32 = jnp.float32
VMEM_LIMIT = 32 * 1024 * 1024


def rms_rows(matrix):
    return matrix * lax.rsqrt(jnp.mean(matrix * matrix, axis=-1, keepdims=True) + 1e-06)


def normalized_heads(tokens, heads, head_size):
    row_count = tokens.shape[0]
    wide = tokens.astype(jnp.float32).reshape(row_count, heads, head_size)
    return rms_rows(wide).astype(jnp.bfloat16)


def head_increments(key_rows, value_rows, rates, weight_in, weight_out, block_root):
    fast = weight_out.shape[0]
    in_root = 1.0 / math.sqrt(weight_in.shape[0])
    out_root = 1.0 / math.sqrt(fast)
    scaled = (rates[:, None] * block_root * value_rows.astype(jnp.float32)).astype(jnp.bfloat16)
    pre = jnp.dot(key_rows, weight_in, preferred_element_type=jnp.float32) * in_root
    gate = pre[:, :fast]
    upper = pre[:, fast:]
    sigma = jax.nn.sigmoid(gate)
    active = gate * sigma
    hidden = (active * upper).astype(jnp.bfloat16)
    back = (
        lax.dot_general(
            scaled, weight_out, (((1,), (1,)), ((), ())), preferred_element_type=jnp.float32
        )
        * out_root
    )
    d_gate = (back * upper * sigma * (1.0 + gate * (1.0 - sigma))).astype(jnp.bfloat16)
    d_up = (back * active).astype(jnp.bfloat16)
    joined = jnp.concatenate([d_gate, d_up], axis=1)
    inc_in = (
        lax.dot_general(
            key_rows, joined, (((0,), (0,)), ((), ())), preferred_element_type=jnp.float32
        )
        * in_root
    )
    inc_out = (
        lax.dot_general(
            hidden, scaled, (((0,), (0,)), ((), ())), preferred_element_type=jnp.float32
        )
        * out_root
    )
    return (inc_in, inc_out)


def local_increments(keyn, values, step_size, weight_in, weight_out, block_root):
    heads = weight_in.shape[0]
    head_size = weight_in.shape[1]
    list_in = []
    list_out = []
    for head_number in range(heads):
        value_rows = values[:, head_number * head_size : (head_number + 1) * head_size]
        part_in, part_out = head_increments(
            keyn[:, head_number, :],
            value_rows,
            step_size[head_number],
            weight_in[head_number],
            weight_out[head_number],
            block_root,
        )
        list_in.append(part_in)
        list_out.append(part_out)
    return (jnp.stack(list_in), jnp.stack(list_out))


def renorm_in(matrix):
    heads, rows_here, double = matrix.shape
    split = matrix.reshape(heads, rows_here, 2, double // 2)
    return rms_rows(split).reshape(heads, rows_here, double)


def apply_head(query_rows, weight_in, weight_out):
    fast = weight_out.shape[0]
    pre = jnp.dot(query_rows, weight_in, preferred_element_type=jnp.float32) * (
        1.0 / math.sqrt(weight_in.shape[0])
    )
    gate = pre[:, :fast]
    hidden = (gate * jax.nn.sigmoid(gate) * pre[:, fast:]).astype(jnp.bfloat16)
    return jnp.dot(hidden, weight_out, preferred_element_type=jnp.float32) * (1.0 / math.sqrt(fast))


def apply_all(queryn, next_in, next_out):
    heads = next_in.shape[0]
    pieces = []
    for head_number in range(heads):
        pieces.append(
            apply_head(queryn[:, head_number, :], next_in[head_number], next_out[head_number])
        )
    return jnp.concatenate(pieces, axis=1).astype(jnp.bfloat16)


def per_device_generic(queries, keys, values, step_size, fast_in, fast_out):
    row_count = keys.shape[0]
    heads = fast_in.shape[0]
    head_size = keys.shape[1] // heads
    block_root = 1.0 / math.sqrt(row_count * lax.axis_size("tok"))
    keyn = normalized_heads(keys, heads, head_size)
    queryn = normalized_heads(queries, heads, head_size)
    master_in, master_out = (
        lax.all_gather(fast_in, "tok", axis=1, tiled=True),
        lax.all_gather(fast_out, "tok", axis=1, tiled=True),
    )
    inc_in, inc_out = local_increments(
        keyn,
        values,
        step_size,
        master_in.astype(jnp.bfloat16),
        master_out.astype(jnp.bfloat16),
        block_root,
    )
    total_in, total_out = lax.psum((inc_in, inc_out), "tok")
    whole_in = renorm_in(master_in + total_in)
    whole_out = rms_rows(master_out + total_out)
    output = apply_all(queryn, whole_in.astype(jnp.bfloat16), whole_out.astype(jnp.bfloat16))
    place = lax.axis_index("tok")
    fast_in_next = lax.dynamic_slice_in_dim(whole_in, place * fast_in.shape[1], fast_in.shape[1], 1)
    fast_out_next = lax.dynamic_slice_in_dim(
        whole_out, place * fast_out.shape[1], fast_out.shape[1], 1
    )
    return (output, fast_in_next, fast_out_next)


def swap(value, bits):
    count = lax.axis_size("tok")
    return lax.ppermute(value, "tok", [(place, place ^ bits) for place in range(count)])


def swap_parts(value):
    return lax.ppermute(value, "parts", [(0, 1), (1, 0)])


def after(value, *before):
    return lax.optimization_barrier((value, before))[0]


def compiler_params():
    return pltpu.CompilerParams(vmem_limit_bytes=VMEM_LIMIT)


def head_of(ids, order, other):
    return 2 * jnp.bitwise_xor(ids[1], other) + jnp.bitwise_xor(ids[2], order)


def normalize_head(block):
    wide = block.astype(F32)
    return (wide * lax.rsqrt(jnp.mean(wide * wide, axis=-1, keepdims=True) + 1e-06)).astype(BF16)


def pack_kernel(ids, in_hbm, out_hbm, own, theirs, in_ref, out_ref, arrived):
    copies = [
        pltpu.make_async_copy(in_hbm, in_ref, arrived.at[0]),
        pltpu.make_async_copy(out_hbm, out_ref, arrived.at[1]),
    ]
    for copy in copies:
        copy.start()
    for copy in copies:
        copy.wait()
    size = out_ref.shape[-1]
    rows = in_ref.shape[1]
    for other, ref in ((0, own), (1, theirs)):
        for order in range(2):
            head = head_of(ids, order, other)
            for block in range(in_ref.shape[2] // size):
                ref[order, block * rows : (block + 1) * rows, :] = in_ref[
                    head, :, block * size : (block + 1) * size
                ]
            ref[order, -out_ref.shape[1] :, :] = out_ref[head]


def pack(ids, fast_in, fast_out):
    rows = 4 * fast_in.shape[1] + fast_out.shape[1]
    shape = jax.ShapeDtypeStruct((2, rows, fast_out.shape[2]), F32)
    return pl.pallas_call(
        pack_kernel,
        in_specs=[pl.BlockSpec(memory_space=pltpu.SMEM)] + [pl.BlockSpec(memory_space=pltpu.HBM)] * 2,
        out_shape=[shape, shape],
        scratch_shapes=[
            pltpu.VMEM(fast_in.shape, F32),
            pltpu.VMEM(fast_out.shape, F32),
            pltpu.SemaphoreType.DMA((2,)),
        ],
        compiler_params=compiler_params(),
        name="pack",
    )(ids, fast_in, fast_out)


def pair_kernel(own, got, master_one, master_two, shard):
    for source, ref in enumerate((own, got)):
        for order, master in enumerate((master_one, master_two)):
            master[source] = ref[order]
        shard[source] = ref[0].astype(BF16)


def pair(own, got):
    wide = jax.ShapeDtypeStruct(own.shape, F32)
    return pl.pallas_call(
        pair_kernel,
        out_shape=[wide, wide, jax.ShapeDtypeStruct(own.shape, BF16)],
        compiler_params=compiler_params(),
        name="pair",
    )(own, got)


def prepare_kernel(heads, block_root, ids, x_ref, *rest):
    own, send = rest[-2:]
    core = ids[1]
    half = heads // 2
    size = x_ref.shape[1] // heads

    if len(rest) == 3:
        rates = rest[0][...]
        columns_of = jnp.concatenate([rates, rates], axis=0).T

    def work(owner, out):
        for local in range(half):
            columns = pl.ds(pl.multiple_of((owner * half + local) * size, size), size)
            into = slice(local * size, (local + 1) * size)
            if len(rest) == 2:
                out[:, into] = normalize_head(x_ref[:, columns])
            else:
                first = columns_of[:, local : local + 1]
                second = columns_of[:, half + local : half + local + 1]
                rate = jnp.where(owner == 0, first, second) * block_root
                out[:, into] = (rate * x_ref[:, columns].astype(F32)).astype(BF16)

    work(core, own)
    work(1 - core, send)


def prepare(ids, tokens, rates, heads, block_root, name):
    rows, width = tokens.shape
    step = 256
    wide = pl.BlockSpec((step, width), lambda i, ids: (i, 0))
    narrow = pl.BlockSpec((step, width // 2), lambda i, ids: (i, 0))
    operands, specs = [tokens], [wide]
    if rates is not None:
        operands.append(rates)
        specs.append(pl.BlockSpec((heads, step), lambda i, ids: (0, i)))
    shape = jax.ShapeDtypeStruct((rows, width // 2), BF16)
    return pl.pallas_call(
        functools.partial(prepare_kernel, heads, block_root),
        grid_spec=pltpu.PrefetchScalarGridSpec(
            num_scalar_prefetch=1,
            grid=(rows // step,),
            in_specs=specs,
            out_specs=[narrow] * 2,
        ),
        out_shape=[shape] * 2,
        compiler_params=compiler_params(),
        cost_estimate=pl.CostEstimate(
            flops=rows * width * 5, bytes_accessed=rows * width * 4, transcendentals=0
        ),
        name=name,
    )(ids, *operands)


def places(chip, core):
    for side in range(2):
        for slot in range(4):
            other = jnp.bitwise_xor(chip, 2 * slot + side)
            for source in range(2):
                yield side, slot, source, 2 * other + jnp.bitwise_xor(core, source)


def assemble(chip, core, lines, w_in, w_out):
    size = w_out.shape[1]
    blocks = w_in.shape[1] // size
    rows_in = w_in.shape[0] // 16
    rows_out = w_out.shape[0] // 16
    for side, slot, source, place in places(chip, core):
        ref = lines[2 * side + slot // 2].at[slot % 2]
        into = pl.ds(pl.multiple_of(place * rows_in, rows_in), rows_in)
        for block in range(blocks):
            w_in[into, block * size : (block + 1) * size] = ref[
                source, block * rows_in : (block + 1) * rows_in, :
            ]
        into = pl.ds(pl.multiple_of(place * rows_out, rows_out), rows_out)
        w_out[into, :] = ref[source, blocks * rows_in :, :]


def increments_kernel(
    ids, near_low, near_high, far_low, far_high, k_own, v_own, k_got, v_got,
    kept, low, high, w_in, w_out, acc_in, acc_out, turned,
):
    step = pl.program_id(0)
    steps = pl.num_programs(0)
    chip, core = ids[0], ids[1]
    size = w_out.shape[1]
    fast = w_out.shape[0]
    in_root = 1.0 / math.sqrt(size)
    out_root = 1.0 / math.sqrt(fast)

    @pl.when(step == 0)
    def _():
        assemble(chip, core, (near_low, near_high, far_low, far_high), w_in, w_out)

    def work(k_ref, v_ref, start_over):
        keyn = k_ref[...]
        scaled = v_ref[...]
        keyn_t = keyn.T
        scaled_t = scaled.T

        def add(ref, columns, value):
            if start_over:
                ref[:, columns] = value
            else:
                ref[:, columns] += value

        chunk = 256
        for start in range(0, fast, chunk):
            gates = slice(start, start + chunk)
            ups = slice(fast + start, fast + start + chunk)
            gate = jnp.dot(keyn, w_in[:, gates], preferred_element_type=F32) * in_root
            upper = jnp.dot(keyn, w_in[:, ups], preferred_element_type=F32) * in_root
            back = (
                lax.dot_general(
                    scaled, w_out[gates, :], (((1,), (1,)), ((), ())), preferred_element_type=F32
                )
                * out_root
            )
            sigma = 0.5 * jnp.tanh(0.5 * gate) + 0.5
            active = gate * sigma
            hidden = (active * upper).astype(BF16)
            d_gate = (back * upper * (sigma + active * (1.0 - sigma))).astype(BF16)
            d_up = (back * active).astype(BF16)
            add(acc_in, gates, jnp.dot(keyn_t, d_gate, preferred_element_type=F32))
            add(acc_in, ups, jnp.dot(keyn_t, d_up, preferred_element_type=F32))
            add(acc_out, gates, jnp.dot(scaled_t, hidden, preferred_element_type=F32))

    @pl.when(step == 0)
    def _():
        work(k_own, v_own, True)

    if k_own.shape[0] * 2 < 2048:

        @pl.when((step > 0) & (step < steps // 2))
        def _():
            work(k_own, v_own, False)

    @pl.when(step >= steps // 2)
    def _():
        work(k_got, v_got, False)

    @pl.when(step == steps - 1)
    def _():
        turned[...] = acc_out[...].T
        blocks = acc_in.shape[1] // size
        rows_in = acc_in.shape[0] // 16
        rows_out = turned.shape[0] // 16
        for side, slot, source, place in places(chip, core):
            ref = kept.at[slot] if side == 0 else (low, high)[slot // 2].at[slot % 2]
            rows = pl.ds(pl.multiple_of(place * rows_in, rows_in), rows_in)
            for block in range(blocks):
                ref[source, block * rows_in : (block + 1) * rows_in, :] = (
                    acc_in[rows, block * size : (block + 1) * size] * in_root
                ).astype(ref.dtype)
            rows = pl.ds(pl.multiple_of(place * rows_out, rows_out), rows_out)
            ref[source, blocks * rows_in :, :] = (turned[rows, :] * out_root).astype(ref.dtype)


def increments(ids, order, lines, k_own, v_own, k_got, v_got, fast):
    rows = k_own.shape[0]
    pair_shape = lines[0].shape
    size = pair_shape[-1]
    step = rows
    half = rows // step
    whole = pl.BlockSpec(pair_shape, lambda i, ids: (0, 0, 0, 0))
    line_shape = (4,) + pair_shape[1:]
    line = pl.BlockSpec(line_shape, lambda i, ids: (0, 0, 0, 0))
    own = pl.BlockSpec((step, size), lambda i, ids: (jnp.minimum(i, half - 1), ids[2] ^ order))
    got = pl.BlockSpec((step, size), lambda i, ids: (jnp.maximum(i - half, 0), ids[2] ^ order))
    return pl.pallas_call(
        increments_kernel,
        grid_spec=pltpu.PrefetchScalarGridSpec(
            num_scalar_prefetch=1,
            grid=(2 * half,),
            in_specs=[whole] * 4 + [own, own, got, got],
            out_specs=[line, whole, whole],
            scratch_shapes=[
                pltpu.VMEM((size, 2 * fast), BF16),
                pltpu.VMEM((fast, size), BF16),
                pltpu.VMEM((size, 2 * fast), F32),
                pltpu.VMEM((size, fast), F32),
                pltpu.VMEM((fast, size), F32),
            ],
        ),
        out_shape=[
            jax.ShapeDtypeStruct(line_shape, F32),
            jax.ShapeDtypeStruct(pair_shape, BF16),
            jax.ShapeDtypeStruct(pair_shape, BF16),
        ],
        compiler_params=compiler_params(),
        cost_estimate=pl.CostEstimate(
            flops=2 * rows * size * fast * 12, bytes_accessed=rows * size * 8, transcendentals=0
        ),
        name="increments",
    )(ids, *lines, k_own, v_own, k_got, v_got)


def add_kernel(kept, came, first, second):
    first[...] = (kept[0] + came[0].astype(F32)).astype(first.dtype)
    second[...] = (kept[1] + came[1].astype(F32)).astype(second.dtype)


def add_pair(kept, came, which, first_type):
    shape = came.shape
    flat = (0,) * (len(shape) - 1)
    return pl.pallas_call(
        add_kernel,
        grid=(1,),
        in_specs=[
            pl.BlockSpec(shape, lambda i: (which,) + flat),
            pl.BlockSpec(shape, lambda i: (0,) + flat),
        ],
        out_specs=[pl.BlockSpec(shape[1:], lambda i: flat)] * 2,
        out_shape=[
            jax.ShapeDtypeStruct(shape[1:], first_type),
            jax.ShapeDtypeStruct(shape[1:], BF16),
        ],
        compiler_params=compiler_params(),
        name="add_pair",
    )(kept, came)


def renorm_kernel(rows_in, master, kept, one, two, three, wide, short):
    size = master.shape[-1]
    for source in range(2):
        fresh = (
            master[source]
            + kept[source]
            + one[source].astype(F32)
            + two[source].astype(F32)
            + three[source].astype(F32)
        )
        for part in range(2):
            first = 2 * part * rows_in
            left = fresh[first : first + rows_in, :]
            right = fresh[first + rows_in : first + 2 * rows_in, :]
            total = jnp.sum(left * left + right * right, axis=-1, keepdims=True)
            factor = lax.rsqrt(total * (1.0 / (2 * size)) + 1e-06)
            for at, value in ((first, left), (first + rows_in, right)):
                done = value * factor
                wide[source, at : at + rows_in, :] = done
                short[source, at : at + rows_in, :] = done.astype(BF16)
        tail = fresh[4 * rows_in :, :]
        done = tail * lax.rsqrt(jnp.mean(tail * tail, axis=-1, keepdims=True) + 1e-06)
        wide[source, 4 * rows_in :, :] = done
        short[source, 4 * rows_in :, :] = done.astype(BF16)


def renorm(master, kept, one, two, three, rows_in):
    shape = master.shape
    return pl.pallas_call(
        functools.partial(renorm_kernel, rows_in),
        out_shape=[jax.ShapeDtypeStruct(shape, F32), jax.ShapeDtypeStruct(shape, BF16)],
        compiler_params=compiler_params(),
        name="renorm",
    )(master, kept, one, two, three)


def apply_kernel(order, other, ids, near_low, near_high, far_low, far_high, q_ref, *rest):
    o_hbm, w_in, w_out, o_ref, sent = rest[-5:]
    chip, core = ids[0], ids[1]
    fast, size = w_out.shape
    lines = (near_low, near_high, far_low, far_high)
    assemble(chip, jnp.bitwise_xor(core, other), lines, w_in, w_out)
    columns = pl.ds(pl.multiple_of(head_of(ids, order, other) * size, size), size)
    in_root = 1.0 / math.sqrt(size)
    out_root = 1.0 / math.sqrt(fast)
    step = 512
    copies = []
    for start in range(0, q_ref.shape[0], step):
        rows = pl.ds(start, step)
        query = normalize_head(q_ref[rows, columns])
        gate = jnp.dot(query, w_in[:, :fast], preferred_element_type=F32) * in_root
        upper = jnp.dot(query, w_in[:, fast:], preferred_element_type=F32) * in_root
        hidden = (gate * (0.5 * jnp.tanh(0.5 * gate) + 0.5) * upper).astype(BF16)
        result = jnp.dot(hidden, w_out[...], preferred_element_type=F32) * out_root
        o_ref[rows, :] = result.astype(BF16)
        at = start // step
        copies.append(
            pltpu.make_async_copy(o_ref.at[rows, :], o_hbm.at[rows, columns], sent.at[at])
        )
        copies[-1].start()
    for copy in copies:
        copy.wait()


def apply_fast(ids, order, other, lines, queries, output, fast):
    rows, width = queries.shape
    size = lines[0].shape[-1]
    inside = pl.BlockSpec(memory_space=pltpu.VMEM)
    operands = [ids, *lines, queries]
    specs = [inside] * 5
    aliases = {}
    if output is not None:
        operands.append(output)
        specs.append(pl.BlockSpec(memory_space=pl.ANY))
        aliases = {6: 0}
    return pl.pallas_call(
        functools.partial(apply_kernel, order, other),
        grid_spec=pltpu.PrefetchScalarGridSpec(
            num_scalar_prefetch=1,
            grid=(1,),
            in_specs=specs,
            out_specs=pl.BlockSpec(memory_space=pl.ANY),
            scratch_shapes=[
                pltpu.VMEM((size, 2 * fast), BF16),
                pltpu.VMEM((fast, size), BF16),
                pltpu.VMEM((rows, size), BF16),
                pltpu.SemaphoreType.DMA((rows // 512,)),
            ],
        ),
        out_shape=jax.ShapeDtypeStruct((rows, width), BF16),
        input_output_aliases=aliases,
        compiler_params=compiler_params(),
        cost_estimate=pl.CostEstimate(
            flops=2 * rows * size * fast * 3, bytes_accessed=rows * size * 4, transcendentals=0
        ),
        name="apply",
    )(*operands)


def finish_kernel(rows_in, ids, one, two, came, in_next, out_next):
    size = out_next.shape[-1]
    for order, mine in enumerate((one, two)):
        for other, ref in ((0, mine.at[0]), (1, came.at[order])):
            head = head_of(ids, order, other)
            for block in range(4):
                in_next[head, :, block * size : (block + 1) * size] = ref[
                    block * rows_in : (block + 1) * rows_in, :
                ]
            out_next[head] = ref[4 * rows_in :, :]


def finish(ids, one, two, came, fast_in, fast_out):
    return pl.pallas_call(
        functools.partial(finish_kernel, fast_in.shape[1]),
        in_specs=[pl.BlockSpec(memory_space=pltpu.SMEM)] + [pl.BlockSpec(memory_space=pltpu.VMEM)] * 3,
        out_shape=[
            jax.ShapeDtypeStruct(fast_in.shape, F32),
            jax.ShapeDtypeStruct(fast_out.shape, F32),
        ],
        compiler_params=compiler_params(),
        name="finish",
    )(ids, one, two, came)


def per_device_cube(queries, keys, values, step_size, fast_in, fast_out):
    rows = keys.shape[0]
    heads = fast_in.shape[0]
    fast = fast_in.shape[2] // 2
    rows_in = fast_in.shape[1]
    place = lax.axis_index("tok")
    ids = jnp.stack([place // 2, place % 2, lax.axis_index("parts")]).astype(jnp.int32)
    block_root = 1.0 / math.sqrt(rows * lax.axis_size("tok"))

    own, theirs = pack(ids, fast_in, fast_out)
    got = swap(theirs, 1)
    later = after(ids, got)
    k_own, k_send = prepare(later, keys, None, heads, None, "keys")
    v_own, v_send = prepare(later, values, step_size, heads, block_root, "values")
    master_one, master_two, shard = pair(own, after(got, k_send, v_send))
    masters = (master_one, master_two)
    k_got, v_got = swap(k_send, 1), swap(v_send, 1)
    z1, z3, z2 = swap(shard, 4), swap(shard, 12), swap(shard, 8)
    near_low = after(jnp.stack([shard, z1]), k_got, v_got)
    far_low, other_near_low = swap(near_low, 2), swap_parts(near_low)
    near_high = after(jnp.stack([z2, z3]), far_low, other_near_low)
    far_high = swap(near_high, 2)
    first = (near_low, near_high, far_low, far_high)
    second = (other_near_low, *(swap_parts(piece) for piece in first[1:]))

    wide, short = [], []
    for order in range(2):
        lines = second if order else first
        later = ids if order else after(ids, second[2])
        kept, low, high = increments(later, order, lines, k_own, v_own, k_got, v_got, fast)
        high, low = swap(high, 2), swap(low, 2)
        sum2, sum3 = add_pair(kept, high, 1, BF16)
        sum0, sum1 = add_pair(kept, low, 0, F32)
        three, two, one = swap(sum3, 12), swap(sum2, 8), swap(sum1, 4)
        a, b = renorm(masters[order], sum0, one, two, three, rows_in)
        wide.append(a)
        short.append(b)

    z1, z3, z2 = swap(short[0], 4), swap(short[0], 12), swap(short[0], 8)
    near_low, near_high = jnp.stack([short[0], z1]), jnp.stack([z2, z3])
    far_low, far_high = swap(near_low, 2), swap(near_high, 2)
    second = after(short[1], near_low)
    z1 = swap(second, 4)
    second_low = after(jnp.stack([second, z1]), near_high)
    later = after(short[1], second_low)
    z3, z2 = swap(later, 12), swap(later, 8)
    second_high = jnp.stack([z2, z3])
    mine = (near_low, near_high, far_low, far_high)
    others = tuple(swap(piece, 1) for piece in mine)
    output = apply_fast(ids, 0, 0, mine, queries, None, fast)
    came = swap(jnp.stack([wide[0][1], wide[1][1]]), 1)
    updated = finish(ids, wide[0], wide[1], came, fast_in, fast_out)
    near_low, near_high = second_low, after(second_high, *updated)
    output = apply_fast(ids, 0, 1, others, queries, output, fast)
    far_low, far_high = swap(near_low, 2), swap(near_high, 2)
    far_high = after(far_high, output)
    mine = (near_low, near_high, far_low, far_high)
    others = tuple(swap(piece, 1) for piece in mine)
    output = apply_fast(ids, 1, 0, mine, queries, output, fast)
    output = apply_fast(ids, 1, 1, others, queries, output, fast)

    return (output, *updated)


def per_device(queries, keys, values, step_size, fast_in, fast_out):
    fits = (
        lax.axis_size("tok") == 16
        and lax.axis_size("parts") == 2
        and fast_in.shape[0] == 4
        and fast_in.shape[1] % 16 == 0
    )
    chosen = per_device_cube if fits else per_device_generic
    return chosen(queries, keys, values, step_size, fast_in, fast_out)


def solution(mesh):
    placed = (
        P(("parts", "tok"), None),
        P(("parts", "tok"), None),
        P(("parts", "tok"), None),
        P(None, ("parts", "tok")),
        P(None, "tok", None),
        P(None, "tok", None),
    )
    return jax.shard_map(
        per_device,
        mesh=mesh,
        in_specs=placed,
        out_specs=(P(("parts", "tok"), None), P("parts", "tok", None), P("parts", "tok", None)),
        check_vma=False,
    )
```

```python
import functools
import math

import jax
import jax.numpy as jnp
from jax import lax
from jax.experimental import pallas as pl
from jax.experimental.pallas import tpu as pltpu
from jax.sharding import PartitionSpec as P

BF16 = jnp.bfloat16
F32 = jnp.float32
VMEM_LIMIT = 32 * 1024 * 1024


def rms_rows(matrix):
    return matrix * lax.rsqrt(jnp.mean(matrix * matrix, axis=-1, keepdims=True) + 1e-06)


def normalized_heads(tokens, heads, head_size):
    row_count = tokens.shape[0]
    wide = tokens.astype(jnp.float32).reshape(row_count, heads, head_size)
    return rms_rows(wide).astype(jnp.bfloat16)


def head_increments(key_rows, value_rows, rates, weight_in, weight_out, block_root):
    fast = weight_out.shape[0]
    in_root = 1.0 / math.sqrt(weight_in.shape[0])
    out_root = 1.0 / math.sqrt(fast)
    scaled = (rates[:, None] * block_root * value_rows.astype(jnp.float32)).astype(jnp.bfloat16)
    pre = jnp.dot(key_rows, weight_in, preferred_element_type=jnp.float32) * in_root
    gate = pre[:, :fast]
    upper = pre[:, fast:]
    sigma = jax.nn.sigmoid(gate)
    active = gate * sigma
    hidden = (active * upper).astype(jnp.bfloat16)
    back = (
        lax.dot_general(
            scaled, weight_out, (((1,), (1,)), ((), ())), preferred_element_type=jnp.float32
        )
        * out_root
    )
    d_gate = (back * upper * sigma * (1.0 + gate * (1.0 - sigma))).astype(jnp.bfloat16)
    d_up = (back * active).astype(jnp.bfloat16)
    joined = jnp.concatenate([d_gate, d_up], axis=1)
    inc_in = (
        lax.dot_general(
            key_rows, joined, (((0,), (0,)), ((), ())), preferred_element_type=jnp.float32
        )
        * in_root
    )
    inc_out = (
        lax.dot_general(
            hidden, scaled, (((0,), (0,)), ((), ())), preferred_element_type=jnp.float32
        )
        * out_root
    )
    return (inc_in, inc_out)


def local_increments(keyn, values, step_size, weight_in, weight_out, block_root):
    heads = weight_in.shape[0]
    head_size = weight_in.shape[1]
    list_in = []
    list_out = []
    for head_number in range(heads):
        value_rows = values[:, head_number * head_size : (head_number + 1) * head_size]
        part_in, part_out = head_increments(
            keyn[:, head_number, :],
            value_rows,
            step_size[head_number],
            weight_in[head_number],
            weight_out[head_number],
            block_root,
        )
        list_in.append(part_in)
        list_out.append(part_out)
    return (jnp.stack(list_in), jnp.stack(list_out))


def renorm_in(matrix):
    heads, rows_here, double = matrix.shape
    split = matrix.reshape(heads, rows_here, 2, double // 2)
    return rms_rows(split).reshape(heads, rows_here, double)


def apply_head(query_rows, weight_in, weight_out):
    fast = weight_out.shape[0]
    pre = jnp.dot(query_rows, weight_in, preferred_element_type=jnp.float32) * (
        1.0 / math.sqrt(weight_in.shape[0])
    )
    gate = pre[:, :fast]
    hidden = (gate * jax.nn.sigmoid(gate) * pre[:, fast:]).astype(jnp.bfloat16)
    return jnp.dot(hidden, weight_out, preferred_element_type=jnp.float32) * (1.0 / math.sqrt(fast))


def apply_all(queryn, next_in, next_out):
    heads = next_in.shape[0]
    pieces = []
    for head_number in range(heads):
        pieces.append(
            apply_head(queryn[:, head_number, :], next_in[head_number], next_out[head_number])
        )
    return jnp.concatenate(pieces, axis=1).astype(jnp.bfloat16)


def per_device_generic(queries, keys, values, step_size, fast_in, fast_out):
    row_count = keys.shape[0]
    heads = fast_in.shape[0]
    head_size = keys.shape[1] // heads
    block_root = 1.0 / math.sqrt(row_count * lax.axis_size("tok"))
    keyn = normalized_heads(keys, heads, head_size)
    queryn = normalized_heads(queries, heads, head_size)
    master_in, master_out = (
        lax.all_gather(fast_in, "tok", axis=1, tiled=True),
        lax.all_gather(fast_out, "tok", axis=1, tiled=True),
    )
    inc_in, inc_out = local_increments(
        keyn,
        values,
        step_size,
        master_in.astype(jnp.bfloat16),
        master_out.astype(jnp.bfloat16),
        block_root,
    )
    total_in, total_out = lax.psum((inc_in, inc_out), "tok")
    whole_in = renorm_in(master_in + total_in)
    whole_out = rms_rows(master_out + total_out)
    output = apply_all(queryn, whole_in.astype(jnp.bfloat16), whole_out.astype(jnp.bfloat16))
    place = lax.axis_index("tok")
    fast_in_next = lax.dynamic_slice_in_dim(whole_in, place * fast_in.shape[1], fast_in.shape[1], 1)
    fast_out_next = lax.dynamic_slice_in_dim(
        whole_out, place * fast_out.shape[1], fast_out.shape[1], 1
    )
    return (output, fast_in_next, fast_out_next)


def swap(value, bits):
    count = lax.axis_size("tok")
    return lax.ppermute(value, "tok", [(place, place ^ bits) for place in range(count)])


def swap_parts(value):
    return lax.ppermute(value, "parts", [(0, 1), (1, 0)])


def after(value, *before):
    return lax.optimization_barrier((value, before))[0]


def compiler_params():
    return pltpu.CompilerParams(vmem_limit_bytes=VMEM_LIMIT)


def head_of(ids, order, other):
    return 2 * jnp.bitwise_xor(ids[1], other) + jnp.bitwise_xor(ids[2], order)


def normalize_head(block):
    wide = block.astype(F32)
    return (wide * lax.rsqrt(jnp.mean(wide * wide, axis=-1, keepdims=True) + 1e-06)).astype(BF16)


def pack_kernel(ids, in_hbm, out_hbm, own, theirs, in_ref, out_ref, arrived):
    copies = [
        pltpu.make_async_copy(in_hbm, in_ref, arrived.at[0]),
        pltpu.make_async_copy(out_hbm, out_ref, arrived.at[1]),
    ]
    for copy in copies:
        copy.start()
    for copy in copies:
        copy.wait()
    size = out_ref.shape[-1]
    rows = in_ref.shape[1]
    for other, ref in ((0, own), (1, theirs)):
        for order in range(2):
            head = head_of(ids, order, other)
            for block in range(in_ref.shape[2] // size):
                ref[order, block * rows : (block + 1) * rows, :] = in_ref[
                    head, :, block * size : (block + 1) * size
                ]
            ref[order, -out_ref.shape[1] :, :] = out_ref[head]


def pack(ids, fast_in, fast_out):
    rows = 4 * fast_in.shape[1] + fast_out.shape[1]
    shape = jax.ShapeDtypeStruct((2, rows, fast_out.shape[2]), F32)
    return pl.pallas_call(
        pack_kernel,
        in_specs=[pl.BlockSpec(memory_space=pltpu.SMEM)] + [pl.BlockSpec(memory_space=pltpu.HBM)] * 2,
        out_shape=[shape, shape],
        scratch_shapes=[
            pltpu.VMEM(fast_in.shape, F32),
            pltpu.VMEM(fast_out.shape, F32),
            pltpu.SemaphoreType.DMA((2,)),
        ],
        compiler_params=compiler_params(),
        name="pack",
    )(ids, fast_in, fast_out)


def pair_kernel(own, got, master_one, master_two, shard):
    for source, ref in enumerate((own, got)):
        for order, master in enumerate((master_one, master_two)):
            master[source] = ref[order]
        shard[source] = ref[0].astype(BF16)


def pair(own, got):
    wide = jax.ShapeDtypeStruct(own.shape, F32)
    return pl.pallas_call(
        pair_kernel,
        out_shape=[wide, wide, jax.ShapeDtypeStruct(own.shape, BF16)],
        compiler_params=compiler_params(),
        name="pair",
    )(own, got)


def prepare_kernel(heads, block_root, ids, x_ref, *rest):
    own, send = rest[-2:]
    core = ids[1]
    half = heads // 2
    size = x_ref.shape[1] // heads

    if len(rest) == 3:
        rates = rest[0][...]
        columns_of = jnp.concatenate([rates, rates], axis=0).T

    def work(owner, out):
        for local in range(half):
            columns = pl.ds(pl.multiple_of((owner * half + local) * size, size), size)
            into = slice(local * size, (local + 1) * size)
            if len(rest) == 2:
                out[:, into] = normalize_head(x_ref[:, columns])
            else:
                first = columns_of[:, local : local + 1]
                second = columns_of[:, half + local : half + local + 1]
                rate = jnp.where(owner == 0, first, second) * block_root
                out[:, into] = (rate * x_ref[:, columns].astype(F32)).astype(BF16)

    work(core, own)
    work(1 - core, send)


def prepare(ids, tokens, rates, heads, block_root, name):
    rows, width = tokens.shape
    step = 256
    wide = pl.BlockSpec((step, width), lambda i, ids: (i, 0))
    narrow = pl.BlockSpec((step, width // 2), lambda i, ids: (i, 0))
    operands, specs = [tokens], [wide]
    if rates is not None:
        operands.append(rates)
        specs.append(pl.BlockSpec((heads, step), lambda i, ids: (0, i)))
    shape = jax.ShapeDtypeStruct((rows, width // 2), BF16)
    return pl.pallas_call(
        functools.partial(prepare_kernel, heads, block_root),
        grid_spec=pltpu.PrefetchScalarGridSpec(
            num_scalar_prefetch=1,
            grid=(rows // step,),
            in_specs=specs,
            out_specs=[narrow] * 2,
        ),
        out_shape=[shape] * 2,
        compiler_params=compiler_params(),
        cost_estimate=pl.CostEstimate(
            flops=rows * width * 5, bytes_accessed=rows * width * 4, transcendentals=0
        ),
        name=name,
    )(ids, *operands)


def places(chip, core):
    for side in range(2):
        for slot in range(4):
            other = jnp.bitwise_xor(chip, 2 * slot + side)
            for source in range(2):
                yield side, slot, source, 2 * other + jnp.bitwise_xor(core, source)


def assemble(chip, core, lines, w_in, w_out):
    size = w_out.shape[1]
    blocks = w_in.shape[1] // size
    rows_in = w_in.shape[0] // 16
    rows_out = w_out.shape[0] // 16
    in_root = 1.0 / math.sqrt(size)
    for side, slot, source, place in places(chip, core):
        ref = lines[2 * side + slot // 2].at[slot % 2]
        into = pl.ds(pl.multiple_of(place * rows_in, rows_in), rows_in)
        for block in range(blocks):
            factor = in_root * (0.5 if block < blocks // 2 else 1.0)
            piece = ref[source, block * rows_in : (block + 1) * rows_in, :].astype(F32)
            w_in[into, block * size : (block + 1) * size] = (piece * factor).astype(BF16)
        into = pl.ds(pl.multiple_of(place * rows_out, rows_out), rows_out)
        w_out[into, :] = ref[source, blocks * rows_in :, :]


def increments_kernel(
    ids, near_low, near_high, far_low, far_high, k_own, v_own, k_got, v_got,
    kept, low, high, w_in, w_out, acc_in, acc_out, turned,
):
    step = pl.program_id(0)
    steps = pl.num_programs(0)
    chip, core = ids[0], ids[1]
    size = w_out.shape[1]
    fast = w_out.shape[0]
    in_root = 1.0 / math.sqrt(size)
    out_root = 1.0 / math.sqrt(fast)

    @pl.when(step == 0)
    def _():
        assemble(chip, core, (near_low, near_high, far_low, far_high), w_in, w_out)

    def work(k_ref, v_ref, start_over):
        keyn = k_ref[...]
        scaled = v_ref[...]
        keyn_t = keyn.T
        scaled_t = scaled.T

        def add(ref, columns, value):
            if start_over:
                ref[:, columns] = value
            else:
                ref[:, columns] += value

        chunk = 256
        for start in range(0, fast, chunk):
            gates = slice(start, start + chunk)
            ups = slice(fast + start, fast + start + chunk)
            gate = jnp.dot(keyn, w_in[:, gates], preferred_element_type=F32)
            upper = jnp.dot(keyn, w_in[:, ups], preferred_element_type=F32)
            back = (
                lax.dot_general(
                    scaled, w_out[gates, :], (((1,), (1,)), ((), ())), preferred_element_type=F32
                )
                * out_root
            )
            twice = jnp.tanh(gate) + 1.0
            active = gate * twice
            hidden = (active * upper).astype(BF16)
            d_gate = (back * upper * (twice + active * (2.0 - twice))).astype(BF16)
            d_up = (back * active).astype(BF16)
            add(acc_in, gates, jnp.dot(keyn_t, d_gate, preferred_element_type=F32))
            add(acc_in, ups, jnp.dot(keyn_t, d_up, preferred_element_type=F32))
            add(acc_out, gates, jnp.dot(scaled_t, hidden, preferred_element_type=F32))

    @pl.when(step == 0)
    def _():
        work(k_own, v_own, True)

    if k_own.shape[0] * 2 < 2048:

        @pl.when((step > 0) & (step < steps // 2))
        def _():
            work(k_own, v_own, False)

    @pl.when(step >= steps // 2)
    def _():
        work(k_got, v_got, False)

    @pl.when(step == steps - 1)
    def _():
        turned[...] = acc_out[...].T
        blocks = acc_in.shape[1] // size
        rows_in = acc_in.shape[0] // 16
        rows_out = turned.shape[0] // 16
        for side, slot, source, place in places(chip, core):
            ref = kept.at[slot] if side == 0 else (low, high)[slot // 2].at[slot % 2]
            rows = pl.ds(pl.multiple_of(place * rows_in, rows_in), rows_in)
            for block in range(blocks):
                ref[source, block * rows_in : (block + 1) * rows_in, :] = (
                    acc_in[rows, block * size : (block + 1) * size]
                    * (in_root * (0.5 if block < blocks // 2 else 1.0))
                ).astype(ref.dtype)
            rows = pl.ds(pl.multiple_of(place * rows_out, rows_out), rows_out)
            ref[source, blocks * rows_in :, :] = (turned[rows, :] * out_root).astype(ref.dtype)


def increments(ids, order, lines, k_own, v_own, k_got, v_got, fast):
    rows = k_own.shape[0]
    pair_shape = lines[0].shape
    size = pair_shape[-1]
    step = rows
    half = rows // step
    whole = pl.BlockSpec(pair_shape, lambda i, ids: (0, 0, 0, 0))
    line_shape = (4,) + pair_shape[1:]
    line = pl.BlockSpec(line_shape, lambda i, ids: (0, 0, 0, 0))
    own = pl.BlockSpec((step, size), lambda i, ids: (jnp.minimum(i, half - 1), ids[2] ^ order))
    got = pl.BlockSpec((step, size), lambda i, ids: (jnp.maximum(i - half, 0), ids[2] ^ order))
    return pl.pallas_call(
        increments_kernel,
        grid_spec=pltpu.PrefetchScalarGridSpec(
            num_scalar_prefetch=1,
            grid=(2 * half,),
            in_specs=[whole] * 4 + [own, own, got, got],
            out_specs=[line, whole, whole],
            scratch_shapes=[
                pltpu.VMEM((size, 2 * fast), BF16),
                pltpu.VMEM((fast, size), BF16),
                pltpu.VMEM((size, 2 * fast), F32),
                pltpu.VMEM((size, fast), F32),
                pltpu.VMEM((fast, size), F32),
            ],
        ),
        out_shape=[
            jax.ShapeDtypeStruct(line_shape, F32),
            jax.ShapeDtypeStruct(pair_shape, BF16),
            jax.ShapeDtypeStruct(pair_shape, BF16),
        ],
        compiler_params=compiler_params(),
        cost_estimate=pl.CostEstimate(
            flops=2 * rows * size * fast * 12, bytes_accessed=rows * size * 8, transcendentals=0
        ),
        name="increments",
    )(ids, *lines, k_own, v_own, k_got, v_got)


def add_kernel(kept, came, first, second):
    first[...] = (kept[0] + came[0].astype(F32)).astype(first.dtype)
    second[...] = (kept[1] + came[1].astype(F32)).astype(second.dtype)


def add_pair(kept, came, which, first_type):
    shape = came.shape
    flat = (0,) * (len(shape) - 1)
    return pl.pallas_call(
        add_kernel,
        grid=(1,),
        in_specs=[
            pl.BlockSpec(shape, lambda i: (which,) + flat),
            pl.BlockSpec(shape, lambda i: (0,) + flat),
        ],
        out_specs=[pl.BlockSpec(shape[1:], lambda i: flat)] * 2,
        out_shape=[
            jax.ShapeDtypeStruct(shape[1:], first_type),
            jax.ShapeDtypeStruct(shape[1:], BF16),
        ],
        compiler_params=compiler_params(),
        name="add_pair",
    )(kept, came)


def renorm_kernel(rows_in, master, kept, one, two, three, wide, short):
    size = master.shape[-1]
    for source in range(2):
        fresh = (
            master[source]
            + kept[source]
            + one[source].astype(F32)
            + two[source].astype(F32)
            + three[source].astype(F32)
        )
        for part in range(2):
            first = 2 * part * rows_in
            left = fresh[first : first + rows_in, :]
            right = fresh[first + rows_in : first + 2 * rows_in, :]
            total = jnp.sum(left * left + right * right, axis=-1, keepdims=True)
            factor = lax.rsqrt(total * (1.0 / (2 * size)) + 1e-06)
            for at, value in ((first, left), (first + rows_in, right)):
                done = value * factor
                wide[source, at : at + rows_in, :] = done
                short[source, at : at + rows_in, :] = done.astype(BF16)
        tail = fresh[4 * rows_in :, :]
        done = tail * lax.rsqrt(jnp.mean(tail * tail, axis=-1, keepdims=True) + 1e-06)
        wide[source, 4 * rows_in :, :] = done
        short[source, 4 * rows_in :, :] = done.astype(BF16)


def renorm(master, kept, one, two, three, rows_in):
    shape = master.shape
    return pl.pallas_call(
        functools.partial(renorm_kernel, rows_in),
        out_shape=[jax.ShapeDtypeStruct(shape, F32), jax.ShapeDtypeStruct(shape, BF16)],
        compiler_params=compiler_params(),
        name="renorm",
    )(master, kept, one, two, three)


def apply_kernel(order, other, ids, near_low, near_high, far_low, far_high, q_ref, *rest):
    o_hbm, w_in, w_out, o_ref, sent = rest[-5:]
    chip, core = ids[0], ids[1]
    fast, size = w_out.shape
    lines = (near_low, near_high, far_low, far_high)
    assemble(chip, jnp.bitwise_xor(core, other), lines, w_in, w_out)
    columns = pl.ds(pl.multiple_of(head_of(ids, order, other) * size, size), size)
    out_root = 1.0 / math.sqrt(fast)
    step = 512
    copies = []
    for start in range(0, q_ref.shape[0], step):
        rows = pl.ds(start, step)
        query = normalize_head(q_ref[rows, columns])
        gate = jnp.dot(query, w_in[:, :fast], preferred_element_type=F32)
        upper = jnp.dot(query, w_in[:, fast:], preferred_element_type=F32)
        hidden = (gate * (jnp.tanh(gate) + 1.0) * upper).astype(BF16)
        result = jnp.dot(hidden, w_out[...], preferred_element_type=F32) * out_root
        o_ref[rows, :] = result.astype(BF16)
        at = start // step
        copies.append(
            pltpu.make_async_copy(o_ref.at[rows, :], o_hbm.at[rows, columns], sent.at[at])
        )
        copies[-1].start()
    for copy in copies:
        copy.wait()


def apply_fast(ids, order, other, lines, queries, output, fast):
    rows, width = queries.shape
    size = lines[0].shape[-1]
    inside = pl.BlockSpec(memory_space=pltpu.VMEM)
    operands = [ids, *lines, queries]
    specs = [inside] * 5
    aliases = {}
    if output is not None:
        operands.append(output)
        specs.append(pl.BlockSpec(memory_space=pl.ANY))
        aliases = {6: 0}
    return pl.pallas_call(
        functools.partial(apply_kernel, order, other),
        grid_spec=pltpu.PrefetchScalarGridSpec(
            num_scalar_prefetch=1,
            grid=(1,),
            in_specs=specs,
            out_specs=pl.BlockSpec(memory_space=pl.ANY),
            scratch_shapes=[
                pltpu.VMEM((size, 2 * fast), BF16),
                pltpu.VMEM((fast, size), BF16),
                pltpu.VMEM((rows, size), BF16),
                pltpu.SemaphoreType.DMA((rows // 512,)),
            ],
        ),
        out_shape=jax.ShapeDtypeStruct((rows, width), BF16),
        input_output_aliases=aliases,
        compiler_params=compiler_params(),
        cost_estimate=pl.CostEstimate(
            flops=2 * rows * size * fast * 3, bytes_accessed=rows * size * 4, transcendentals=0
        ),
        name="apply",
    )(*operands)


def finish_kernel(rows_in, ids, one, two, came, in_next, out_next):
    size = out_next.shape[-1]
    for order, mine in enumerate((one, two)):
        for other, ref in ((0, mine.at[0]), (1, came.at[order])):
            head = head_of(ids, order, other)
            for block in range(4):
                in_next[head, :, block * size : (block + 1) * size] = ref[
                    block * rows_in : (block + 1) * rows_in, :
                ]
            out_next[head] = ref[4 * rows_in :, :]


def finish(ids, one, two, came, fast_in, fast_out):
    return pl.pallas_call(
        functools.partial(finish_kernel, fast_in.shape[1]),
        in_specs=[pl.BlockSpec(memory_space=pltpu.SMEM)] + [pl.BlockSpec(memory_space=pltpu.VMEM)] * 3,
        out_shape=[
            jax.ShapeDtypeStruct(fast_in.shape, F32),
            jax.ShapeDtypeStruct(fast_out.shape, F32),
        ],
        compiler_params=compiler_params(),
        name="finish",
    )(ids, one, two, came)


def per_device_cube(queries, keys, values, step_size, fast_in, fast_out):
    rows = keys.shape[0]
    heads = fast_in.shape[0]
    fast = fast_in.shape[2] // 2
    rows_in = fast_in.shape[1]
    place = lax.axis_index("tok")
    ids = jnp.stack([place // 2, place % 2, lax.axis_index("parts")]).astype(jnp.int32)
    block_root = 1.0 / math.sqrt(rows * lax.axis_size("tok"))

    k_own, k_send = prepare(ids, keys, None, heads, None, "keys")
    own, theirs = pack(after(ids, k_own), fast_in, fast_out)
    got = swap(theirs, 1)
    later = after(ids, got)
    v_own, v_send = prepare(later, values, step_size, heads, block_root, "values")
    master_one, master_two, shard = pair(own, after(got, k_send, v_send))
    masters = (master_one, master_two)
    k_got, v_got = swap(k_send, 1), swap(v_send, 1)
    z1, z3, z2 = swap(shard, 4), swap(shard, 12), swap(shard, 8)
    near_low = after(jnp.stack([shard, z1]), k_got, v_got)
    far_low, other_near_low = swap(near_low, 2), swap_parts(near_low)
    near_high = after(jnp.stack([z2, z3]), far_low, other_near_low)
    far_high = swap(near_high, 2)
    first = (near_low, near_high, far_low, far_high)
    second = (other_near_low, *(swap_parts(piece) for piece in first[1:]))

    wide, short = [], []
    for order in range(2):
        lines = second if order else first
        later = ids if order else after(ids, second[2])
        kept, low, high = increments(later, order, lines, k_own, v_own, k_got, v_got, fast)
        high, low = swap(high, 2), swap(low, 2)
        sum2, sum3 = add_pair(kept, high, 1, BF16)
        sum0, sum1 = add_pair(kept, low, 0, F32)
        three, two, one = swap(sum3, 12), swap(sum2, 8), swap(sum1, 4)
        a, b = renorm(masters[order], sum0, one, two, three, rows_in)
        wide.append(a)
        short.append(b)

    z1, z3, z2 = swap(short[0], 4), swap(short[0], 12), swap(short[0], 8)
    near_low, near_high = jnp.stack([short[0], z1]), jnp.stack([z2, z3])
    far_low, far_high = swap(near_low, 2), swap(near_high, 2)
    second = after(short[1], near_low)
    z1 = swap(second, 4)
    second_low = after(jnp.stack([second, z1]), near_high)
    later = after(short[1], second_low)
    z3, z2 = swap(later, 12), swap(later, 8)
    second_high = jnp.stack([z2, z3])
    mine = (near_low, near_high, far_low, far_high)
    others = tuple(swap(piece, 1) for piece in mine)
    output = apply_fast(ids, 0, 0, mine, queries, None, fast)
    came = swap(jnp.stack([wide[0][1], wide[1][1]]), 1)
    updated = finish(ids, wide[0], wide[1], came, fast_in, fast_out)
    near_low, near_high = second_low, after(second_high, *updated)
    output = apply_fast(ids, 0, 1, others, queries, output, fast)
    far_low, far_high = swap(near_low, 2), swap(near_high, 2)
    far_high = after(far_high, output)
    mine = (near_low, near_high, far_low, far_high)
    others = tuple(swap(piece, 1) for piece in mine)
    output = apply_fast(ids, 1, 0, mine, queries, output, fast)
    output = apply_fast(ids, 1, 1, others, queries, output, fast)

    return (output, *updated)


def per_device(queries, keys, values, step_size, fast_in, fast_out):
    fits = (
        lax.axis_size("tok") == 16
        and lax.axis_size("parts") == 2
        and fast_in.shape[0] == 4
        and fast_in.shape[1] % 16 == 0
    )
    chosen = per_device_cube if fits else per_device_generic
    return chosen(queries, keys, values, step_size, fast_in, fast_out)


def solution(mesh):
    placed = (
        P(("parts", "tok"), None),
        P(("parts", "tok"), None),
        P(("parts", "tok"), None),
        P(None, ("parts", "tok")),
        P(None, "tok", None),
        P(None, "tok", None),
    )
    return jax.shard_map(
        per_device,
        mesh=mesh,
        in_specs=placed,
        out_specs=(P(("parts", "tok"), None), P("parts", "tok", None), P("parts", "tok", None)),
        check_vma=False,
    )
```

```python
import functools
import math

import jax
import jax.numpy as jnp
from jax import lax
from jax.experimental import pallas as pl
from jax.experimental.pallas import tpu as pltpu
from jax.sharding import PartitionSpec as P

BF16 = jnp.bfloat16
F32 = jnp.float32
VMEM_LIMIT = 32 * 1024 * 1024


def rms_rows(matrix):
    return matrix * lax.rsqrt(jnp.mean(matrix * matrix, axis=-1, keepdims=True) + 1e-06)


def normalized_heads(tokens, heads, head_size):
    row_count = tokens.shape[0]
    wide = tokens.astype(jnp.float32).reshape(row_count, heads, head_size)
    return rms_rows(wide).astype(jnp.bfloat16)


def head_increments(key_rows, value_rows, rates, weight_in, weight_out, block_root):
    fast = weight_out.shape[0]
    in_root = 1.0 / math.sqrt(weight_in.shape[0])
    out_root = 1.0 / math.sqrt(fast)
    scaled = (rates[:, None] * block_root * value_rows.astype(jnp.float32)).astype(jnp.bfloat16)
    pre = jnp.dot(key_rows, weight_in, preferred_element_type=jnp.float32) * in_root
    gate = pre[:, :fast]
    upper = pre[:, fast:]
    sigma = jax.nn.sigmoid(gate)
    active = gate * sigma
    hidden = (active * upper).astype(jnp.bfloat16)
    back = (
        lax.dot_general(
            scaled, weight_out, (((1,), (1,)), ((), ())), preferred_element_type=jnp.float32
        )
        * out_root
    )
    d_gate = (back * upper * sigma * (1.0 + gate * (1.0 - sigma))).astype(jnp.bfloat16)
    d_up = (back * active).astype(jnp.bfloat16)
    joined = jnp.concatenate([d_gate, d_up], axis=1)
    inc_in = (
        lax.dot_general(
            key_rows, joined, (((0,), (0,)), ((), ())), preferred_element_type=jnp.float32
        )
        * in_root
    )
    inc_out = (
        lax.dot_general(
            hidden, scaled, (((0,), (0,)), ((), ())), preferred_element_type=jnp.float32
        )
        * out_root
    )
    return (inc_in, inc_out)


def local_increments(keyn, values, step_size, weight_in, weight_out, block_root):
    heads = weight_in.shape[0]
    head_size = weight_in.shape[1]
    list_in = []
    list_out = []
    for head_number in range(heads):
        value_rows = values[:, head_number * head_size : (head_number + 1) * head_size]
        part_in, part_out = head_increments(
            keyn[:, head_number, :],
            value_rows,
            step_size[head_number],
            weight_in[head_number],
            weight_out[head_number],
            block_root,
        )
        list_in.append(part_in)
        list_out.append(part_out)
    return (jnp.stack(list_in), jnp.stack(list_out))


def renorm_in(matrix):
    heads, rows_here, double = matrix.shape
    split = matrix.reshape(heads, rows_here, 2, double // 2)
    return rms_rows(split).reshape(heads, rows_here, double)


def apply_head(query_rows, weight_in, weight_out):
    fast = weight_out.shape[0]
    pre = jnp.dot(query_rows, weight_in, preferred_element_type=jnp.float32) * (
        1.0 / math.sqrt(weight_in.shape[0])
    )
    gate = pre[:, :fast]
    hidden = (gate * jax.nn.sigmoid(gate) * pre[:, fast:]).astype(jnp.bfloat16)
    return jnp.dot(hidden, weight_out, preferred_element_type=jnp.float32) * (1.0 / math.sqrt(fast))


def apply_all(queryn, next_in, next_out):
    heads = next_in.shape[0]
    pieces = []
    for head_number in range(heads):
        pieces.append(
            apply_head(queryn[:, head_number, :], next_in[head_number], next_out[head_number])
        )
    return jnp.concatenate(pieces, axis=1).astype(jnp.bfloat16)


def per_device_generic(queries, keys, values, step_size, fast_in, fast_out):
    row_count = keys.shape[0]
    heads = fast_in.shape[0]
    head_size = keys.shape[1] // heads
    block_root = 1.0 / math.sqrt(row_count * lax.axis_size("tok"))
    keyn = normalized_heads(keys, heads, head_size)
    queryn = normalized_heads(queries, heads, head_size)
    master_in, master_out = (
        lax.all_gather(fast_in, "tok", axis=1, tiled=True),
        lax.all_gather(fast_out, "tok", axis=1, tiled=True),
    )
    inc_in, inc_out = local_increments(
        keyn,
        values,
        step_size,
        master_in.astype(jnp.bfloat16),
        master_out.astype(jnp.bfloat16),
        block_root,
    )
    total_in, total_out = lax.psum((inc_in, inc_out), "tok")
    whole_in = renorm_in(master_in + total_in)
    whole_out = rms_rows(master_out + total_out)
    output = apply_all(queryn, whole_in.astype(jnp.bfloat16), whole_out.astype(jnp.bfloat16))
    place = lax.axis_index("tok")
    fast_in_next = lax.dynamic_slice_in_dim(whole_in, place * fast_in.shape[1], fast_in.shape[1], 1)
    fast_out_next = lax.dynamic_slice_in_dim(
        whole_out, place * fast_out.shape[1], fast_out.shape[1], 1
    )
    return (output, fast_in_next, fast_out_next)


def swap(value, bits):
    count = lax.axis_size("tok")
    return lax.ppermute(value, "tok", [(place, place ^ bits) for place in range(count)])


def swap_parts(value):
    return lax.ppermute(value, "parts", [(0, 1), (1, 0)])


def after(value, *before):
    return lax.optimization_barrier((value, before))[0]


def compiler_params():
    return pltpu.CompilerParams(vmem_limit_bytes=VMEM_LIMIT)


def head_of(ids, order, other):
    return 2 * jnp.bitwise_xor(ids[1], other) + jnp.bitwise_xor(ids[2], order)


def normalize_head(block):
    wide = block.astype(F32)
    return (wide * lax.rsqrt(jnp.mean(wide * wide, axis=-1, keepdims=True) + 1e-06)).astype(BF16)


def pack_kernel(ids, in_hbm, out_hbm, own, theirs, in_ref, out_ref, arrived):
    copies = [
        pltpu.make_async_copy(in_hbm, in_ref, arrived.at[0]),
        pltpu.make_async_copy(out_hbm, out_ref, arrived.at[1]),
    ]
    for copy in copies:
        copy.start()
    for copy in copies:
        copy.wait()
    size = out_ref.shape[-1]
    rows = in_ref.shape[1]
    for other, ref in ((0, own), (1, theirs)):
        for order in range(2):
            head = head_of(ids, order, other)
            for block in range(in_ref.shape[2] // size):
                ref[order, block * rows : (block + 1) * rows, :] = in_ref[
                    head, :, block * size : (block + 1) * size
                ]
            ref[order, -out_ref.shape[1] :, :] = out_ref[head]


def pack(ids, fast_in, fast_out):
    rows = 4 * fast_in.shape[1] + fast_out.shape[1]
    shape = jax.ShapeDtypeStruct((2, rows, fast_out.shape[2]), F32)
    return pl.pallas_call(
        pack_kernel,
        in_specs=[pl.BlockSpec(memory_space=pltpu.SMEM)] + [pl.BlockSpec(memory_space=pltpu.HBM)] * 2,
        out_shape=[shape, shape],
        scratch_shapes=[
            pltpu.VMEM(fast_in.shape, F32),
            pltpu.VMEM(fast_out.shape, F32),
            pltpu.SemaphoreType.DMA((2,)),
        ],
        compiler_params=compiler_params(),
        name="pack",
    )(ids, fast_in, fast_out)


def pair_kernel(own, got, master_one, master_two, shard):
    for source, ref in enumerate((own, got)):
        for order, master in enumerate((master_one, master_two)):
            master[source] = ref[order]
        shard[source] = ref[0].astype(BF16)


def pair(own, got):
    wide = jax.ShapeDtypeStruct(own.shape, F32)
    return pl.pallas_call(
        pair_kernel,
        out_shape=[wide, wide, jax.ShapeDtypeStruct(own.shape, BF16)],
        compiler_params=compiler_params(),
        name="pair",
    )(own, got)


def prepare_kernel(heads, block_root, ids, x_ref, *rest):
    own, send = rest[-2:]
    core = ids[1]
    half = heads // 2
    size = x_ref.shape[1] // heads

    if len(rest) == 3:
        rates = rest[0][...]
        columns_of = jnp.concatenate([rates, rates], axis=0).T

    def work(owner, out):
        for local in range(half):
            columns = pl.ds(pl.multiple_of((owner * half + local) * size, size), size)
            into = slice(local * size, (local + 1) * size)
            if len(rest) == 2:
                out[:, into] = normalize_head(x_ref[:, columns])
            else:
                first = columns_of[:, local : local + 1]
                second = columns_of[:, half + local : half + local + 1]
                rate = jnp.where(owner == 0, first, second) * block_root
                out[:, into] = (rate * x_ref[:, columns].astype(F32)).astype(BF16)

    work(core, own)
    work(1 - core, send)


def prepare(ids, tokens, rates, heads, block_root, name):
    rows, width = tokens.shape
    step = 256
    wide = pl.BlockSpec((step, width), lambda i, ids: (i, 0))
    narrow = pl.BlockSpec((step, width // 2), lambda i, ids: (i, 0))
    operands, specs = [tokens], [wide]
    if rates is not None:
        operands.append(rates)
        specs.append(pl.BlockSpec((heads, step), lambda i, ids: (0, i)))
    shape = jax.ShapeDtypeStruct((rows, width // 2), BF16)
    return pl.pallas_call(
        functools.partial(prepare_kernel, heads, block_root),
        grid_spec=pltpu.PrefetchScalarGridSpec(
            num_scalar_prefetch=1,
            grid=(rows // step,),
            in_specs=specs,
            out_specs=[narrow] * 2,
        ),
        out_shape=[shape] * 2,
        compiler_params=compiler_params(),
        cost_estimate=pl.CostEstimate(
            flops=rows * width * 5, bytes_accessed=rows * width * 4, transcendentals=0
        ),
        name=name,
    )(ids, *operands)


def places(chip, core):
    for side in range(2):
        for slot in range(4):
            other = jnp.bitwise_xor(chip, 2 * slot + side)
            for source in range(2):
                yield side, slot, source, 2 * other + jnp.bitwise_xor(core, source)


def assemble(chip, core, lines, w_in, w_out):
    size = w_out.shape[1]
    blocks = w_in.shape[1] // size
    rows_in = w_in.shape[0] // 16
    rows_out = w_out.shape[0] // 16
    in_root = 1.0 / math.sqrt(size)
    slots = [line.at[index] for line in lines for index in range(line.shape[0])]
    for side, slot, source, place in places(chip, core):
        ref = slots[4 * side + slot]
        into = pl.ds(pl.multiple_of(place * rows_in, rows_in), rows_in)
        for block in range(blocks):
            factor = in_root * (0.5 if block < blocks // 2 else 1.0)
            piece = ref[source, block * rows_in : (block + 1) * rows_in, :].astype(F32)
            w_in[into, block * size : (block + 1) * size] = (piece * factor).astype(BF16)
        into = pl.ds(pl.multiple_of(place * rows_out, rows_out), rows_out)
        w_out[into, :] = ref[source, blocks * rows_in :, :]


def increments_kernel(
    ids, near_low, near_high, far_low, far_high, k_own, v_own, k_got, v_got,
    kept, low, high, w_in, w_out, acc_in, acc_out, turned,
):
    step = pl.program_id(0)
    steps = pl.num_programs(0)
    chip, core = ids[0], ids[1]
    size = w_out.shape[1]
    fast = w_out.shape[0]
    in_root = 1.0 / math.sqrt(size)
    out_root = 1.0 / math.sqrt(fast)

    @pl.when(step == 0)
    def _():
        assemble(chip, core, (near_low, near_high, far_low, far_high), w_in, w_out)

    def work(k_ref, v_ref, start_over):
        keyn = k_ref[...]
        scaled = v_ref[...]
        keyn_t = keyn.T
        scaled_t = scaled.T

        def add(ref, columns, value):
            if start_over:
                ref[:, columns] = value
            else:
                ref[:, columns] += value

        chunk = 256
        for start in range(0, fast, chunk):
            gates = slice(start, start + chunk)
            ups = slice(fast + start, fast + start + chunk)
            gate = jnp.dot(keyn, w_in[:, gates], preferred_element_type=F32)
            upper = jnp.dot(keyn, w_in[:, ups], preferred_element_type=F32)
            back = (
                lax.dot_general(
                    scaled, w_out[gates, :], (((1,), (1,)), ((), ())), preferred_element_type=F32
                )
                * out_root
            )
            twice = jnp.tanh(gate) + 1.0
            active = gate * twice
            hidden = (active * upper).astype(BF16)
            d_gate = (back * upper * (twice + active * (2.0 - twice))).astype(BF16)
            d_up = (back * active).astype(BF16)
            add(acc_in, gates, jnp.dot(keyn_t, d_gate, preferred_element_type=F32))
            add(acc_in, ups, jnp.dot(keyn_t, d_up, preferred_element_type=F32))
            add(acc_out, gates, jnp.dot(scaled_t, hidden, preferred_element_type=F32))

    @pl.when(step == 0)
    def _():
        work(k_own, v_own, True)

    if k_own.shape[0] * 2 < 2048:

        @pl.when((step > 0) & (step < steps // 2))
        def _():
            work(k_own, v_own, False)

    @pl.when(step >= steps // 2)
    def _():
        work(k_got, v_got, False)

    @pl.when(step == steps - 1)
    def _():
        turned[...] = acc_out[...].T
        blocks = acc_in.shape[1] // size
        rows_in = acc_in.shape[0] // 16
        rows_out = turned.shape[0] // 16
        for side, slot, source, place in places(chip, core):
            ref = kept.at[slot] if side == 0 else (low, high)[slot // 2].at[slot % 2]
            rows = pl.ds(pl.multiple_of(place * rows_in, rows_in), rows_in)
            for block in range(blocks):
                ref[source, block * rows_in : (block + 1) * rows_in, :] = (
                    acc_in[rows, block * size : (block + 1) * size]
                    * (in_root * (0.5 if block < blocks // 2 else 1.0))
                ).astype(ref.dtype)
            rows = pl.ds(pl.multiple_of(place * rows_out, rows_out), rows_out)
            ref[source, blocks * rows_in :, :] = (turned[rows, :] * out_root).astype(ref.dtype)


def increments(ids, order, lines, k_own, v_own, k_got, v_got, fast):
    rows = k_own.shape[0]
    pair_shape = lines[0].shape
    size = pair_shape[-1]
    step = rows
    half = rows // step
    whole = pl.BlockSpec(pair_shape, lambda i, ids: (0, 0, 0, 0))
    line_shape = (4,) + pair_shape[1:]
    line = pl.BlockSpec(line_shape, lambda i, ids: (0, 0, 0, 0))
    own = pl.BlockSpec((step, size), lambda i, ids: (jnp.minimum(i, half - 1), ids[2] ^ order))
    got = pl.BlockSpec((step, size), lambda i, ids: (jnp.maximum(i - half, 0), ids[2] ^ order))
    return pl.pallas_call(
        increments_kernel,
        grid_spec=pltpu.PrefetchScalarGridSpec(
            num_scalar_prefetch=1,
            grid=(2 * half,),
            in_specs=[whole] * 4 + [own, own, got, got],
            out_specs=[line, whole, whole],
            scratch_shapes=[
                pltpu.VMEM((size, 2 * fast), BF16),
                pltpu.VMEM((fast, size), BF16),
                pltpu.VMEM((size, 2 * fast), F32),
                pltpu.VMEM((size, fast), F32),
                pltpu.VMEM((fast, size), F32),
            ],
        ),
        out_shape=[
            jax.ShapeDtypeStruct(line_shape, F32),
            jax.ShapeDtypeStruct(pair_shape, BF16),
            jax.ShapeDtypeStruct(pair_shape, BF16),
        ],
        compiler_params=compiler_params(),
        cost_estimate=pl.CostEstimate(
            flops=2 * rows * size * fast * 12, bytes_accessed=rows * size * 8, transcendentals=0
        ),
        name="increments",
    )(ids, *lines, k_own, v_own, k_got, v_got)


def add_kernel(kept, came, first, second):
    first[...] = (kept[0] + came[0].astype(F32)).astype(first.dtype)
    second[...] = (kept[1] + came[1].astype(F32)).astype(second.dtype)


def add_pair(kept, came, which, first_type):
    shape = came.shape
    flat = (0,) * (len(shape) - 1)
    return pl.pallas_call(
        add_kernel,
        grid=(1,),
        in_specs=[
            pl.BlockSpec(shape, lambda i: (which,) + flat),
            pl.BlockSpec(shape, lambda i: (0,) + flat),
        ],
        out_specs=[pl.BlockSpec(shape[1:], lambda i: flat)] * 2,
        out_shape=[
            jax.ShapeDtypeStruct(shape[1:], first_type),
            jax.ShapeDtypeStruct(shape[1:], BF16),
        ],
        compiler_params=compiler_params(),
        name="add_pair",
    )(kept, came)


def renorm_kernel(rows_in, master, kept, one, two, three, wide, short):
    size = master.shape[-1]
    for source in range(2):
        fresh = (
            master[source]
            + kept[source]
            + one[source].astype(F32)
            + two[source].astype(F32)
            + three[source].astype(F32)
        )
        for part in range(2):
            first = 2 * part * rows_in
            left = fresh[first : first + rows_in, :]
            right = fresh[first + rows_in : first + 2 * rows_in, :]
            total = jnp.sum(left * left + right * right, axis=-1, keepdims=True)
            factor = lax.rsqrt(total * (1.0 / (2 * size)) + 1e-06)
            for at, value in ((first, left), (first + rows_in, right)):
                done = value * factor
                wide[source, at : at + rows_in, :] = done
                short[source, at : at + rows_in, :] = done.astype(BF16)
        tail = fresh[4 * rows_in :, :]
        done = tail * lax.rsqrt(jnp.mean(tail * tail, axis=-1, keepdims=True) + 1e-06)
        wide[source, 4 * rows_in :, :] = done
        short[source, 4 * rows_in :, :] = done.astype(BF16)


def renorm(master, kept, one, two, three, rows_in):
    shape = master.shape
    return pl.pallas_call(
        functools.partial(renorm_kernel, rows_in),
        out_shape=[jax.ShapeDtypeStruct(shape, F32), jax.ShapeDtypeStruct(shape, BF16)],
        compiler_params=compiler_params(),
        name="renorm",
    )(master, kept, one, two, three)


def apply_kernel(order, other, count, ids, *rest):
    lines, q_ref = rest[:count], rest[count]
    o_hbm, w_in, w_out, o_ref, sent = rest[-5:]
    chip, core = ids[0], ids[1]
    fast, size = w_out.shape
    assemble(chip, jnp.bitwise_xor(core, other), lines, w_in, w_out)
    columns = pl.ds(pl.multiple_of(head_of(ids, order, other) * size, size), size)
    out_root = 1.0 / math.sqrt(fast)
    step = 512
    copies = []
    for start in range(0, q_ref.shape[0], step):
        rows = pl.ds(start, step)
        query = normalize_head(q_ref[rows, columns])
        gate = jnp.dot(query, w_in[:, :fast], preferred_element_type=F32)
        upper = jnp.dot(query, w_in[:, fast:], preferred_element_type=F32)
        hidden = (gate * (jnp.tanh(gate) + 1.0) * upper).astype(BF16)
        result = jnp.dot(hidden, w_out[...], preferred_element_type=F32) * out_root
        o_ref[rows, :] = result.astype(BF16)
        at = start // step
        copies.append(
            pltpu.make_async_copy(o_ref.at[rows, :], o_hbm.at[rows, columns], sent.at[at])
        )
        copies[-1].start()
    for copy in copies:
        copy.wait()


def apply_fast(ids, order, other, lines, queries, output, fast):
    rows, width = queries.shape
    size = lines[0].shape[-1]
    inside = pl.BlockSpec(memory_space=pltpu.VMEM)
    operands = [ids, *lines, queries]
    specs = [inside] * (len(lines) + 1)
    aliases = {}
    if output is not None:
        operands.append(output)
        specs.append(pl.BlockSpec(memory_space=pl.ANY))
        aliases = {len(lines) + 2: 0}
    return pl.pallas_call(
        functools.partial(apply_kernel, order, other, len(lines)),
        grid_spec=pltpu.PrefetchScalarGridSpec(
            num_scalar_prefetch=1,
            grid=(1,),
            in_specs=specs,
            out_specs=pl.BlockSpec(memory_space=pl.ANY),
            scratch_shapes=[
                pltpu.VMEM((size, 2 * fast), BF16),
                pltpu.VMEM((fast, size), BF16),
                pltpu.VMEM((rows, size), BF16),
                pltpu.SemaphoreType.DMA((rows // 512,)),
            ],
        ),
        out_shape=jax.ShapeDtypeStruct((rows, width), BF16),
        input_output_aliases=aliases,
        compiler_params=compiler_params(),
        cost_estimate=pl.CostEstimate(
            flops=2 * rows * size * fast * 3, bytes_accessed=rows * size * 4, transcendentals=0
        ),
        name="apply",
    )(*operands)


def finish_kernel(rows_in, ids, one, two, came, in_next, out_next):
    size = out_next.shape[-1]
    for order, mine in enumerate((one, two)):
        for other, ref in ((0, mine.at[0]), (1, came.at[order])):
            head = head_of(ids, order, other)
            for block in range(4):
                in_next[head, :, block * size : (block + 1) * size] = ref[
                    block * rows_in : (block + 1) * rows_in, :
                ]
            out_next[head] = ref[4 * rows_in :, :]


def finish(ids, one, two, came, fast_in, fast_out):
    return pl.pallas_call(
        functools.partial(finish_kernel, fast_in.shape[1]),
        in_specs=[pl.BlockSpec(memory_space=pltpu.SMEM)] + [pl.BlockSpec(memory_space=pltpu.VMEM)] * 3,
        out_shape=[
            jax.ShapeDtypeStruct(fast_in.shape, F32),
            jax.ShapeDtypeStruct(fast_out.shape, F32),
        ],
        compiler_params=compiler_params(),
        name="finish",
    )(ids, one, two, came)


def per_device_cube(queries, keys, values, step_size, fast_in, fast_out):
    rows = keys.shape[0]
    heads = fast_in.shape[0]
    fast = fast_in.shape[2] // 2
    rows_in = fast_in.shape[1]
    place = lax.axis_index("tok")
    ids = jnp.stack([place // 2, place % 2, lax.axis_index("parts")]).astype(jnp.int32)
    block_root = 1.0 / math.sqrt(rows * lax.axis_size("tok"))

    k_own, k_send = prepare(ids, keys, None, heads, None, "keys")
    own, theirs = pack(after(ids, k_own), fast_in, fast_out)
    got = swap(theirs, 1)
    later = after(ids, got)
    v_own, v_send = prepare(later, values, step_size, heads, block_root, "values")
    master_one, master_two, shard = pair(own, after(got, k_send, v_send))
    masters = (master_one, master_two)
    k_got, v_got = swap(k_send, 1), swap(v_send, 1)
    z1, z3, z2 = swap(shard, 4), swap(shard, 12), swap(shard, 8)
    near_low = after(jnp.stack([shard, z1]), k_got, v_got)
    far_low, other_near_low = swap(near_low, 2), swap_parts(near_low)
    near_high = after(jnp.stack([z2, z3]), far_low, other_near_low)
    far_high = swap(near_high, 2)
    first = (near_low, near_high, far_low, far_high)
    second = (other_near_low, *(swap_parts(piece) for piece in first[1:]))

    kept_one, low_one, high_one = increments(
        after(ids, second[2]), 0, first, k_own, v_own, k_got, v_got, fast
    )
    kept_two, low_two, high_two = increments(ids, 1, second, k_own, v_own, k_got, v_got, fast)
    low_one, high_one = after((swap(low_one, 2), swap(high_one, 2)), kept_two)
    low_two, high_two = swap(low_two, 2), swap(high_two, 2)
    wide, short = [], []
    for order, (kept, low, high) in enumerate(
        ((kept_one, low_one, high_one), (kept_two, low_two, high_two))
    ):
        sum2, sum3 = add_pair(kept, high, 1, BF16)
        sum0, sum1 = add_pair(kept, low, 0, F32)
        sums = (sum1, sum2, sum3)
        three, two, one = swap(sum3, 12), swap(sum2, 8), swap(sum1, 4)
        a, b = renorm(masters[order], sum0, one, two, three, rows_in)
        wide.append(a)
        short.append(b)

    shard = after(short[0], low_two, high_two)
    z1, z3, z2 = swap(shard, 4), swap(shard, 12), swap(shard, 8)
    near = after(jnp.stack([shard, z1, z2, z3]), short[1])
    far = swap(near, 2)
    second = short[1]
    z1, z3, z2 = swap(second, 4), swap(second, 12), swap(second, 8)
    second_low, second_high = jnp.stack([second, z1]), jnp.stack([z2, z3])
    mine = (near, far)
    others = tuple(swap(piece, 1) for piece in mine)
    output = apply_fast(ids, 0, 0, mine, queries, None, fast)
    came = swap(jnp.stack([wide[0][1], wide[1][1]]), 1)
    updated = finish(ids, wide[0], wide[1], came, fast_in, fast_out)
    near_low, near_high = second_low, second_high
    output = after(output, *updated)
    output = apply_fast(ids, 0, 1, others, queries, output, fast)
    far_low, far_high = swap(near_low, 2), swap(near_high, 2)
    far_high = after(far_high, output)
    mine = (near_low, near_high, far_low, far_high)
    others = tuple(swap(piece, 1) for piece in mine)
    output = apply_fast(ids, 1, 0, mine, queries, output, fast)
    output = apply_fast(ids, 1, 1, others, queries, output, fast)

    return (output, *updated)


def per_device(queries, keys, values, step_size, fast_in, fast_out):
    fits = (
        lax.axis_size("tok") == 16
        and lax.axis_size("parts") == 2
        and fast_in.shape[0] == 4
        and fast_in.shape[1] % 16 == 0
    )
    chosen = per_device_cube if fits else per_device_generic
    return chosen(queries, keys, values, step_size, fast_in, fast_out)


def solution(mesh):
    placed = (
        P(("parts", "tok"), None),
        P(("parts", "tok"), None),
        P(("parts", "tok"), None),
        P(None, ("parts", "tok")),
        P(None, "tok", None),
        P(None, "tok", None),
    )
    return jax.shard_map(
        per_device,
        mesh=mesh,
        in_specs=placed,
        out_specs=(P(("parts", "tok"), None), P("parts", "tok", None), P("parts", "tok", None)),
        check_vma=False,
    )
```

```python
import functools
import math

import jax
import jax.numpy as jnp
from jax import lax
from jax.experimental import pallas as pl
from jax.experimental.pallas import tpu as pltpu
from jax.sharding import PartitionSpec as P

BF16 = jnp.bfloat16
F32 = jnp.float32
VMEM_LIMIT = 32 * 1024 * 1024


def rms_rows(matrix):
    return matrix * lax.rsqrt(jnp.mean(matrix * matrix, axis=-1, keepdims=True) + 1e-06)


def normalized_heads(tokens, heads, head_size):
    row_count = tokens.shape[0]
    wide = tokens.astype(jnp.float32).reshape(row_count, heads, head_size)
    return rms_rows(wide).astype(jnp.bfloat16)


def head_increments(key_rows, value_rows, rates, weight_in, weight_out, block_root):
    fast = weight_out.shape[0]
    in_root = 1.0 / math.sqrt(weight_in.shape[0])
    out_root = 1.0 / math.sqrt(fast)
    scaled = (rates[:, None] * block_root * value_rows.astype(jnp.float32)).astype(jnp.bfloat16)
    pre = jnp.dot(key_rows, weight_in, preferred_element_type=jnp.float32) * in_root
    gate = pre[:, :fast]
    upper = pre[:, fast:]
    sigma = jax.nn.sigmoid(gate)
    active = gate * sigma
    hidden = (active * upper).astype(jnp.bfloat16)
    back = (
        lax.dot_general(
            scaled, weight_out, (((1,), (1,)), ((), ())), preferred_element_type=jnp.float32
        )
        * out_root
    )
    d_gate = (back * upper * sigma * (1.0 + gate * (1.0 - sigma))).astype(jnp.bfloat16)
    d_up = (back * active).astype(jnp.bfloat16)
    joined = jnp.concatenate([d_gate, d_up], axis=1)
    inc_in = (
        lax.dot_general(
            key_rows, joined, (((0,), (0,)), ((), ())), preferred_element_type=jnp.float32
        )
        * in_root
    )
    inc_out = (
        lax.dot_general(
            hidden, scaled, (((0,), (0,)), ((), ())), preferred_element_type=jnp.float32
        )
        * out_root
    )
    return (inc_in, inc_out)


def local_increments(keyn, values, step_size, weight_in, weight_out, block_root):
    heads = weight_in.shape[0]
    head_size = weight_in.shape[1]
    list_in = []
    list_out = []
    for head_number in range(heads):
        value_rows = values[:, head_number * head_size : (head_number + 1) * head_size]
        part_in, part_out = head_increments(
            keyn[:, head_number, :],
            value_rows,
            step_size[head_number],
            weight_in[head_number],
            weight_out[head_number],
            block_root,
        )
        list_in.append(part_in)
        list_out.append(part_out)
    return (jnp.stack(list_in), jnp.stack(list_out))


def renorm_in(matrix):
    heads, rows_here, double = matrix.shape
    split = matrix.reshape(heads, rows_here, 2, double // 2)
    return rms_rows(split).reshape(heads, rows_here, double)


def apply_head(query_rows, weight_in, weight_out):
    fast = weight_out.shape[0]
    pre = jnp.dot(query_rows, weight_in, preferred_element_type=jnp.float32) * (
        1.0 / math.sqrt(weight_in.shape[0])
    )
    gate = pre[:, :fast]
    hidden = (gate * jax.nn.sigmoid(gate) * pre[:, fast:]).astype(jnp.bfloat16)
    return jnp.dot(hidden, weight_out, preferred_element_type=jnp.float32) * (1.0 / math.sqrt(fast))


def apply_all(queryn, next_in, next_out):
    heads = next_in.shape[0]
    pieces = []
    for head_number in range(heads):
        pieces.append(
            apply_head(queryn[:, head_number, :], next_in[head_number], next_out[head_number])
        )
    return jnp.concatenate(pieces, axis=1).astype(jnp.bfloat16)


def per_device_generic(queries, keys, values, step_size, fast_in, fast_out):
    row_count = keys.shape[0]
    heads = fast_in.shape[0]
    head_size = keys.shape[1] // heads
    block_root = 1.0 / math.sqrt(row_count * lax.axis_size("tok"))
    keyn = normalized_heads(keys, heads, head_size)
    queryn = normalized_heads(queries, heads, head_size)
    master_in, master_out = (
        lax.all_gather(fast_in, "tok", axis=1, tiled=True),
        lax.all_gather(fast_out, "tok", axis=1, tiled=True),
    )
    inc_in, inc_out = local_increments(
        keyn,
        values,
        step_size,
        master_in.astype(jnp.bfloat16),
        master_out.astype(jnp.bfloat16),
        block_root,
    )
    total_in, total_out = lax.psum((inc_in, inc_out), "tok")
    whole_in = renorm_in(master_in + total_in)
    whole_out = rms_rows(master_out + total_out)
    output = apply_all(queryn, whole_in.astype(jnp.bfloat16), whole_out.astype(jnp.bfloat16))
    place = lax.axis_index("tok")
    fast_in_next = lax.dynamic_slice_in_dim(whole_in, place * fast_in.shape[1], fast_in.shape[1], 1)
    fast_out_next = lax.dynamic_slice_in_dim(
        whole_out, place * fast_out.shape[1], fast_out.shape[1], 1
    )
    return (output, fast_in_next, fast_out_next)


def swap(value, bits):
    count = lax.axis_size("tok")
    return lax.ppermute(value, "tok", [(place, place ^ bits) for place in range(count)])


def swap_parts(value):
    return lax.ppermute(value, "parts", [(0, 1), (1, 0)])


def after(value, *before):
    return lax.optimization_barrier((value, before))[0]


def compiler_params():
    return pltpu.CompilerParams(vmem_limit_bytes=VMEM_LIMIT)


def head_of(ids, order, other):
    return 2 * jnp.bitwise_xor(ids[1], other) + jnp.bitwise_xor(ids[2], order)


def normalize_head(block):
    wide = block.astype(F32)
    return (wide * lax.rsqrt(jnp.mean(wide * wide, axis=-1, keepdims=True) + 1e-06)).astype(BF16)


def pack_kernel(ids, in_ref, out_ref, own, theirs):
    size = out_ref.shape[-1]
    rows = in_ref.shape[1]
    for other, ref in ((0, own), (1, theirs)):
        for order in range(2):
            head = head_of(ids, order, other)
            for block in range(in_ref.shape[2] // size):
                ref[order, block * rows : (block + 1) * rows, :] = in_ref[
                    head, :, block * size : (block + 1) * size
                ]
            ref[order, -out_ref.shape[1] :, :] = out_ref[head]


def pack(ids, fast_in, fast_out):
    rows = 4 * fast_in.shape[1] + fast_out.shape[1]
    shape = (2, rows, fast_out.shape[2])
    whole = [pl.BlockSpec(each, lambda i, ids: (0, 0, 0)) for each in (fast_in.shape, fast_out.shape, shape)]
    return pl.pallas_call(
        pack_kernel,
        grid_spec=pltpu.PrefetchScalarGridSpec(
            num_scalar_prefetch=1,
            grid=(1,),
            in_specs=whole[:2],
            out_specs=[whole[2]] * 2,
        ),
        out_shape=[jax.ShapeDtypeStruct(shape, F32)] * 2,
        compiler_params=compiler_params(),
        name="pack",
    )(ids, fast_in, fast_out)


def pair_kernel(own, got, master_one, master_two, shard):
    for source, ref in enumerate((own, got)):
        for order, master in enumerate((master_one, master_two)):
            master[source] = ref[order]
        shard[source] = ref[0].astype(BF16)


def pair(own, got):
    wide = jax.ShapeDtypeStruct(own.shape, F32)
    return pl.pallas_call(
        pair_kernel,
        out_shape=[wide, wide, jax.ShapeDtypeStruct(own.shape, BF16)],
        compiler_params=compiler_params(),
        name="pair",
    )(own, got)


def prepare_kernel(heads, block_root, ids, x_ref, *rest):
    own, send = rest[-2:]
    core = ids[1]
    half = heads // 2
    size = x_ref.shape[1] // heads

    if len(rest) == 3:
        rates = rest[0][...]
        columns_of = jnp.concatenate([rates, rates], axis=0).T

    def work(owner, out):
        for local in range(half):
            columns = pl.ds(pl.multiple_of((owner * half + local) * size, size), size)
            into = slice(local * size, (local + 1) * size)
            if len(rest) == 2:
                out[:, into] = normalize_head(x_ref[:, columns])
            else:
                first = columns_of[:, local : local + 1]
                second = columns_of[:, half + local : half + local + 1]
                rate = jnp.where(owner == 0, first, second) * block_root
                out[:, into] = (rate * x_ref[:, columns].astype(F32)).astype(BF16)

    work(core, own)
    work(1 - core, send)


def prepare(ids, tokens, rates, heads, block_root, name):
    rows, width = tokens.shape
    step = 256
    wide = pl.BlockSpec((step, width), lambda i, ids: (i, 0))
    narrow = pl.BlockSpec((step, width // 2), lambda i, ids: (i, 0))
    operands, specs = [tokens], [wide]
    if rates is not None:
        operands.append(rates)
        specs.append(pl.BlockSpec((heads, step), lambda i, ids: (0, i)))
    shape = jax.ShapeDtypeStruct((rows, width // 2), BF16)
    return pl.pallas_call(
        functools.partial(prepare_kernel, heads, block_root),
        grid_spec=pltpu.PrefetchScalarGridSpec(
            num_scalar_prefetch=1,
            grid=(rows // step,),
            in_specs=specs,
            out_specs=[narrow] * 2,
        ),
        out_shape=[shape] * 2,
        compiler_params=compiler_params(),
        cost_estimate=pl.CostEstimate(
            flops=rows * width * 5000, bytes_accessed=rows * width * 40, transcendentals=0
        ),
        name=name,
    )(ids, *operands)


def places(chip, core):
    for side in range(2):
        for slot in range(4):
            other = jnp.bitwise_xor(chip, 2 * slot + side)
            for source in range(2):
                yield side, slot, source, 2 * other + jnp.bitwise_xor(core, source)


def assemble(chip, core, lines, w_in, w_out):
    size = w_out.shape[1]
    blocks = w_in.shape[1] // size
    rows_in = w_in.shape[0] // 16
    rows_out = w_out.shape[0] // 16
    in_root = 1.0 / math.sqrt(size)
    for side, slot, source, place in places(chip, core):
        ref = lines[2 * side + slot // 2].at[slot % 2]
        into = pl.ds(pl.multiple_of(place * rows_in, rows_in), rows_in)
        for block in range(blocks):
            factor = in_root * (0.5 if block < blocks // 2 else 1.0)
            piece = ref[source, block * rows_in : (block + 1) * rows_in, :].astype(F32)
            w_in[into, block * size : (block + 1) * size] = (piece * factor).astype(BF16)
        into = pl.ds(pl.multiple_of(place * rows_out, rows_out), rows_out)
        w_out[into, :] = ref[source, blocks * rows_in :, :]


def increments_kernel(
    ids, near_low, near_high, far_low, far_high, k_own, v_own, k_got, v_got,
    kept, low, high, w_in, w_out, acc_in, acc_out, turned,
):
    step = pl.program_id(0)
    steps = pl.num_programs(0)
    chip, core = ids[0], ids[1]
    size = w_out.shape[1]
    fast = w_out.shape[0]
    in_root = 1.0 / math.sqrt(size)
    out_root = 1.0 / math.sqrt(fast)

    @pl.when(step == 0)
    def _():
        assemble(chip, core, (near_low, near_high, far_low, far_high), w_in, w_out)

    def work(k_ref, v_ref, start_over):
        keyn = k_ref[...]
        scaled = v_ref[...]
        keyn_t = keyn.T
        scaled_t = scaled.T

        def add(ref, columns, value):
            if start_over:
                ref[:, columns] = value
            else:
                ref[:, columns] += value

        chunk = 256
        for start in range(0, fast, chunk):
            gates = slice(start, start + chunk)
            ups = slice(fast + start, fast + start + chunk)
            gate = jnp.dot(keyn, w_in[:, gates], preferred_element_type=F32)
            upper = jnp.dot(keyn, w_in[:, ups], preferred_element_type=F32)
            back = (
                lax.dot_general(
                    scaled, w_out[gates, :], (((1,), (1,)), ((), ())), preferred_element_type=F32
                )
                * out_root
            )
            twice = jnp.tanh(gate) + 1.0
            active = gate * twice
            hidden = (active * upper).astype(BF16)
            d_gate = (back * upper * (twice + active * (2.0 - twice))).astype(BF16)
            d_up = (back * active).astype(BF16)
            add(acc_in, gates, jnp.dot(keyn_t, d_gate, preferred_element_type=F32))
            add(acc_in, ups, jnp.dot(keyn_t, d_up, preferred_element_type=F32))
            add(acc_out, gates, jnp.dot(scaled_t, hidden, preferred_element_type=F32))

    @pl.when(step == 0)
    def _():
        work(k_own, v_own, True)

    if k_own.shape[0] * 2 < 2048:

        @pl.when((step > 0) & (step < steps // 2))
        def _():
            work(k_own, v_own, False)

    @pl.when(step >= steps // 2)
    def _():
        work(k_got, v_got, False)

    @pl.when(step == steps - 1)
    def _():
        turned[...] = acc_out[...].T
        blocks = acc_in.shape[1] // size
        rows_in = acc_in.shape[0] // 16
        rows_out = turned.shape[0] // 16
        for side, slot, source, place in places(chip, core):
            ref = kept.at[slot] if side == 0 else (low, high)[slot // 2].at[slot % 2]
            rows = pl.ds(pl.multiple_of(place * rows_in, rows_in), rows_in)
            for block in range(blocks):
                ref[source, block * rows_in : (block + 1) * rows_in, :] = (
                    acc_in[rows, block * size : (block + 1) * size]
                    * (in_root * (0.5 if block < blocks // 2 else 1.0))
                ).astype(ref.dtype)
            rows = pl.ds(pl.multiple_of(place * rows_out, rows_out), rows_out)
            ref[source, blocks * rows_in :, :] = (turned[rows, :] * out_root).astype(ref.dtype)


def increments(ids, order, lines, k_own, v_own, k_got, v_got, fast):
    rows = k_own.shape[0]
    pair_shape = lines[0].shape
    size = pair_shape[-1]
    step = rows
    half = rows // step
    whole = pl.BlockSpec(pair_shape, lambda i, ids: (0, 0, 0, 0))
    line_shape = (4,) + pair_shape[1:]
    line = pl.BlockSpec(line_shape, lambda i, ids: (0, 0, 0, 0))
    own = pl.BlockSpec((step, size), lambda i, ids: (jnp.minimum(i, half - 1), ids[2] ^ order))
    got = pl.BlockSpec((step, size), lambda i, ids: (jnp.maximum(i - half, 0), ids[2] ^ order))
    return pl.pallas_call(
        increments_kernel,
        grid_spec=pltpu.PrefetchScalarGridSpec(
            num_scalar_prefetch=1,
            grid=(2 * half,),
            in_specs=[whole] * 4 + [own, own, got, got],
            out_specs=[line, whole, whole],
            scratch_shapes=[
                pltpu.VMEM((size, 2 * fast), BF16),
                pltpu.VMEM((fast, size), BF16),
                pltpu.VMEM((size, 2 * fast), F32),
                pltpu.VMEM((size, fast), F32),
                pltpu.VMEM((fast, size), F32),
            ],
        ),
        out_shape=[
            jax.ShapeDtypeStruct(line_shape, F32),
            jax.ShapeDtypeStruct(pair_shape, BF16),
            jax.ShapeDtypeStruct(pair_shape, BF16),
        ],
        compiler_params=compiler_params(),
        cost_estimate=pl.CostEstimate(
            flops=2 * rows * size * fast * 12, bytes_accessed=rows * size * 8, transcendentals=0
        ),
        name="increments",
    )(ids, *lines, k_own, v_own, k_got, v_got)


def add_kernel(kept, came, first, second):
    first[...] = (kept[0] + came[0].astype(F32)).astype(first.dtype)
    second[...] = (kept[1] + came[1].astype(F32)).astype(second.dtype)


def add_pair(kept, came, which, first_type):
    shape = came.shape
    flat = (0,) * (len(shape) - 1)
    return pl.pallas_call(
        add_kernel,
        grid=(1,),
        in_specs=[
            pl.BlockSpec(shape, lambda i: (which,) + flat),
            pl.BlockSpec(shape, lambda i: (0,) + flat),
        ],
        out_specs=[pl.BlockSpec(shape[1:], lambda i: flat)] * 2,
        out_shape=[
            jax.ShapeDtypeStruct(shape[1:], first_type),
            jax.ShapeDtypeStruct(shape[1:], BF16),
        ],
        compiler_params=compiler_params(),
        name="add_pair",
    )(kept, came)


def renorm_kernel(rows_in, master, kept, one, two, three, wide, short):
    size = master.shape[-1]
    for source in range(2):
        fresh = (
            master[source]
            + kept[source]
            + one[source].astype(F32)
            + two[source].astype(F32)
            + three[source].astype(F32)
        )
        for part in range(2):
            first = 2 * part * rows_in
            left = fresh[first : first + rows_in, :]
            right = fresh[first + rows_in : first + 2 * rows_in, :]
            total = jnp.sum(left * left + right * right, axis=-1, keepdims=True)
            factor = lax.rsqrt(total * (1.0 / (2 * size)) + 1e-06)
            for at, value in ((first, left), (first + rows_in, right)):
                done = value * factor
                wide[source, at : at + rows_in, :] = done
                short[source, at : at + rows_in, :] = done.astype(BF16)
        tail = fresh[4 * rows_in :, :]
        done = tail * lax.rsqrt(jnp.mean(tail * tail, axis=-1, keepdims=True) + 1e-06)
        wide[source, 4 * rows_in :, :] = done
        short[source, 4 * rows_in :, :] = done.astype(BF16)


def renorm(master, kept, one, two, three, rows_in):
    shape = master.shape
    return pl.pallas_call(
        functools.partial(renorm_kernel, rows_in),
        out_shape=[jax.ShapeDtypeStruct(shape, F32), jax.ShapeDtypeStruct(shape, BF16)],
        compiler_params=compiler_params(),
        name="renorm",
    )(master, kept, one, two, three)


def apply_kernel(order, other, ids, near_low, near_high, far_low, far_high, q_ref, *rest):
    o_hbm, w_in, w_out, o_ref, sent = rest[-5:]
    chip, core = ids[0], ids[1]
    fast, size = w_out.shape
    lines = (near_low, near_high, far_low, far_high)
    assemble(chip, jnp.bitwise_xor(core, other), lines, w_in, w_out)
    columns = pl.ds(pl.multiple_of(head_of(ids, order, other) * size, size), size)
    out_root = 1.0 / math.sqrt(fast)
    step = 512
    copies = []
    for start in range(0, q_ref.shape[0], step):
        rows = pl.ds(start, step)
        query = normalize_head(q_ref[rows, columns])
        gate = jnp.dot(query, w_in[:, :fast], preferred_element_type=F32)
        upper = jnp.dot(query, w_in[:, fast:], preferred_element_type=F32)
        hidden = (gate * (jnp.tanh(gate) + 1.0) * upper).astype(BF16)
        result = jnp.dot(hidden, w_out[...], preferred_element_type=F32) * out_root
        o_ref[rows, :] = result.astype(BF16)
        at = start // step
        copies.append(
            pltpu.make_async_copy(o_ref.at[rows, :], o_hbm.at[rows, columns], sent.at[at])
        )
        copies[-1].start()
    for copy in copies:
        copy.wait()


def apply_fast(ids, order, other, lines, queries, output, fast):
    rows, width = queries.shape
    size = lines[0].shape[-1]
    inside = pl.BlockSpec(memory_space=pltpu.VMEM)
    operands = [ids, *lines, queries]
    specs = [inside] * 5
    aliases = {}
    if output is not None:
        operands.append(output)
        specs.append(pl.BlockSpec(memory_space=pl.ANY))
        aliases = {6: 0}
    return pl.pallas_call(
        functools.partial(apply_kernel, order, other),
        grid_spec=pltpu.PrefetchScalarGridSpec(
            num_scalar_prefetch=1,
            grid=(1,),
            in_specs=specs,
            out_specs=pl.BlockSpec(memory_space=pl.ANY),
            scratch_shapes=[
                pltpu.VMEM((size, 2 * fast), BF16),
                pltpu.VMEM((fast, size), BF16),
                pltpu.VMEM((rows, size), BF16),
                pltpu.SemaphoreType.DMA((rows // 512,)),
            ],
        ),
        out_shape=jax.ShapeDtypeStruct((rows, width), BF16),
        input_output_aliases=aliases,
        compiler_params=compiler_params(),
        cost_estimate=pl.CostEstimate(
            flops=2 * rows * size * fast * 3, bytes_accessed=rows * size * 4, transcendentals=0
        ),
        name="apply",
    )(*operands)


def finish_kernel(rows_in, ids, one, two, came, in_next, out_next):
    size = out_next.shape[-1]
    for order, mine in enumerate((one, two)):
        for other, ref in ((0, mine.at[0]), (1, came.at[order])):
            head = head_of(ids, order, other)
            for block in range(4):
                in_next[head, :, block * size : (block + 1) * size] = ref[
                    block * rows_in : (block + 1) * rows_in, :
                ]
            out_next[head] = ref[4 * rows_in :, :]


def finish(ids, one, two, came, fast_in, fast_out):
    return pl.pallas_call(
        functools.partial(finish_kernel, fast_in.shape[1]),
        in_specs=[pl.BlockSpec(memory_space=pltpu.SMEM)] + [pl.BlockSpec(memory_space=pltpu.VMEM)] * 3,
        out_shape=[
            jax.ShapeDtypeStruct(fast_in.shape, F32),
            jax.ShapeDtypeStruct(fast_out.shape, F32),
        ],
        compiler_params=compiler_params(),
        name="finish",
    )(ids, one, two, came)


def per_device_cube(queries, keys, values, step_size, fast_in, fast_out):
    rows = keys.shape[0]
    heads = fast_in.shape[0]
    fast = fast_in.shape[2] // 2
    rows_in = fast_in.shape[1]
    place = lax.axis_index("tok")
    ids = jnp.stack([place // 2, place % 2, lax.axis_index("parts")]).astype(jnp.int32)
    block_root = 1.0 / math.sqrt(rows * lax.axis_size("tok"))

    k_own, k_send = prepare(ids, keys, None, heads, None, "keys")
    own, theirs = pack(after(ids, k_own), fast_in, fast_out)
    got = swap(theirs, 1)
    later = after(ids, got)
    v_own, v_send = prepare(later, values, step_size, heads, block_root, "values")
    master_one, master_two, shard = pair(own, after(got, k_send, v_send))
    masters = (master_one, master_two)
    k_got, v_got = swap(k_send, 1), swap(v_send, 1)
    z1, z3, z2 = swap(shard, 4), swap(shard, 12), swap(shard, 8)
    near_low = after(jnp.stack([shard, z1]), k_got, v_got)
    far_low, other_near_low = swap(near_low, 2), swap_parts(near_low)
    near_high = after(jnp.stack([z2, z3]), far_low, other_near_low)
    far_high = swap(near_high, 2)
    first = (near_low, near_high, far_low, far_high)
    second = (other_near_low, *(swap_parts(piece) for piece in first[1:]))

    wide, short = [], []
    for order in range(2):
        lines = second if order else first
        later = ids if order else after(ids, second[2])
        kept, low, high = increments(later, order, lines, k_own, v_own, k_got, v_got, fast)
        high, low = swap(high, 2), swap(low, 2)
        sum2, sum3 = add_pair(kept, high, 1, BF16)
        sum0, sum1 = add_pair(kept, low, 0, F32)
        three, two, one = swap(sum3, 12), swap(sum2, 8), swap(sum1, 4)
        a, b = renorm(masters[order], sum0, one, two, three, rows_in)
        wide.append(a)
        short.append(b)

    z1, z3, z2 = swap(short[0], 4), swap(short[0], 12), swap(short[0], 8)
    near_low, near_high = jnp.stack([short[0], z1]), jnp.stack([z2, z3])
    far_low, far_high = swap(near_low, 2), swap(near_high, 2)
    second = after(short[1], near_low)
    z1 = swap(second, 4)
    second_low = after(jnp.stack([second, z1]), near_high)
    later = after(short[1], second_low)
    z3, z2 = swap(later, 12), swap(later, 8)
    second_high = jnp.stack([z2, z3])
    mine = (near_low, near_high, far_low, far_high)
    others = tuple(swap(piece, 1) for piece in mine)
    output = apply_fast(ids, 0, 0, mine, queries, None, fast)
    came = swap(jnp.stack([wide[0][1], wide[1][1]]), 1)
    updated = finish(ids, wide[0], wide[1], came, fast_in, fast_out)
    near_low, near_high = second_low, after(second_high, *updated)
    output = apply_fast(ids, 0, 1, others, queries, output, fast)
    far_low, far_high = swap(near_low, 2), swap(near_high, 2)
    far_high = after(far_high, output)
    mine = (near_low, near_high, far_low, far_high)
    others = tuple(swap(piece, 1) for piece in mine)
    output = apply_fast(ids, 1, 0, mine, queries, output, fast)
    output = apply_fast(ids, 1, 1, others, queries, output, fast)

    return (output, *updated)


def per_device(queries, keys, values, step_size, fast_in, fast_out):
    fits = (
        lax.axis_size("tok") == 16
        and lax.axis_size("parts") == 2
        and fast_in.shape[0] == 4
        and fast_in.shape[1] % 16 == 0
    )
    chosen = per_device_cube if fits else per_device_generic
    return chosen(queries, keys, values, step_size, fast_in, fast_out)


def solution(mesh):
    placed = (
        P(("parts", "tok"), None),
        P(("parts", "tok"), None),
        P(("parts", "tok"), None),
        P(None, ("parts", "tok")),
        P(None, "tok", None),
        P(None, "tok", None),
    )
    return jax.shard_map(
        per_device,
        mesh=mesh,
        in_specs=placed,
        out_specs=(P(("parts", "tok"), None), P("parts", "tok", None), P("parts", "tok", None)),
        check_vma=False,
    )
```

```python
import functools
import math

import jax
import jax.numpy as jnp
from jax import lax
from jax.experimental import pallas as pl
from jax.experimental.pallas import tpu as pltpu
from jax.sharding import PartitionSpec as P

BF16 = jnp.bfloat16
F32 = jnp.float32
VMEM_LIMIT = 32 * 1024 * 1024


def rms_rows(matrix):
    return matrix * lax.rsqrt(jnp.mean(matrix * matrix, axis=-1, keepdims=True) + 1e-06)


def normalized_heads(tokens, heads, head_size):
    row_count = tokens.shape[0]
    wide = tokens.astype(jnp.float32).reshape(row_count, heads, head_size)
    return rms_rows(wide).astype(jnp.bfloat16)


def head_increments(key_rows, value_rows, rates, weight_in, weight_out, block_root):
    fast = weight_out.shape[0]
    in_root = 1.0 / math.sqrt(weight_in.shape[0])
    out_root = 1.0 / math.sqrt(fast)
    scaled = (rates[:, None] * block_root * value_rows.astype(jnp.float32)).astype(jnp.bfloat16)
    pre = jnp.dot(key_rows, weight_in, preferred_element_type=jnp.float32) * in_root
    gate = pre[:, :fast]
    upper = pre[:, fast:]
    sigma = jax.nn.sigmoid(gate)
    active = gate * sigma
    hidden = (active * upper).astype(jnp.bfloat16)
    back = (
        lax.dot_general(
            scaled, weight_out, (((1,), (1,)), ((), ())), preferred_element_type=jnp.float32
        )
        * out_root
    )
    d_gate = (back * upper * sigma * (1.0 + gate * (1.0 - sigma))).astype(jnp.bfloat16)
    d_up = (back * active).astype(jnp.bfloat16)
    joined = jnp.concatenate([d_gate, d_up], axis=1)
    inc_in = (
        lax.dot_general(
            key_rows, joined, (((0,), (0,)), ((), ())), preferred_element_type=jnp.float32
        )
        * in_root
    )
    inc_out = (
        lax.dot_general(
            hidden, scaled, (((0,), (0,)), ((), ())), preferred_element_type=jnp.float32
        )
        * out_root
    )
    return (inc_in, inc_out)


def local_increments(keyn, values, step_size, weight_in, weight_out, block_root):
    heads = weight_in.shape[0]
    head_size = weight_in.shape[1]
    list_in = []
    list_out = []
    for head_number in range(heads):
        value_rows = values[:, head_number * head_size : (head_number + 1) * head_size]
        part_in, part_out = head_increments(
            keyn[:, head_number, :],
            value_rows,
            step_size[head_number],
            weight_in[head_number],
            weight_out[head_number],
            block_root,
        )
        list_in.append(part_in)
        list_out.append(part_out)
    return (jnp.stack(list_in), jnp.stack(list_out))


def renorm_in(matrix):
    heads, rows_here, double = matrix.shape
    split = matrix.reshape(heads, rows_here, 2, double // 2)
    return rms_rows(split).reshape(heads, rows_here, double)


def apply_head(query_rows, weight_in, weight_out):
    fast = weight_out.shape[0]
    pre = jnp.dot(query_rows, weight_in, preferred_element_type=jnp.float32) * (
        1.0 / math.sqrt(weight_in.shape[0])
    )
    gate = pre[:, :fast]
    hidden = (gate * jax.nn.sigmoid(gate) * pre[:, fast:]).astype(jnp.bfloat16)
    return jnp.dot(hidden, weight_out, preferred_element_type=jnp.float32) * (1.0 / math.sqrt(fast))


def apply_all(queryn, next_in, next_out):
    heads = next_in.shape[0]
    pieces = []
    for head_number in range(heads):
        pieces.append(
            apply_head(queryn[:, head_number, :], next_in[head_number], next_out[head_number])
        )
    return jnp.concatenate(pieces, axis=1).astype(jnp.bfloat16)


def per_device_generic(queries, keys, values, step_size, fast_in, fast_out):
    row_count = keys.shape[0]
    heads = fast_in.shape[0]
    head_size = keys.shape[1] // heads
    block_root = 1.0 / math.sqrt(row_count * lax.axis_size("tok"))
    keyn = normalized_heads(keys, heads, head_size)
    queryn = normalized_heads(queries, heads, head_size)
    master_in, master_out = (
        lax.all_gather(fast_in, "tok", axis=1, tiled=True),
        lax.all_gather(fast_out, "tok", axis=1, tiled=True),
    )
    inc_in, inc_out = local_increments(
        keyn,
        values,
        step_size,
        master_in.astype(jnp.bfloat16),
        master_out.astype(jnp.bfloat16),
        block_root,
    )
    total_in, total_out = lax.psum((inc_in, inc_out), "tok")
    whole_in = renorm_in(master_in + total_in)
    whole_out = rms_rows(master_out + total_out)
    output = apply_all(queryn, whole_in.astype(jnp.bfloat16), whole_out.astype(jnp.bfloat16))
    place = lax.axis_index("tok")
    fast_in_next = lax.dynamic_slice_in_dim(whole_in, place * fast_in.shape[1], fast_in.shape[1], 1)
    fast_out_next = lax.dynamic_slice_in_dim(
        whole_out, place * fast_out.shape[1], fast_out.shape[1], 1
    )
    return (output, fast_in_next, fast_out_next)


def swap(value, bits):
    count = lax.axis_size("tok")
    return lax.ppermute(value, "tok", [(place, place ^ bits) for place in range(count)])


def swap_parts(value):
    return lax.ppermute(value, "parts", [(0, 1), (1, 0)])


def after(value, *before):
    return lax.optimization_barrier((value, before))[0]


def compiler_params():
    return pltpu.CompilerParams(vmem_limit_bytes=VMEM_LIMIT)


def head_of(ids, order, other):
    return 2 * jnp.bitwise_xor(ids[1], other) + jnp.bitwise_xor(ids[2], order)


def normalize_head(block):
    wide = block.astype(F32)
    return (wide * lax.rsqrt(jnp.mean(wide * wide, axis=-1, keepdims=True) + 1e-06)).astype(BF16)


def pack_kernel(ids, in_ref, out_ref, own, theirs):
    size = out_ref.shape[-1]
    rows = in_ref.shape[1]
    for other, ref in ((0, own), (1, theirs)):
        for order in range(2):
            head = head_of(ids, order, other)
            for block in range(in_ref.shape[2] // size):
                ref[order, block * rows : (block + 1) * rows, :] = in_ref[
                    head, :, block * size : (block + 1) * size
                ]
            ref[order, -out_ref.shape[1] :, :] = out_ref[head]


def pack(ids, fast_in, fast_out):
    rows = 4 * fast_in.shape[1] + fast_out.shape[1]
    shape = (2, rows, fast_out.shape[2])
    whole = [pl.BlockSpec(each, lambda i, ids: (0, 0, 0)) for each in (fast_in.shape, fast_out.shape, shape)]
    return pl.pallas_call(
        pack_kernel,
        grid_spec=pltpu.PrefetchScalarGridSpec(
            num_scalar_prefetch=1,
            grid=(1,),
            in_specs=whole[:2],
            out_specs=[whole[2]] * 2,
        ),
        out_shape=[jax.ShapeDtypeStruct(shape, F32)] * 2,
        compiler_params=compiler_params(),
        name="pack",
    )(ids, fast_in, fast_out)


def pair_kernel(own, got, master_one, master_two, shard):
    for source, ref in enumerate((own, got)):
        for order, master in enumerate((master_one, master_two)):
            master[source] = ref[order]
        shard[source] = ref[0].astype(BF16)


def pair(own, got):
    wide = jax.ShapeDtypeStruct(own.shape, F32)
    return pl.pallas_call(
        pair_kernel,
        out_shape=[wide, wide, jax.ShapeDtypeStruct(own.shape, BF16)],
        compiler_params=compiler_params(),
        name="pair",
    )(own, got)


def prepare_kernel(heads, block_root, ids, x_ref, *rest):
    own, send = rest[-2:]
    core = ids[1]
    half = heads // 2
    size = x_ref.shape[1] // heads

    if len(rest) == 3:
        rates = rest[0][...]
        columns_of = jnp.concatenate([rates, rates], axis=0).T

    def work(owner, out):
        for local in range(half):
            columns = pl.ds(pl.multiple_of((owner * half + local) * size, size), size)
            into = slice(local * size, (local + 1) * size)
            if len(rest) == 2:
                out[:, into] = normalize_head(x_ref[:, columns])
            else:
                first = columns_of[:, local : local + 1]
                second = columns_of[:, half + local : half + local + 1]
                rate = jnp.where(owner == 0, first, second) * block_root
                out[:, into] = (rate * x_ref[:, columns].astype(F32)).astype(BF16)

    work(core, own)
    work(1 - core, send)


def prepare(ids, tokens, rates, heads, block_root, name):
    rows, width = tokens.shape
    step = 256
    wide = pl.BlockSpec((step, width), lambda i, ids: (i, 0))
    narrow = pl.BlockSpec((step, width // 2), lambda i, ids: (i, 0))
    operands, specs = [tokens], [wide]
    if rates is not None:
        operands.append(rates)
        specs.append(pl.BlockSpec((heads, step), lambda i, ids: (0, i)))
    shape = jax.ShapeDtypeStruct((rows, width // 2), BF16)
    return pl.pallas_call(
        functools.partial(prepare_kernel, heads, block_root),
        grid_spec=pltpu.PrefetchScalarGridSpec(
            num_scalar_prefetch=1,
            grid=(rows // step,),
            in_specs=specs,
            out_specs=[narrow] * 2,
        ),
        out_shape=[shape] * 2,
        compiler_params=compiler_params(),
        cost_estimate=pl.CostEstimate(
            flops=rows * width * 5000, bytes_accessed=rows * width * 40, transcendentals=0
        ),
        name=name,
    )(ids, *operands)


def places(chip, core):
    for side in range(2):
        for slot in range(4):
            other = jnp.bitwise_xor(chip, 2 * slot + side)
            for source in range(2):
                yield side, slot, source, 2 * other + jnp.bitwise_xor(core, source)


def assemble(chip, core, lines, w_in, w_out):
    size = w_out.shape[1]
    blocks = w_in.shape[1] // size
    rows_in = w_in.shape[0] // 16
    rows_out = w_out.shape[0] // 16
    in_root = 1.0 / math.sqrt(size)
    for side, slot, source, place in places(chip, core):
        ref = lines[2 * side + slot // 2].at[slot % 2]
        into = pl.ds(pl.multiple_of(place * rows_in, rows_in), rows_in)
        for block in range(blocks):
            factor = in_root * (0.5 if block < blocks // 2 else 1.0)
            piece = ref[source, block * rows_in : (block + 1) * rows_in, :].astype(F32)
            w_in[into, block * size : (block + 1) * size] = (piece * factor).astype(BF16)
        into = pl.ds(pl.multiple_of(place * rows_out, rows_out), rows_out)
        w_out[into, :] = ref[source, blocks * rows_in :, :]


def increments_kernel(
    ids, near_low, near_high, far_low, far_high, k_own, v_own, k_got, v_got,
    kept, low, high, w_in, w_out, acc_in, acc_out, turned,
):
    step = pl.program_id(0)
    steps = pl.num_programs(0)
    chip, core = ids[0], ids[1]
    size = w_out.shape[1]
    fast = w_out.shape[0]
    in_root = 1.0 / math.sqrt(size)
    out_root = 1.0 / math.sqrt(fast)

    @pl.when(step == 0)
    def _():
        assemble(chip, core, (near_low, near_high, far_low, far_high), w_in, w_out)

    def work(k_ref, v_ref, start_over):
        keyn = k_ref[...]
        scaled = v_ref[...]
        keyn_t = keyn.T
        scaled_t = scaled.T

        def add(ref, columns, value):
            if start_over:
                ref[:, columns] = value
            else:
                ref[:, columns] += value

        chunk = 256
        for start in range(0, fast, chunk):
            gates = slice(start, start + chunk)
            ups = slice(fast + start, fast + start + chunk)
            gate = jnp.dot(keyn, w_in[:, gates], preferred_element_type=F32)
            upper = jnp.dot(keyn, w_in[:, ups], preferred_element_type=F32)
            back = (
                lax.dot_general(
                    scaled, w_out[gates, :], (((1,), (1,)), ((), ())), preferred_element_type=F32
                )
                * out_root
            )
            twice = jnp.tanh(gate) + 1.0
            active = gate * twice
            hidden = (active * upper).astype(BF16)
            d_gate = (back * upper * (twice + active * (2.0 - twice))).astype(BF16)
            d_up = (back * active).astype(BF16)
            add(acc_in, gates, jnp.dot(keyn_t, d_gate, preferred_element_type=F32))
            add(acc_in, ups, jnp.dot(keyn_t, d_up, preferred_element_type=F32))
            add(acc_out, gates, jnp.dot(scaled_t, hidden, preferred_element_type=F32))

    @pl.when(step == 0)
    def _():
        work(k_own, v_own, True)

    if k_own.shape[0] * 2 < 2048:

        @pl.when((step > 0) & (step < steps // 2))
        def _():
            work(k_own, v_own, False)

    @pl.when(step >= steps // 2)
    def _():
        work(k_got, v_got, False)

    @pl.when(step == steps - 1)
    def _():
        turned[...] = acc_out[...].T
        blocks = acc_in.shape[1] // size
        rows_in = acc_in.shape[0] // 16
        rows_out = turned.shape[0] // 16
        for side, slot, source, place in places(chip, core):
            ref = kept.at[slot] if side == 0 else (low, high)[slot // 2].at[slot % 2]
            rows = pl.ds(pl.multiple_of(place * rows_in, rows_in), rows_in)
            for block in range(blocks):
                ref[source, block * rows_in : (block + 1) * rows_in, :] = (
                    acc_in[rows, block * size : (block + 1) * size]
                    * (in_root * (0.5 if block < blocks // 2 else 1.0))
                ).astype(ref.dtype)
            rows = pl.ds(pl.multiple_of(place * rows_out, rows_out), rows_out)
            ref[source, blocks * rows_in :, :] = (turned[rows, :] * out_root).astype(ref.dtype)


def increments(ids, order, lines, k_own, v_own, k_got, v_got, fast):
    rows = k_own.shape[0]
    pair_shape = lines[0].shape
    size = pair_shape[-1]
    step = rows
    half = rows // step
    whole = pl.BlockSpec(pair_shape, lambda i, ids: (0, 0, 0, 0))
    line_shape = (4,) + pair_shape[1:]
    line = pl.BlockSpec(line_shape, lambda i, ids: (0, 0, 0, 0))
    own = pl.BlockSpec((step, size), lambda i, ids: (jnp.minimum(i, half - 1), ids[2] ^ order))
    got = pl.BlockSpec((step, size), lambda i, ids: (jnp.maximum(i - half, 0), ids[2] ^ order))
    return pl.pallas_call(
        increments_kernel,
        grid_spec=pltpu.PrefetchScalarGridSpec(
            num_scalar_prefetch=1,
            grid=(2 * half,),
            in_specs=[whole] * 4 + [own, own, got, got],
            out_specs=[line, whole, whole],
            scratch_shapes=[
                pltpu.VMEM((size, 2 * fast), BF16),
                pltpu.VMEM((fast, size), BF16),
                pltpu.VMEM((size, 2 * fast), F32),
                pltpu.VMEM((size, fast), F32),
                pltpu.VMEM((fast, size), F32),
            ],
        ),
        out_shape=[
            jax.ShapeDtypeStruct(line_shape, F32),
            jax.ShapeDtypeStruct(pair_shape, BF16),
            jax.ShapeDtypeStruct(pair_shape, BF16),
        ],
        compiler_params=compiler_params(),
        cost_estimate=pl.CostEstimate(
            flops=2 * rows * size * fast * 12, bytes_accessed=rows * size * 8, transcendentals=0
        ),
        name="increments",
    )(ids, *lines, k_own, v_own, k_got, v_got)


def add_kernel(kept, came, first, second):
    first[...] = (kept[0] + came[0].astype(F32)).astype(first.dtype)
    second[...] = (kept[1] + came[1].astype(F32)).astype(second.dtype)


def add_pair(kept, came, which, first_type):
    shape = came.shape
    flat = (0,) * (len(shape) - 1)
    return pl.pallas_call(
        add_kernel,
        grid=(1,),
        in_specs=[
            pl.BlockSpec(shape, lambda i: (which,) + flat),
            pl.BlockSpec(shape, lambda i: (0,) + flat),
        ],
        out_specs=[pl.BlockSpec(shape[1:], lambda i: flat)] * 2,
        out_shape=[
            jax.ShapeDtypeStruct(shape[1:], first_type),
            jax.ShapeDtypeStruct(shape[1:], BF16),
        ],
        compiler_params=compiler_params(),
        name="add_pair",
    )(kept, came)


def renorm_kernel(rows_in, master, kept, one, two, three, wide, short):
    size = master.shape[-1]
    for source in range(2):
        fresh = (
            master[source]
            + kept[source]
            + one[source].astype(F32)
            + two[source].astype(F32)
            + three[source].astype(F32)
        )
        for part in range(2):
            first = 2 * part * rows_in
            left = fresh[first : first + rows_in, :]
            right = fresh[first + rows_in : first + 2 * rows_in, :]
            total = jnp.sum(left * left + right * right, axis=-1, keepdims=True)
            factor = lax.rsqrt(total * (1.0 / (2 * size)) + 1e-06)
            for at, value in ((first, left), (first + rows_in, right)):
                done = value * factor
                wide[source, at : at + rows_in, :] = done
                short[source, at : at + rows_in, :] = done.astype(BF16)
        tail = fresh[4 * rows_in :, :]
        done = tail * lax.rsqrt(jnp.mean(tail * tail, axis=-1, keepdims=True) + 1e-06)
        wide[source, 4 * rows_in :, :] = done
        short[source, 4 * rows_in :, :] = done.astype(BF16)


def renorm(master, kept, one, two, three, rows_in):
    shape = master.shape
    return pl.pallas_call(
        functools.partial(renorm_kernel, rows_in),
        out_shape=[jax.ShapeDtypeStruct(shape, F32), jax.ShapeDtypeStruct(shape, BF16)],
        compiler_params=compiler_params(),
        name="renorm",
    )(master, kept, one, two, three)


def apply_kernel(order, other, ids, near_low, near_high, far_low, far_high, q_ref, *rest):
    o_hbm, w_in, w_out, o_ref, sent = rest[-5:]
    chip, core = ids[0], ids[1]
    fast, size = w_out.shape
    lines = (near_low, near_high, far_low, far_high)
    assemble(chip, jnp.bitwise_xor(core, other), lines, w_in, w_out)
    columns = pl.ds(pl.multiple_of(head_of(ids, order, other) * size, size), size)
    out_root = 1.0 / math.sqrt(fast)
    step = 512
    copies = []
    for start in range(0, q_ref.shape[0], step):
        rows = pl.ds(start, step)
        query = normalize_head(q_ref[rows, columns])
        gate = jnp.dot(query, w_in[:, :fast], preferred_element_type=F32)
        upper = jnp.dot(query, w_in[:, fast:], preferred_element_type=F32)
        hidden = (gate * (jnp.tanh(gate) + 1.0) * upper).astype(BF16)
        result = jnp.dot(hidden, w_out[...], preferred_element_type=F32) * out_root
        o_ref[rows, :] = result.astype(BF16)
        at = start // step
        copies.append(
            pltpu.make_async_copy(o_ref.at[rows, :], o_hbm.at[rows, columns], sent.at[at])
        )
        copies[-1].start()
    for copy in copies:
        copy.wait()


def apply_fast(ids, order, other, lines, queries, output, fast):
    rows, width = queries.shape
    size = lines[0].shape[-1]
    inside = pl.BlockSpec(memory_space=pltpu.VMEM)
    operands = [ids, *lines, queries]
    specs = [inside] * 5
    aliases = {}
    if output is not None:
        operands.append(output)
        specs.append(pl.BlockSpec(memory_space=pl.ANY))
        aliases = {6: 0}
    return pl.pallas_call(
        functools.partial(apply_kernel, order, other),
        grid_spec=pltpu.PrefetchScalarGridSpec(
            num_scalar_prefetch=1,
            grid=(1,),
            in_specs=specs,
            out_specs=pl.BlockSpec(memory_space=pl.ANY),
            scratch_shapes=[
                pltpu.VMEM((size, 2 * fast), BF16),
                pltpu.VMEM((fast, size), BF16),
                pltpu.VMEM((rows, size), BF16),
                pltpu.SemaphoreType.DMA((rows // 512,)),
            ],
        ),
        out_shape=jax.ShapeDtypeStruct((rows, width), BF16),
        input_output_aliases=aliases,
        compiler_params=compiler_params(),
        cost_estimate=pl.CostEstimate(
            flops=2 * rows * size * fast * 3, bytes_accessed=rows * size * 4, transcendentals=0
        ),
        name="apply",
    )(*operands)


def finish_kernel(rows_in, ids, one, two, came, in_next, out_next):
    size = out_next.shape[-1]
    for order, mine in enumerate((one, two)):
        for other, ref in ((0, mine.at[0]), (1, came.at[order])):
            head = head_of(ids, order, other)
            for block in range(4):
                in_next[head, :, block * size : (block + 1) * size] = ref[
                    block * rows_in : (block + 1) * rows_in, :
                ]
            out_next[head] = ref[4 * rows_in :, :]


def finish(ids, one, two, came, fast_in, fast_out):
    return pl.pallas_call(
        functools.partial(finish_kernel, fast_in.shape[1]),
        in_specs=[pl.BlockSpec(memory_space=pltpu.SMEM)] + [pl.BlockSpec(memory_space=pltpu.VMEM)] * 3,
        out_shape=[
            jax.ShapeDtypeStruct(fast_in.shape, F32),
            jax.ShapeDtypeStruct(fast_out.shape, F32),
        ],
        compiler_params=compiler_params(),
        name="finish",
    )(ids, one, two, came)


def per_device_cube(queries, keys, values, step_size, fast_in, fast_out):
    rows = keys.shape[0]
    heads = fast_in.shape[0]
    fast = fast_in.shape[2] // 2
    rows_in = fast_in.shape[1]
    place = lax.axis_index("tok")
    ids = jnp.stack([place // 2, place % 2, lax.axis_index("parts")]).astype(jnp.int32)
    block_root = 1.0 / math.sqrt(rows * lax.axis_size("tok"))

    k_own, k_send = prepare(ids, keys, None, heads, None, "keys")
    own, theirs = pack(after(ids, k_own), fast_in, fast_out)
    master_one, master_two, shard = pair(own, swap(theirs, 1))
    masters = (master_one, master_two)
    k_got = swap(k_send, 1)
    z1, z3, z2 = swap(shard, 4), swap(shard, 12), swap(shard, 8)
    near_low = after(jnp.stack([shard, z1]), k_got)
    far_low, other_near_low = swap(near_low, 2), swap_parts(near_low)
    near_high = after(jnp.stack([z2, z3]), far_low, other_near_low)
    far_high = swap(near_high, 2)
    later = after(ids, near_high)
    v_own, v_send = prepare(later, values, step_size, heads, block_root, "values")
    v_got = swap(v_send, 1)
    first = (near_low, near_high, far_low, far_high)
    second = (other_near_low, *(swap_parts(piece) for piece in first[1:]))

    wide, short = [], []
    for order in range(2):
        lines = second if order else first
        later = ids if order else after(ids, second[2])
        kept, low, high = increments(later, order, lines, k_own, v_own, k_got, v_got, fast)
        high, low = swap(high, 2), swap(low, 2)
        sum2, sum3 = add_pair(kept, high, 1, BF16)
        sum0, sum1 = add_pair(kept, low, 0, F32)
        three, two, one = swap(sum3, 12), swap(sum2, 8), swap(sum1, 4)
        a, b = renorm(masters[order], sum0, one, two, three, rows_in)
        wide.append(a)
        short.append(b)

    z1, z3, z2 = swap(short[0], 4), swap(short[0], 12), swap(short[0], 8)
    near_low, near_high = jnp.stack([short[0], z1]), jnp.stack([z2, z3])
    far_low, far_high = swap(near_low, 2), swap(near_high, 2)
    second = after(short[1], near_low)
    z1 = swap(second, 4)
    second_low = after(jnp.stack([second, z1]), near_high)
    later = after(short[1], second_low)
    z3, z2 = swap(later, 12), swap(later, 8)
    second_high = jnp.stack([z2, z3])
    mine = (near_low, near_high, far_low, far_high)
    others = tuple(swap(piece, 1) for piece in mine)
    output = apply_fast(ids, 0, 0, mine, queries, None, fast)
    came = swap(jnp.stack([wide[0][1], wide[1][1]]), 1)
    updated = finish(ids, wide[0], wide[1], came, fast_in, fast_out)
    near_low, near_high = second_low, after(second_high, *updated)
    output = apply_fast(ids, 0, 1, others, queries, output, fast)
    far_low, far_high = swap(near_low, 2), swap(near_high, 2)
    far_high = after(far_high, output)
    mine = (near_low, near_high, far_low, far_high)
    others = tuple(swap(piece, 1) for piece in mine)
    output = apply_fast(ids, 1, 0, mine, queries, output, fast)
    output = apply_fast(ids, 1, 1, others, queries, output, fast)

    return (output, *updated)


def per_device(queries, keys, values, step_size, fast_in, fast_out):
    fits = (
        lax.axis_size("tok") == 16
        and lax.axis_size("parts") == 2
        and fast_in.shape[0] == 4
        and fast_in.shape[1] % 16 == 0
    )
    chosen = per_device_cube if fits else per_device_generic
    return chosen(queries, keys, values, step_size, fast_in, fast_out)


def solution(mesh):
    placed = (
        P(("parts", "tok"), None),
        P(("parts", "tok"), None),
        P(("parts", "tok"), None),
        P(None, ("parts", "tok")),
        P(None, "tok", None),
        P(None, "tok", None),
    )
    return jax.shard_map(
        per_device,
        mesh=mesh,
        in_specs=placed,
        out_specs=(P(("parts", "tok"), None), P("parts", "tok", None), P("parts", "tok", None)),
        check_vma=False,
    )
```

```python
import functools
import math

import jax
import jax.numpy as jnp
from jax import lax
from jax.experimental import pallas as pl
from jax.experimental.pallas import tpu as pltpu
from jax.sharding import PartitionSpec as P

BF16 = jnp.bfloat16
F32 = jnp.float32
VMEM_LIMIT = 32 * 1024 * 1024


def rms_rows(matrix):
    return matrix * lax.rsqrt(jnp.mean(matrix * matrix, axis=-1, keepdims=True) + 1e-06)


def normalized_heads(tokens, heads, head_size):
    row_count = tokens.shape[0]
    wide = tokens.astype(jnp.float32).reshape(row_count, heads, head_size)
    return rms_rows(wide).astype(jnp.bfloat16)


def head_increments(key_rows, value_rows, rates, weight_in, weight_out, block_root):
    fast = weight_out.shape[0]
    in_root = 1.0 / math.sqrt(weight_in.shape[0])
    out_root = 1.0 / math.sqrt(fast)
    scaled = (rates[:, None] * block_root * value_rows.astype(jnp.float32)).astype(jnp.bfloat16)
    pre = jnp.dot(key_rows, weight_in, preferred_element_type=jnp.float32) * in_root
    gate = pre[:, :fast]
    upper = pre[:, fast:]
    sigma = jax.nn.sigmoid(gate)
    active = gate * sigma
    hidden = (active * upper).astype(jnp.bfloat16)
    back = (
        lax.dot_general(
            scaled, weight_out, (((1,), (1,)), ((), ())), preferred_element_type=jnp.float32
        )
        * out_root
    )
    d_gate = (back * upper * sigma * (1.0 + gate * (1.0 - sigma))).astype(jnp.bfloat16)
    d_up = (back * active).astype(jnp.bfloat16)
    joined = jnp.concatenate([d_gate, d_up], axis=1)
    inc_in = (
        lax.dot_general(
            key_rows, joined, (((0,), (0,)), ((), ())), preferred_element_type=jnp.float32
        )
        * in_root
    )
    inc_out = (
        lax.dot_general(
            hidden, scaled, (((0,), (0,)), ((), ())), preferred_element_type=jnp.float32
        )
        * out_root
    )
    return (inc_in, inc_out)


def local_increments(keyn, values, step_size, weight_in, weight_out, block_root):
    heads = weight_in.shape[0]
    head_size = weight_in.shape[1]
    list_in = []
    list_out = []
    for head_number in range(heads):
        value_rows = values[:, head_number * head_size : (head_number + 1) * head_size]
        part_in, part_out = head_increments(
            keyn[:, head_number, :],
            value_rows,
            step_size[head_number],
            weight_in[head_number],
            weight_out[head_number],
            block_root,
        )
        list_in.append(part_in)
        list_out.append(part_out)
    return (jnp.stack(list_in), jnp.stack(list_out))


def renorm_in(matrix):
    heads, rows_here, double = matrix.shape
    split = matrix.reshape(heads, rows_here, 2, double // 2)
    return rms_rows(split).reshape(heads, rows_here, double)


def apply_head(query_rows, weight_in, weight_out):
    fast = weight_out.shape[0]
    pre = jnp.dot(query_rows, weight_in, preferred_element_type=jnp.float32) * (
        1.0 / math.sqrt(weight_in.shape[0])
    )
    gate = pre[:, :fast]
    hidden = (gate * jax.nn.sigmoid(gate) * pre[:, fast:]).astype(jnp.bfloat16)
    return jnp.dot(hidden, weight_out, preferred_element_type=jnp.float32) * (1.0 / math.sqrt(fast))


def apply_all(queryn, next_in, next_out):
    heads = next_in.shape[0]
    pieces = []
    for head_number in range(heads):
        pieces.append(
            apply_head(queryn[:, head_number, :], next_in[head_number], next_out[head_number])
        )
    return jnp.concatenate(pieces, axis=1).astype(jnp.bfloat16)


def per_device_generic(queries, keys, values, step_size, fast_in, fast_out):
    row_count = keys.shape[0]
    heads = fast_in.shape[0]
    head_size = keys.shape[1] // heads
    block_root = 1.0 / math.sqrt(row_count * lax.axis_size("tok"))
    keyn = normalized_heads(keys, heads, head_size)
    queryn = normalized_heads(queries, heads, head_size)
    master_in, master_out = (
        lax.all_gather(fast_in, "tok", axis=1, tiled=True),
        lax.all_gather(fast_out, "tok", axis=1, tiled=True),
    )
    inc_in, inc_out = local_increments(
        keyn,
        values,
        step_size,
        master_in.astype(jnp.bfloat16),
        master_out.astype(jnp.bfloat16),
        block_root,
    )
    total_in, total_out = lax.psum((inc_in, inc_out), "tok")
    whole_in = renorm_in(master_in + total_in)
    whole_out = rms_rows(master_out + total_out)
    output = apply_all(queryn, whole_in.astype(jnp.bfloat16), whole_out.astype(jnp.bfloat16))
    place = lax.axis_index("tok")
    fast_in_next = lax.dynamic_slice_in_dim(whole_in, place * fast_in.shape[1], fast_in.shape[1], 1)
    fast_out_next = lax.dynamic_slice_in_dim(
        whole_out, place * fast_out.shape[1], fast_out.shape[1], 1
    )
    return (output, fast_in_next, fast_out_next)


def swap(value, bits):
    count = lax.axis_size("tok")
    return lax.ppermute(value, "tok", [(place, place ^ bits) for place in range(count)])


def swap_parts(value):
    return lax.ppermute(value, "parts", [(0, 1), (1, 0)])


def after(value, *before):
    return lax.optimization_barrier((value, before))[0]


def compiler_params():
    return pltpu.CompilerParams(vmem_limit_bytes=VMEM_LIMIT)


def head_of(ids, order, other):
    return 2 * jnp.bitwise_xor(ids[1], other) + jnp.bitwise_xor(ids[2], order)


def normalize_head(block):
    wide = block.astype(F32)
    return (wide * lax.rsqrt(jnp.mean(wide * wide, axis=-1, keepdims=True) + 1e-06)).astype(BF16)


def pack_kernel(ids, in_ref, out_ref, own, theirs):
    size = out_ref.shape[-1]
    rows = in_ref.shape[1]
    for other, ref in ((0, own), (1, theirs)):
        for order in range(2):
            head = head_of(ids, order, other)
            for block in range(in_ref.shape[2] // size):
                ref[order, block * rows : (block + 1) * rows, :] = in_ref[
                    head, :, block * size : (block + 1) * size
                ]
            ref[order, -out_ref.shape[1] :, :] = out_ref[head]


def pack(ids, fast_in, fast_out):
    rows = 4 * fast_in.shape[1] + fast_out.shape[1]
    shape = (2, rows, fast_out.shape[2])
    whole = [pl.BlockSpec(each, lambda i, ids: (0, 0, 0)) for each in (fast_in.shape, fast_out.shape, shape)]
    return pl.pallas_call(
        pack_kernel,
        grid_spec=pltpu.PrefetchScalarGridSpec(
            num_scalar_prefetch=1,
            grid=(1,),
            in_specs=whole[:2],
            out_specs=[whole[2]] * 2,
        ),
        out_shape=[jax.ShapeDtypeStruct(shape, F32)] * 2,
        compiler_params=compiler_params(),
        name="pack",
    )(ids, fast_in, fast_out)


def pair_kernel(own, got, master_one, master_two, shard):
    for source, ref in enumerate((own, got)):
        for order, master in enumerate((master_one, master_two)):
            master[source] = ref[order]
        shard[source] = ref[0].astype(BF16)


def pair(own, got):
    wide = jax.ShapeDtypeStruct(own.shape, F32)
    return pl.pallas_call(
        pair_kernel,
        out_shape=[wide, wide, jax.ShapeDtypeStruct(own.shape, BF16)],
        compiler_params=compiler_params(),
        name="pair",
    )(own, got)


def prepare_kernel(heads, block_root, ids, x_ref, *rest):
    own, send = rest[-2:]
    core = ids[1]
    half = heads // 2
    size = x_ref.shape[1] // heads

    if len(rest) == 3:
        rates = rest[0][...]
        columns_of = jnp.concatenate([rates, rates], axis=0).T

    def work(owner, out):
        for local in range(half):
            columns = pl.ds(pl.multiple_of((owner * half + local) * size, size), size)
            into = slice(local * size, (local + 1) * size)
            if len(rest) == 2:
                out[:, into] = normalize_head(x_ref[:, columns])
            else:
                first = columns_of[:, local : local + 1]
                second = columns_of[:, half + local : half + local + 1]
                rate = jnp.where(owner == 0, first, second) * block_root
                out[:, into] = (rate * x_ref[:, columns].astype(F32)).astype(BF16)

    work(core, own)
    work(1 - core, send)


def prepare(ids, tokens, rates, heads, block_root, name):
    rows, width = tokens.shape
    step = 256
    wide = pl.BlockSpec((step, width), lambda i, ids: (i, 0))
    narrow = pl.BlockSpec((step, width // 2), lambda i, ids: (i, 0))
    operands, specs = [tokens], [wide]
    if rates is not None:
        operands.append(rates)
        specs.append(pl.BlockSpec((heads, step), lambda i, ids: (0, i)))
    shape = jax.ShapeDtypeStruct((rows, width // 2), BF16)
    return pl.pallas_call(
        functools.partial(prepare_kernel, heads, block_root),
        grid_spec=pltpu.PrefetchScalarGridSpec(
            num_scalar_prefetch=1,
            grid=(rows // step,),
            in_specs=specs,
            out_specs=[narrow] * 2,
        ),
        out_shape=[shape] * 2,
        compiler_params=compiler_params(),
        cost_estimate=pl.CostEstimate(
            flops=rows * width * 5000, bytes_accessed=rows * width * 40, transcendentals=0
        ),
        name=name,
    )(ids, *operands)


def places(chip, core):
    for side in range(2):
        for slot in range(4):
            other = jnp.bitwise_xor(chip, 2 * slot + side)
            for source in range(2):
                yield side, slot, source, 2 * other + jnp.bitwise_xor(core, source)


def assemble(chip, core, lines, w_in, w_out):
    size = w_out.shape[1]
    blocks = w_in.shape[1] // size
    rows_in = w_in.shape[0] // 16
    rows_out = w_out.shape[0] // 16
    in_root = 1.0 / math.sqrt(size)
    for side, slot, source, place in places(chip, core):
        ref = lines[2 * side + slot // 2].at[slot % 2]
        into = pl.ds(pl.multiple_of(place * rows_in, rows_in), rows_in)
        for block in range(blocks):
            factor = in_root * (0.5 if block < blocks // 2 else 1.0)
            piece = ref[source, block * rows_in : (block + 1) * rows_in, :].astype(F32)
            w_in[into, block * size : (block + 1) * size] = (piece * factor).astype(BF16)
        into = pl.ds(pl.multiple_of(place * rows_out, rows_out), rows_out)
        w_out[into, :] = ref[source, blocks * rows_in :, :]


def increments_kernel(
    ids, near_low, near_high, far_low, far_high, k_own, v_own, k_got, v_got,
    kept, low, high, w_in, w_out, acc_in, acc_out, turned,
):
    step = pl.program_id(0)
    steps = pl.num_programs(0)
    chip, core = ids[0], ids[1]
    size = w_out.shape[1]
    fast = w_out.shape[0]
    in_root = 1.0 / math.sqrt(size)
    out_root = 1.0 / math.sqrt(fast)

    @pl.when(step == 0)
    def _():
        assemble(chip, core, (near_low, near_high, far_low, far_high), w_in, w_out)

    def work(k_ref, v_ref, start_over):
        keyn = k_ref[...]
        scaled = v_ref[...]
        keyn_t = keyn.T
        scaled_t = scaled.T

        def add(ref, columns, value):
            if start_over:
                ref[:, columns] = value
            else:
                ref[:, columns] += value

        chunk = 256
        for start in range(0, fast, chunk):
            gates = slice(start, start + chunk)
            ups = slice(fast + start, fast + start + chunk)
            gate = jnp.dot(keyn, w_in[:, gates], preferred_element_type=F32)
            upper = jnp.dot(keyn, w_in[:, ups], preferred_element_type=F32)
            back = (
                lax.dot_general(
                    scaled, w_out[gates, :], (((1,), (1,)), ((), ())), preferred_element_type=F32
                )
                * out_root
            )
            twice = jnp.tanh(gate) + 1.0
            active = gate * twice
            hidden = (active * upper).astype(BF16)
            d_gate = (back * upper * (twice + active * (2.0 - twice))).astype(BF16)
            d_up = (back * active).astype(BF16)
            add(acc_in, gates, jnp.dot(keyn_t, d_gate, preferred_element_type=F32))
            add(acc_in, ups, jnp.dot(keyn_t, d_up, preferred_element_type=F32))
            add(acc_out, gates, jnp.dot(scaled_t, hidden, preferred_element_type=F32))

    @pl.when(step == 0)
    def _():
        work(k_own, v_own, True)

    if k_own.shape[0] * 2 < 2048:

        @pl.when((step > 0) & (step < steps // 2))
        def _():
            work(k_own, v_own, False)

    @pl.when(step >= steps // 2)
    def _():
        work(k_got, v_got, False)

    @pl.when(step == steps - 1)
    def _():
        turned[...] = acc_out[...].T
        blocks = acc_in.shape[1] // size
        rows_in = acc_in.shape[0] // 16
        rows_out = turned.shape[0] // 16
        for side, slot, source, place in places(chip, core):
            ref = kept.at[slot] if side == 0 else (low, high)[slot // 2].at[slot % 2]
            rows = pl.ds(pl.multiple_of(place * rows_in, rows_in), rows_in)
            for block in range(blocks):
                ref[source, block * rows_in : (block + 1) * rows_in, :] = (
                    acc_in[rows, block * size : (block + 1) * size]
                    * (in_root * (0.5 if block < blocks // 2 else 1.0))
                ).astype(ref.dtype)
            rows = pl.ds(pl.multiple_of(place * rows_out, rows_out), rows_out)
            ref[source, blocks * rows_in :, :] = (turned[rows, :] * out_root).astype(ref.dtype)


def increments(ids, order, lines, k_own, v_own, k_got, v_got, fast):
    rows = k_own.shape[0]
    pair_shape = lines[0].shape
    size = pair_shape[-1]
    step = rows
    half = rows // step
    whole = pl.BlockSpec(pair_shape, lambda i, ids: (0, 0, 0, 0))
    line_shape = (4,) + pair_shape[1:]
    line = pl.BlockSpec(line_shape, lambda i, ids: (0, 0, 0, 0))
    own = pl.BlockSpec((step, size), lambda i, ids: (jnp.minimum(i, half - 1), ids[2] ^ order))
    got = pl.BlockSpec((step, size), lambda i, ids: (jnp.maximum(i - half, 0), ids[2] ^ order))
    return pl.pallas_call(
        increments_kernel,
        grid_spec=pltpu.PrefetchScalarGridSpec(
            num_scalar_prefetch=1,
            grid=(2 * half,),
            in_specs=[whole] * 4 + [own, own, got, got],
            out_specs=[line, whole, whole],
            scratch_shapes=[
                pltpu.VMEM((size, 2 * fast), BF16),
                pltpu.VMEM((fast, size), BF16),
                pltpu.VMEM((size, 2 * fast), F32),
                pltpu.VMEM((size, fast), F32),
                pltpu.VMEM((fast, size), F32),
            ],
        ),
        out_shape=[
            jax.ShapeDtypeStruct(line_shape, F32),
            jax.ShapeDtypeStruct(pair_shape, BF16),
            jax.ShapeDtypeStruct(pair_shape, BF16),
        ],
        compiler_params=compiler_params(),
        cost_estimate=pl.CostEstimate(
            flops=2 * rows * size * fast * 12, bytes_accessed=rows * size * 8, transcendentals=0
        ),
        name="increments",
    )(ids, *lines, k_own, v_own, k_got, v_got)


def add_kernel(kept, came, first, second):
    first[...] = (kept[0] + came[0].astype(F32)).astype(first.dtype)
    second[...] = (kept[1] + came[1].astype(F32)).astype(second.dtype)


def add_pair(kept, came, which, first_type):
    shape = came.shape
    flat = (0,) * (len(shape) - 1)
    return pl.pallas_call(
        add_kernel,
        grid=(1,),
        in_specs=[
            pl.BlockSpec(shape, lambda i: (which,) + flat),
            pl.BlockSpec(shape, lambda i: (0,) + flat),
        ],
        out_specs=[pl.BlockSpec(shape[1:], lambda i: flat)] * 2,
        out_shape=[
            jax.ShapeDtypeStruct(shape[1:], first_type),
            jax.ShapeDtypeStruct(shape[1:], BF16),
        ],
        compiler_params=compiler_params(),
        name="add_pair",
    )(kept, came)


def renorm_kernel(rows_in, master, kept, one, two, three, wide, short):
    size = master.shape[-1]
    for source in range(2):
        fresh = (
            master[source]
            + kept[source]
            + one[source].astype(F32)
            + two[source].astype(F32)
            + three[source].astype(F32)
        )
        for part in range(2):
            first = 2 * part * rows_in
            left = fresh[first : first + rows_in, :]
            right = fresh[first + rows_in : first + 2 * rows_in, :]
            total = jnp.sum(left * left + right * right, axis=-1, keepdims=True)
            factor = lax.rsqrt(total * (1.0 / (2 * size)) + 1e-06)
            for at, value in ((first, left), (first + rows_in, right)):
                done = value * factor
                wide[source, at : at + rows_in, :] = done
                short[source, at : at + rows_in, :] = done.astype(BF16)
        tail = fresh[4 * rows_in :, :]
        done = tail * lax.rsqrt(jnp.mean(tail * tail, axis=-1, keepdims=True) + 1e-06)
        wide[source, 4 * rows_in :, :] = done
        short[source, 4 * rows_in :, :] = done.astype(BF16)


def renorm(master, kept, one, two, three, rows_in):
    shape = master.shape
    return pl.pallas_call(
        functools.partial(renorm_kernel, rows_in),
        out_shape=[jax.ShapeDtypeStruct(shape, F32), jax.ShapeDtypeStruct(shape, BF16)],
        compiler_params=compiler_params(),
        name="renorm",
    )(master, kept, one, two, three)


def apply_kernel(order, other, ids, near_low, near_high, far_low, far_high, q_ref, *rest):
    o_hbm, w_in, w_out, o_ref, sent = rest[-5:]
    chip, core = ids[0], ids[1]
    fast, size = w_out.shape
    lines = (near_low, near_high, far_low, far_high)
    assemble(chip, jnp.bitwise_xor(core, other), lines, w_in, w_out)
    columns = pl.ds(pl.multiple_of(head_of(ids, order, other) * size, size), size)
    out_root = 1.0 / math.sqrt(fast)
    step = 512
    copies = []
    for start in range(0, q_ref.shape[0], step):
        rows = pl.ds(start, step)
        query = normalize_head(q_ref[rows, columns])
        gate = jnp.dot(query, w_in[:, :fast], preferred_element_type=F32)
        upper = jnp.dot(query, w_in[:, fast:], preferred_element_type=F32)
        hidden = (gate * (jnp.tanh(gate) + 1.0) * upper).astype(BF16)
        result = jnp.dot(hidden, w_out[...], preferred_element_type=F32) * out_root
        o_ref[rows, :] = result.astype(BF16)
        at = start // step
        copies.append(
            pltpu.make_async_copy(o_ref.at[rows, :], o_hbm.at[rows, columns], sent.at[at])
        )
        copies[-1].start()
    for copy in copies:
        copy.wait()


def apply_fast(ids, order, other, lines, queries, output, fast):
    rows, width = queries.shape
    size = lines[0].shape[-1]
    inside = pl.BlockSpec(memory_space=pltpu.VMEM)
    operands = [ids, *lines, queries]
    specs = [inside] * 5
    aliases = {}
    if output is not None:
        operands.append(output)
        specs.append(pl.BlockSpec(memory_space=pl.ANY))
        aliases = {6: 0}
    return pl.pallas_call(
        functools.partial(apply_kernel, order, other),
        grid_spec=pltpu.PrefetchScalarGridSpec(
            num_scalar_prefetch=1,
            grid=(1,),
            in_specs=specs,
            out_specs=pl.BlockSpec(memory_space=pl.ANY),
            scratch_shapes=[
                pltpu.VMEM((size, 2 * fast), BF16),
                pltpu.VMEM((fast, size), BF16),
                pltpu.VMEM((rows, size), BF16),
                pltpu.SemaphoreType.DMA((rows // 512,)),
            ],
        ),
        out_shape=jax.ShapeDtypeStruct((rows, width), BF16),
        input_output_aliases=aliases,
        compiler_params=compiler_params(),
        cost_estimate=pl.CostEstimate(
            flops=2 * rows * size * fast * 3, bytes_accessed=rows * size * 4, transcendentals=0
        ),
        name="apply",
    )(*operands)


def finish_kernel(rows_in, ids, one, two, came, in_next, out_next):
    size = out_next.shape[-1]
    for order, mine in enumerate((one, two)):
        for other, ref in ((0, mine.at[0]), (1, came.at[order])):
            head = head_of(ids, order, other)
            for block in range(4):
                in_next[head, :, block * size : (block + 1) * size] = ref[
                    block * rows_in : (block + 1) * rows_in, :
                ]
            out_next[head] = ref[4 * rows_in :, :]


def finish(ids, one, two, came, fast_in, fast_out):
    return pl.pallas_call(
        functools.partial(finish_kernel, fast_in.shape[1]),
        in_specs=[pl.BlockSpec(memory_space=pltpu.SMEM)] + [pl.BlockSpec(memory_space=pltpu.VMEM)] * 3,
        out_shape=[
            jax.ShapeDtypeStruct(fast_in.shape, F32),
            jax.ShapeDtypeStruct(fast_out.shape, F32),
        ],
        compiler_params=compiler_params(),
        name="finish",
    )(ids, one, two, came)


def per_device_cube(queries, keys, values, step_size, fast_in, fast_out):
    rows = keys.shape[0]
    heads = fast_in.shape[0]
    fast = fast_in.shape[2] // 2
    rows_in = fast_in.shape[1]
    place = lax.axis_index("tok")
    ids = jnp.stack([place // 2, place % 2, lax.axis_index("parts")]).astype(jnp.int32)
    block_root = 1.0 / math.sqrt(rows * lax.axis_size("tok"))

    k_own, k_send = prepare(ids, keys, None, heads, None, "keys")
    own, theirs = pack(after(ids, k_own), fast_in, fast_out)
    got = swap(theirs, 1)
    later = after(ids, got)
    v_own, v_send = prepare(later, values, step_size, heads, block_root, "values")
    master_one, master_two, shard = pair(own, after(got, k_send, v_send))
    masters = (master_one, master_two)
    k_got, v_got = swap(k_send, 1), swap(v_send, 1)
    z1, z3, z2 = swap(shard, 4), swap(shard, 12), swap(shard, 8)
    near_low = after(jnp.stack([shard, z1]), k_got, v_got)
    far_low, other_near_low = swap(near_low, 2), swap_parts(near_low)
    near_high = after(jnp.stack([z2, z3]), far_low, other_near_low)
    far_high = swap(near_high, 2)
    first = (near_low, near_high, far_low, far_high)
    second = (other_near_low, *(swap_parts(piece) for piece in first[1:]))

    wide, short = [], []
    for order in range(2):
        lines = second if order else first
        later = ids if order else after(ids, second[2])
        kept, low, high = increments(later, order, lines, k_own, v_own, k_got, v_got, fast)
        high, low = swap(high, 2), swap(low, 2)
        sum2, sum3 = add_pair(kept, high, 1, BF16)
        sum0, sum1 = add_pair(kept, low, 0, F32)
        three, two, one = swap(sum3, 12), swap(sum2, 8), swap(sum1, 4)
        a, b = renorm(masters[order], sum0, one, two, three, rows_in)
        wide.append(a)
        short.append(b)

    z1, z3, z2 = swap(short[0], 4), swap(short[0], 12), swap(short[0], 8)
    near_low, near_high = jnp.stack([short[0], z1]), jnp.stack([z2, z3])
    far_low, far_high = swap(near_low, 2), swap(near_high, 2)
    second = after(short[1], near_low)
    z1 = swap(second, 4)
    second_low = after(jnp.stack([second, z1]), near_high)
    later = after(short[1], second_low)
    z3, z2 = swap(later, 12), swap(later, 8)
    second_high = jnp.stack([z2, z3])
    mine = (near_low, near_high, far_low, far_high)
    others = tuple(swap(piece, 1) for piece in mine)
    output = apply_fast(ids, 0, 0, mine, queries, None, fast)
    came = swap(jnp.stack([wide[0][1], wide[1][1]]), 1)
    updated = finish(ids, wide[0], wide[1], came, fast_in, fast_out)
    near_low, far_low = second_low, swap(second_low, 2)
    near_high = after(second_high, far_low, output, *updated)
    output = apply_fast(ids, 0, 1, others, queries, output, fast)
    far_high = after(swap(near_high, 2), output)
    mine = (near_low, near_high, far_low, far_high)
    others = tuple(swap(piece, 1) for piece in mine)
    output = apply_fast(ids, 1, 0, mine, queries, output, fast)
    output = apply_fast(ids, 1, 1, others, queries, output, fast)

    return (output, *updated)


def per_device(queries, keys, values, step_size, fast_in, fast_out):
    fits = (
        lax.axis_size("tok") == 16
        and lax.axis_size("parts") == 2
        and fast_in.shape[0] == 4
        and fast_in.shape[1] % 16 == 0
    )
    chosen = per_device_cube if fits else per_device_generic
    return chosen(queries, keys, values, step_size, fast_in, fast_out)


def solution(mesh):
    placed = (
        P(("parts", "tok"), None),
        P(("parts", "tok"), None),
        P(("parts", "tok"), None),
        P(None, ("parts", "tok")),
        P(None, "tok", None),
        P(None, "tok", None),
    )
    return jax.shard_map(
        per_device,
        mesh=mesh,
        in_specs=placed,
        out_specs=(P(("parts", "tok"), None), P("parts", "tok", None), P("parts", "tok", None)),
        check_vma=False,
    )
```

```python
import functools
import math

import jax
import jax.numpy as jnp
from jax import lax
from jax.experimental import pallas as pl
from jax.experimental.pallas import tpu as pltpu
from jax.sharding import PartitionSpec as P

BF16 = jnp.bfloat16
F32 = jnp.float32
VMEM_LIMIT = 32 * 1024 * 1024


def rms_rows(matrix):
    return matrix * lax.rsqrt(jnp.mean(matrix * matrix, axis=-1, keepdims=True) + 1e-06)


def normalized_heads(tokens, heads, head_size):
    row_count = tokens.shape[0]
    wide = tokens.astype(jnp.float32).reshape(row_count, heads, head_size)
    return rms_rows(wide).astype(jnp.bfloat16)


def head_increments(key_rows, value_rows, rates, weight_in, weight_out, block_root):
    fast = weight_out.shape[0]
    in_root = 1.0 / math.sqrt(weight_in.shape[0])
    out_root = 1.0 / math.sqrt(fast)
    scaled = (rates[:, None] * block_root * value_rows.astype(jnp.float32)).astype(jnp.bfloat16)
    pre = jnp.dot(key_rows, weight_in, preferred_element_type=jnp.float32) * in_root
    gate = pre[:, :fast]
    upper = pre[:, fast:]
    sigma = jax.nn.sigmoid(gate)
    active = gate * sigma
    hidden = (active * upper).astype(jnp.bfloat16)
    back = (
        lax.dot_general(
            scaled, weight_out, (((1,), (1,)), ((), ())), preferred_element_type=jnp.float32
        )
        * out_root
    )
    d_gate = (back * upper * sigma * (1.0 + gate * (1.0 - sigma))).astype(jnp.bfloat16)
    d_up = (back * active).astype(jnp.bfloat16)
    joined = jnp.concatenate([d_gate, d_up], axis=1)
    inc_in = (
        lax.dot_general(
            key_rows, joined, (((0,), (0,)), ((), ())), preferred_element_type=jnp.float32
        )
        * in_root
    )
    inc_out = (
        lax.dot_general(
            hidden, scaled, (((0,), (0,)), ((), ())), preferred_element_type=jnp.float32
        )
        * out_root
    )
    return (inc_in, inc_out)


def local_increments(keyn, values, step_size, weight_in, weight_out, block_root):
    heads = weight_in.shape[0]
    head_size = weight_in.shape[1]
    list_in = []
    list_out = []
    for head_number in range(heads):
        value_rows = values[:, head_number * head_size : (head_number + 1) * head_size]
        part_in, part_out = head_increments(
            keyn[:, head_number, :],
            value_rows,
            step_size[head_number],
            weight_in[head_number],
            weight_out[head_number],
            block_root,
        )
        list_in.append(part_in)
        list_out.append(part_out)
    return (jnp.stack(list_in), jnp.stack(list_out))


def renorm_in(matrix):
    heads, rows_here, double = matrix.shape
    split = matrix.reshape(heads, rows_here, 2, double // 2)
    return rms_rows(split).reshape(heads, rows_here, double)


def apply_head(query_rows, weight_in, weight_out):
    fast = weight_out.shape[0]
    pre = jnp.dot(query_rows, weight_in, preferred_element_type=jnp.float32) * (
        1.0 / math.sqrt(weight_in.shape[0])
    )
    gate = pre[:, :fast]
    hidden = (gate * jax.nn.sigmoid(gate) * pre[:, fast:]).astype(jnp.bfloat16)
    return jnp.dot(hidden, weight_out, preferred_element_type=jnp.float32) * (1.0 / math.sqrt(fast))


def apply_all(queryn, next_in, next_out):
    heads = next_in.shape[0]
    pieces = []
    for head_number in range(heads):
        pieces.append(
            apply_head(queryn[:, head_number, :], next_in[head_number], next_out[head_number])
        )
    return jnp.concatenate(pieces, axis=1).astype(jnp.bfloat16)


def per_device_generic(queries, keys, values, step_size, fast_in, fast_out):
    row_count = keys.shape[0]
    heads = fast_in.shape[0]
    head_size = keys.shape[1] // heads
    block_root = 1.0 / math.sqrt(row_count * lax.axis_size("tok"))
    keyn = normalized_heads(keys, heads, head_size)
    queryn = normalized_heads(queries, heads, head_size)
    master_in, master_out = (
        lax.all_gather(fast_in, "tok", axis=1, tiled=True),
        lax.all_gather(fast_out, "tok", axis=1, tiled=True),
    )
    inc_in, inc_out = local_increments(
        keyn,
        values,
        step_size,
        master_in.astype(jnp.bfloat16),
        master_out.astype(jnp.bfloat16),
        block_root,
    )
    total_in, total_out = lax.psum((inc_in, inc_out), "tok")
    whole_in = renorm_in(master_in + total_in)
    whole_out = rms_rows(master_out + total_out)
    output = apply_all(queryn, whole_in.astype(jnp.bfloat16), whole_out.astype(jnp.bfloat16))
    place = lax.axis_index("tok")
    fast_in_next = lax.dynamic_slice_in_dim(whole_in, place * fast_in.shape[1], fast_in.shape[1], 1)
    fast_out_next = lax.dynamic_slice_in_dim(
        whole_out, place * fast_out.shape[1], fast_out.shape[1], 1
    )
    return (output, fast_in_next, fast_out_next)


def swap(value, bits):
    count = lax.axis_size("tok")
    return lax.ppermute(value, "tok", [(place, place ^ bits) for place in range(count)])


def swap_parts(value):
    return lax.ppermute(value, "parts", [(0, 1), (1, 0)])


def after(value, *before):
    return lax.optimization_barrier((value, before))[0]


def compiler_params():
    return pltpu.CompilerParams(vmem_limit_bytes=VMEM_LIMIT)


def head_of(ids, order, other):
    return 2 * jnp.bitwise_xor(ids[1], other) + jnp.bitwise_xor(ids[2], order)


def normalize_head(block):
    wide = block.astype(F32)
    return (wide * lax.rsqrt(jnp.mean(wide * wide, axis=-1, keepdims=True) + 1e-06)).astype(BF16)


def pack_kernel(ids, in_ref, out_ref, own, theirs):
    size = out_ref.shape[-1]
    rows = in_ref.shape[1]
    for other, ref in ((0, own), (1, theirs)):
        for order in range(2):
            head = head_of(ids, order, other)
            for block in range(in_ref.shape[2] // size):
                ref[order, block * rows : (block + 1) * rows, :] = in_ref[
                    head, :, block * size : (block + 1) * size
                ]
            ref[order, -out_ref.shape[1] :, :] = out_ref[head]


def pack(ids, fast_in, fast_out):
    rows = 4 * fast_in.shape[1] + fast_out.shape[1]
    shape = (2, rows, fast_out.shape[2])
    whole = [pl.BlockSpec(each, lambda i, ids: (0, 0, 0)) for each in (fast_in.shape, fast_out.shape, shape)]
    return pl.pallas_call(
        pack_kernel,
        grid_spec=pltpu.PrefetchScalarGridSpec(
            num_scalar_prefetch=1,
            grid=(1,),
            in_specs=whole[:2],
            out_specs=[whole[2]] * 2,
        ),
        out_shape=[jax.ShapeDtypeStruct(shape, F32)] * 2,
        compiler_params=compiler_params(),
        name="pack",
    )(ids, fast_in, fast_out)


def pair_kernel(own, got, master_one, master_two, shard):
    for source, ref in enumerate((own, got)):
        for order, master in enumerate((master_one, master_two)):
            master[source] = ref[order]
        shard[source] = ref[0].astype(BF16)


def pair(own, got):
    wide = jax.ShapeDtypeStruct(own.shape, F32)
    return pl.pallas_call(
        pair_kernel,
        out_shape=[wide, wide, jax.ShapeDtypeStruct(own.shape, BF16)],
        compiler_params=compiler_params(),
        name="pair",
    )(own, got)


def prepare_kernel(heads, block_root, ids, x_ref, *rest):
    own, send = rest[-2:]
    core = ids[1]
    half = heads // 2
    size = x_ref.shape[1] // heads

    if len(rest) == 3:
        rates = rest[0][...]
        columns_of = jnp.concatenate([rates, rates], axis=0).T

    def work(owner, out):
        for local in range(half):
            columns = pl.ds(pl.multiple_of((owner * half + local) * size, size), size)
            into = slice(local * size, (local + 1) * size)
            if len(rest) == 2:
                out[:, into] = normalize_head(x_ref[:, columns])
            else:
                first = columns_of[:, local : local + 1]
                second = columns_of[:, half + local : half + local + 1]
                rate = jnp.where(owner == 0, first, second) * block_root
                out[:, into] = (rate * x_ref[:, columns].astype(F32)).astype(BF16)

    work(core, own)
    work(1 - core, send)


def prepare(ids, tokens, rates, heads, block_root, name):
    rows, width = tokens.shape
    step = 256
    wide = pl.BlockSpec((step, width), lambda i, ids: (i, 0))
    narrow = pl.BlockSpec((step, width // 2), lambda i, ids: (i, 0))
    operands, specs = [tokens], [wide]
    if rates is not None:
        operands.append(rates)
        specs.append(pl.BlockSpec((heads, step), lambda i, ids: (0, i)))
    shape = jax.ShapeDtypeStruct((rows, width // 2), BF16)
    return pl.pallas_call(
        functools.partial(prepare_kernel, heads, block_root),
        grid_spec=pltpu.PrefetchScalarGridSpec(
            num_scalar_prefetch=1,
            grid=(rows // step,),
            in_specs=specs,
            out_specs=[narrow] * 2,
        ),
        out_shape=[shape] * 2,
        compiler_params=compiler_params(),
        cost_estimate=pl.CostEstimate(
            flops=rows * width * 5000, bytes_accessed=rows * width * 40, transcendentals=0
        ),
        name=name,
    )(ids, *operands)


def places(chip, core):
    for side in range(2):
        for slot in range(4):
            other = jnp.bitwise_xor(chip, 2 * slot + side)
            for source in range(2):
                yield side, slot, source, 2 * other + jnp.bitwise_xor(core, source)


def assemble(chip, core, lines, w_in, w_out):
    size = w_out.shape[1]
    blocks = w_in.shape[1] // size
    rows_in = w_in.shape[0] // 16
    rows_out = w_out.shape[0] // 16
    in_root = 1.0 / math.sqrt(size)
    for side, slot, source, place in places(chip, core):
        ref = lines[2 * side + slot // 2].at[slot % 2]
        into = pl.ds(pl.multiple_of(place * rows_in, rows_in), rows_in)
        for block in range(blocks):
            factor = in_root * (0.5 if block < blocks // 2 else 1.0)
            piece = ref[source, block * rows_in : (block + 1) * rows_in, :].astype(F32)
            w_in[into, block * size : (block + 1) * size] = (piece * factor).astype(BF16)
        into = pl.ds(pl.multiple_of(place * rows_out, rows_out), rows_out)
        w_out[into, :] = ref[source, blocks * rows_in :, :]


def increments_kernel(
    ids, near_low, near_high, far_low, far_high, k_own, v_own, k_got, v_got,
    kept, low, high, w_in, w_out, acc_in, acc_out, turned,
):
    step = pl.program_id(0)
    steps = pl.num_programs(0)
    chip, core = ids[0], ids[1]
    size = w_out.shape[1]
    fast = w_out.shape[0]
    in_root = 1.0 / math.sqrt(size)
    out_root = 1.0 / math.sqrt(fast)

    @pl.when(step == 0)
    def _():
        assemble(chip, core, (near_low, near_high, far_low, far_high), w_in, w_out)

    def work(k_ref, v_ref, start_over):
        keyn = k_ref[...]
        scaled = v_ref[...]
        keyn_t = keyn.T
        scaled_t = scaled.T

        def add(ref, columns, value):
            if start_over:
                ref[:, columns] = value
            else:
                ref[:, columns] += value

        chunk = 256
        for start in range(0, fast, chunk):
            gates = slice(start, start + chunk)
            ups = slice(fast + start, fast + start + chunk)
            gate = jnp.dot(keyn, w_in[:, gates], preferred_element_type=F32)
            upper = jnp.dot(keyn, w_in[:, ups], preferred_element_type=F32)
            back = (
                lax.dot_general(
                    scaled, w_out[gates, :], (((1,), (1,)), ((), ())), preferred_element_type=F32
                )
                * out_root
            )
            twice = jnp.tanh(gate) + 1.0
            active = gate * twice
            hidden = (active * upper).astype(BF16)
            d_gate = (back * upper * (twice + active * (2.0 - twice))).astype(BF16)
            d_up = (back * active).astype(BF16)
            add(acc_in, gates, jnp.dot(keyn_t, d_gate, preferred_element_type=F32))
            add(acc_in, ups, jnp.dot(keyn_t, d_up, preferred_element_type=F32))
            add(acc_out, gates, jnp.dot(scaled_t, hidden, preferred_element_type=F32))

    @pl.when(step == 0)
    def _():
        work(k_own, v_own, True)

    if k_own.shape[0] * 2 < 2048:

        @pl.when((step > 0) & (step < steps // 2))
        def _():
            work(k_own, v_own, False)

    @pl.when(step >= steps // 2)
    def _():
        work(k_got, v_got, False)

    @pl.when(step == steps - 1)
    def _():
        turned[...] = acc_out[...].T
        blocks = acc_in.shape[1] // size
        rows_in = acc_in.shape[0] // 16
        rows_out = turned.shape[0] // 16
        for side, slot, source, place in places(chip, core):
            ref = kept.at[slot] if side == 0 else (low, high)[slot // 2].at[slot % 2]
            rows = pl.ds(pl.multiple_of(place * rows_in, rows_in), rows_in)
            for block in range(blocks):
                ref[source, block * rows_in : (block + 1) * rows_in, :] = (
                    acc_in[rows, block * size : (block + 1) * size]
                    * (in_root * (0.5 if block < blocks // 2 else 1.0))
                ).astype(ref.dtype)
            rows = pl.ds(pl.multiple_of(place * rows_out, rows_out), rows_out)
            ref[source, blocks * rows_in :, :] = (turned[rows, :] * out_root).astype(ref.dtype)


def increments(ids, order, lines, k_own, v_own, k_got, v_got, fast):
    rows = k_own.shape[0]
    pair_shape = lines[0].shape
    size = pair_shape[-1]
    step = rows
    half = rows // step
    whole = pl.BlockSpec(pair_shape, lambda i, ids: (0, 0, 0, 0))
    line_shape = (4,) + pair_shape[1:]
    line = pl.BlockSpec(line_shape, lambda i, ids: (0, 0, 0, 0))
    own = pl.BlockSpec((step, size), lambda i, ids: (jnp.minimum(i, half - 1), ids[2] ^ order))
    got = pl.BlockSpec((step, size), lambda i, ids: (jnp.maximum(i - half, 0), ids[2] ^ order))
    return pl.pallas_call(
        increments_kernel,
        grid_spec=pltpu.PrefetchScalarGridSpec(
            num_scalar_prefetch=1,
            grid=(2 * half,),
            in_specs=[whole] * 4 + [own, own, got, got],
            out_specs=[line, whole, whole],
            scratch_shapes=[
                pltpu.VMEM((size, 2 * fast), BF16),
                pltpu.VMEM((fast, size), BF16),
                pltpu.VMEM((size, 2 * fast), F32),
                pltpu.VMEM((size, fast), F32),
                pltpu.VMEM((fast, size), F32),
            ],
        ),
        out_shape=[
            jax.ShapeDtypeStruct(line_shape, F32),
            jax.ShapeDtypeStruct(pair_shape, BF16),
            jax.ShapeDtypeStruct(pair_shape, BF16),
        ],
        compiler_params=compiler_params(),
        cost_estimate=pl.CostEstimate(
            flops=2 * rows * size * fast * 12, bytes_accessed=rows * size * 8, transcendentals=0
        ),
        name="increments",
    )(ids, *lines, k_own, v_own, k_got, v_got)


def add_kernel(kept, came, first, second):
    first[...] = (kept[0] + came[0].astype(F32)).astype(first.dtype)
    second[...] = (kept[1] + came[1].astype(F32)).astype(second.dtype)


def add_pair(kept, came, which, first_type):
    shape = came.shape
    flat = (0,) * (len(shape) - 1)
    return pl.pallas_call(
        add_kernel,
        grid=(1,),
        in_specs=[
            pl.BlockSpec(shape, lambda i: (which,) + flat),
            pl.BlockSpec(shape, lambda i: (0,) + flat),
        ],
        out_specs=[pl.BlockSpec(shape[1:], lambda i: flat)] * 2,
        out_shape=[
            jax.ShapeDtypeStruct(shape[1:], first_type),
            jax.ShapeDtypeStruct(shape[1:], BF16),
        ],
        compiler_params=compiler_params(),
        name="add_pair",
    )(kept, came)


def renorm_kernel(rows_in, master, kept, one, two, three, wide, short):
    size = master.shape[-1]
    for source in range(2):
        fresh = (
            master[source]
            + kept[source]
            + one[source].astype(F32)
            + two[source].astype(F32)
            + three[source].astype(F32)
        )
        for part in range(2):
            first = 2 * part * rows_in
            left = fresh[first : first + rows_in, :]
            right = fresh[first + rows_in : first + 2 * rows_in, :]
            total = jnp.sum(left * left + right * right, axis=-1, keepdims=True)
            factor = lax.rsqrt(total * (1.0 / (2 * size)) + 1e-06)
            for at, value in ((first, left), (first + rows_in, right)):
                done = value * factor
                wide[source, at : at + rows_in, :] = done
                short[source, at : at + rows_in, :] = done.astype(BF16)
        tail = fresh[4 * rows_in :, :]
        done = tail * lax.rsqrt(jnp.mean(tail * tail, axis=-1, keepdims=True) + 1e-06)
        wide[source, 4 * rows_in :, :] = done
        short[source, 4 * rows_in :, :] = done.astype(BF16)


def renorm(master, kept, one, two, three, rows_in):
    shape = master.shape
    return pl.pallas_call(
        functools.partial(renorm_kernel, rows_in),
        out_shape=[jax.ShapeDtypeStruct(shape, F32), jax.ShapeDtypeStruct(shape, BF16)],
        compiler_params=compiler_params(),
        name="renorm",
    )(master, kept, one, two, three)


def apply_kernel(order, other, ids, near_low, near_high, far_low, far_high, q_ref, *rest):
    o_hbm, w_in, w_out, o_ref, sent = rest[-5:]
    chip, core = ids[0], ids[1]
    fast, size = w_out.shape
    lines = (near_low, near_high, far_low, far_high)
    assemble(chip, jnp.bitwise_xor(core, other), lines, w_in, w_out)
    columns = pl.ds(pl.multiple_of(head_of(ids, order, other) * size, size), size)
    out_root = 1.0 / math.sqrt(fast)
    step = 512
    copies = []
    for start in range(0, q_ref.shape[0], step):
        rows = pl.ds(start, step)
        query = normalize_head(q_ref[rows, columns])
        gate = jnp.dot(query, w_in[:, :fast], preferred_element_type=F32)
        upper = jnp.dot(query, w_in[:, fast:], preferred_element_type=F32)
        hidden = (gate * (jnp.tanh(gate) + 1.0) * upper).astype(BF16)
        result = jnp.dot(hidden, w_out[...], preferred_element_type=F32) * out_root
        o_ref[rows, :] = result.astype(BF16)
        at = start // step
        copies.append(
            pltpu.make_async_copy(o_ref.at[rows, :], o_hbm.at[rows, columns], sent.at[at])
        )
        copies[-1].start()
    for copy in copies:
        copy.wait()


def apply_fast(ids, order, other, lines, queries, output, fast):
    rows, width = queries.shape
    size = lines[0].shape[-1]
    inside = pl.BlockSpec(memory_space=pltpu.VMEM)
    operands = [ids, *lines, queries]
    specs = [inside] * 5
    aliases = {}
    if output is not None:
        operands.append(output)
        specs.append(pl.BlockSpec(memory_space=pl.ANY))
        aliases = {6: 0}
    return pl.pallas_call(
        functools.partial(apply_kernel, order, other),
        grid_spec=pltpu.PrefetchScalarGridSpec(
            num_scalar_prefetch=1,
            grid=(1,),
            in_specs=specs,
            out_specs=pl.BlockSpec(memory_space=pl.ANY),
            scratch_shapes=[
                pltpu.VMEM((size, 2 * fast), BF16),
                pltpu.VMEM((fast, size), BF16),
                pltpu.VMEM((rows, size), BF16),
                pltpu.SemaphoreType.DMA((rows // 512,)),
            ],
        ),
        out_shape=jax.ShapeDtypeStruct((rows, width), BF16),
        input_output_aliases=aliases,
        compiler_params=compiler_params(),
        cost_estimate=pl.CostEstimate(
            flops=2 * rows * size * fast * 3, bytes_accessed=rows * size * 4, transcendentals=0
        ),
        name="apply",
    )(*operands)


def finish_kernel(rows_in, ids, one, two, came, in_next, out_next):
    size = out_next.shape[-1]
    for order, mine in enumerate((one, two)):
        for other, ref in ((0, mine.at[0]), (1, came.at[order])):
            head = head_of(ids, order, other)
            for block in range(4):
                in_next[head, :, block * size : (block + 1) * size] = ref[
                    block * rows_in : (block + 1) * rows_in, :
                ]
            out_next[head] = ref[4 * rows_in :, :]


def finish(ids, one, two, came, fast_in, fast_out):
    return pl.pallas_call(
        functools.partial(finish_kernel, fast_in.shape[1]),
        in_specs=[pl.BlockSpec(memory_space=pltpu.SMEM)] + [pl.BlockSpec(memory_space=pltpu.VMEM)] * 3,
        out_shape=[
            jax.ShapeDtypeStruct(fast_in.shape, F32),
            jax.ShapeDtypeStruct(fast_out.shape, F32),
        ],
        compiler_params=compiler_params(),
        name="finish",
    )(ids, one, two, came)


def per_device_cube(queries, keys, values, step_size, fast_in, fast_out):
    rows = keys.shape[0]
    heads = fast_in.shape[0]
    fast = fast_in.shape[2] // 2
    rows_in = fast_in.shape[1]
    place = lax.axis_index("tok")
    ids = jnp.stack([place // 2, place % 2, lax.axis_index("parts")]).astype(jnp.int32)
    block_root = 1.0 / math.sqrt(rows * lax.axis_size("tok"))

    k_own, k_send = prepare(ids, keys, None, heads, None, "keys")
    own, theirs = pack(after(ids, k_own), fast_in, fast_out)
    got = swap(theirs, 1)
    later = after(ids, got)
    v_own, v_send = prepare(later, values, step_size, heads, block_root, "values")
    master_one, master_two, shard = pair(own, after(got, k_send, v_send))
    masters = (master_one, master_two)
    k_got, v_got = swap(k_send, 1), swap(v_send, 1)
    z1, z3, z2 = swap(shard, 4), swap(shard, 12), swap(shard, 8)
    near_low = after(jnp.stack([shard, z1]), k_got, v_got)
    far_low, other_near_low = swap(near_low, 2), swap_parts(near_low)
    near_high = after(jnp.stack([z2, z3]), far_low, other_near_low)
    far_high = swap(near_high, 2)
    first = (near_low, near_high, far_low, far_high)
    second = (other_near_low, *(swap_parts(piece) for piece in first[1:]))

    wide, short = [], []
    for order in range(2):
        lines = second if order else first
        later = ids if order else after(ids, second[2])
        kept, low, high = increments(later, order, lines, k_own, v_own, k_got, v_got, fast)
        high, low = swap(high, 2), swap(low, 2)
        sum2, sum3 = add_pair(kept, high, 1, BF16)
        sum0, sum1 = add_pair(kept, low, 0, F32)
        three, two, one = swap(sum3, 12), swap(sum2, 8), swap(sum1, 4)
        a, b = renorm(masters[order], sum0, one, two, three, rows_in)
        wide.append(a)
        short.append(b)

    z1, z3, z2 = swap(short[0], 4), swap(short[0], 12), swap(short[0], 8)
    near_low, near_high = jnp.stack([short[0], z1]), jnp.stack([z2, z3])
    far_low, far_high = swap(near_low, 2), swap(near_high, 2)
    second = after(short[1], near_low)
    z1 = swap(second, 4)
    second_low = after(jnp.stack([second, z1]), near_high)
    later = second
    z3, z2 = swap(later, 12), swap(later, 8)
    second_high = jnp.stack([z2, z3])
    mine = (near_low, near_high, far_low, far_high)
    others = tuple(swap(piece, 1) for piece in mine)
    output = apply_fast(ids, 0, 0, mine, queries, None, fast)
    came = swap(after(jnp.stack([wide[0][1], wide[1][1]]), second_low), 1)
    updated = finish(ids, wide[0], wide[1], came, fast_in, fast_out)
    near_low, far_low = second_low, swap(second_low, 2)
    near_high = after(second_high, far_low, output, *updated)
    output = apply_fast(ids, 0, 1, others, queries, output, fast)
    far_high = after(swap(near_high, 2), output)
    mine = (near_low, near_high, far_low, far_high)
    others = tuple(swap(piece, 1) for piece in mine)
    output = apply_fast(ids, 1, 0, mine, queries, output, fast)
    output = apply_fast(ids, 1, 1, others, queries, output, fast)

    return (output, *updated)


def per_device(queries, keys, values, step_size, fast_in, fast_out):
    fits = (
        lax.axis_size("tok") == 16
        and lax.axis_size("parts") == 2
        and fast_in.shape[0] == 4
        and fast_in.shape[1] % 16 == 0
    )
    chosen = per_device_cube if fits else per_device_generic
    return chosen(queries, keys, values, step_size, fast_in, fast_out)


def solution(mesh):
    placed = (
        P(("parts", "tok"), None),
        P(("parts", "tok"), None),
        P(("parts", "tok"), None),
        P(None, ("parts", "tok")),
        P(None, "tok", None),
        P(None, "tok", None),
    )
    return jax.shard_map(
        per_device,
        mesh=mesh,
        in_specs=placed,
        out_specs=(P(("parts", "tok"), None), P("parts", "tok", None), P("parts", "tok", None)),
        check_vma=False,
    )
```
